128 devices in a mesh: dp: 32 (over z, y, x_hi), tensor: 4 (over x_lo, core).
Axes of the slice: x: 4 (x_hi: 2, x_lo: 2; x = x_hi * 2 + x_lo), y: 4, z: 4, core: 2. Of those that a mesh axis runs over, the one named last changes fastest.
Arguments:
- block_input: bfloat16 [32768, 1024], P(('dp', 'tensor')), may hold values from -6 to 6
- positions: int32 [32768], P('dp'), may hold values from 0 to 1021, as said below
- attn_gain: float32 [1024], replicated, may hold values from 0.1 to 1.9
- w_query: bfloat16 [1024, 1024], P('dp', 'tensor'), may hold values from -0.1875 to 0.1875
- w_key: bfloat16 [1024, 512], P('dp', 'tensor'), may hold values from -0.1875 to 0.1875
- w_value: bfloat16 [1024, 512], P('dp', 'tensor'), may hold values from -0.1875 to 0.1875
- w_output: bfloat16 [1024, 1024], P('tensor', 'dp'), may hold values from -0.75 to 0.75
- q_gain: float32 [64], replicated, may hold values from 0.7 to 2
- k_gain: float32 [64], replicated, may hold values from 0.7 to 2
- ffn_gain: float32 [1024], replicated, may hold values from 0.1 to 1.9
- w_gate: bfloat16 [1024, 4608], P('dp', 'tensor'), may hold values from -0.1875 to 0.1875
- w_up: bfloat16 [1024, 4608], P('dp', 'tensor'), may hold values from -0.1875 to 0.1875
- w_down: bfloat16 [4608, 1024], P('tensor', 'dp'), may hold values from -0.09375 to 0.09375
- cotangent: bfloat16 [32768, 1024], P(('dp', 'tensor')), may hold values from -6 to 6
Outputs:
- layer_output: bfloat16 [32768, 1024], P(('dp', 'tensor'))
- input_grad: float32 [32768, 1024], P(('dp', 'tensor'))
- attn_gain_grad: float32 [1024], replicated
- query_weight_grad: float32 [1024, 1024], P('dp', 'tensor')
- key_weight_grad: float32 [1024, 512], P('dp', 'tensor')
- value_weight_grad: float32 [1024, 512], P('dp', 'tensor')
- output_weight_grad: float32 [1024, 1024], P('tensor', 'dp')
- q_gain_grad: float32 [64], replicated
- k_gain_grad: float32 [64], replicated
- ffn_gain_grad: float32 [1024], replicated
- gate_weight_grad: float32 [1024, 4608], P('dp', 'tensor')
- up_weight_grad: float32 [1024, 4608], P('dp', 'tensor')
- down_weight_grad: float32 [4608, 1024], P('tensor', 'dp')
The draws below stay inside these ranges and needn't reach their ends.
Inputs may be any that keep to these rules, and one draw needn't show every extreme that they name: Within each sequence of 1024 tokens positions count up by one and fall back to 0 where a document starts; each sequence holds three documents, the middle one starting within the first 256 tokens and ending within the last 256; in one sequence the middle document starts at row 1 and ends at row 1022.
All inputs are finite; a program needn't handle non-finite values.
Results may differ from the reference program's by a relative error of at most 0.025.
Values may be sent and summed in bfloat16 or wider, within the bound.
A program may use at most 128 MiB of HBM per device.

```python
import math
import jax
import jax.numpy as jnp
from jax import lax

D = 1024
HEADS = 16
KV = 8
HSIZE = 64
FF = 4608
TOK_DEV = 256
SEQ = 1024
TOKENS = 32768
N_DP = 32
N_TENSOR = 4


def draw_positions(key, part):
    key = jax.random.fold_in(key, 11)
    start_key, stop_key, pick_key = jax.random.split(key, 3)
    starts = jax.random.randint(start_key, (N_DP, 1), 1, TOK_DEV)
    stops = jax.random.randint(stop_key, (N_DP, 1), (N_TENSOR - 1) * TOK_DEV + 1, SEQ)
    chosen = jax.random.randint(pick_key, (), 0, N_DP)
    seq_index = jnp.arange(N_DP, dtype=jnp.int32)[:, None]
    starts = jnp.where(seq_index == chosen, 1, starts)
    stops = jnp.where(seq_index == chosen, SEQ - 1, stops)
    row_index = jnp.arange(SEQ, dtype=jnp.int32)[None, :]
    begins = jnp.where(row_index >= stops, stops, jnp.where(row_index >= starts, starts, 0))
    return (row_index - begins).reshape(-1).astype(jnp.int32)


def level_of(key, dims, shards, low, top_value):
    gain = 1.0
    for position, parts in shards:
        steps = jax.random.uniform(jax.random.fold_in(jax.random.fold_in(key, 6), position), (parts,), jnp.float32, low / len(shards), top_value / len(shards))
        gain = gain * jnp.repeat(jnp.exp(steps), dims[position] // parts).reshape((-1,) + (1,) * (len(dims) - 1 - position))
    return gain


def centred(stream_key, shape, spread, limit, cuts=(), kind=jnp.bfloat16):
    array = spread * jax.random.normal(stream_key, shape, jnp.float32)
    if cuts:
        array = array * level_of(stream_key, shape, cuts, -0.22, 0.18)
    return jnp.clip(array, -limit, limit).astype(kind)


def setup_inputs(seed: int = 0) -> dict:
    keys = jax.random.split(jax.random.key(seed), 15)
    return {
        "block_input": centred(keys[0], (TOKENS, D), 1.0, 6.0, ((0, 128),)),
        "positions": draw_positions(jax.random.fold_in(keys[14], 71), 0),
        "attn_gain": jnp.clip(1.0 + 0.18 * jax.random.normal(keys[2], (D,), jnp.float32), 0.1, 1.9),
        "w_query": centred(keys[3], (D, HEADS * HSIZE), D ** -0.5, 0.1875, ((0, 32), (1, 4))),
        "w_key": centred(keys[4], (D, KV * HSIZE), D ** -0.5, 0.1875, ((0, 32), (1, 4))),
        "w_value": centred(keys[5], (D, KV * HSIZE), D ** -0.5, 0.1875, ((0, 32), (1, 4))),
        "w_output": centred(keys[6], (HEADS * HSIZE, D), (HEADS * HSIZE // 16) ** -0.5, 0.75, ((0, 4), (1, 32))),
        "q_gain": jnp.clip(jnp.exp(jax.random.uniform(keys[7], (HSIZE,), jnp.float32, math.log(0.7), math.log(2.0))), 0.7, 2.0),
        "k_gain": jnp.clip(jnp.exp(jax.random.uniform(keys[8], (HSIZE,), jnp.float32, math.log(0.7), math.log(2.0))), 0.7, 2.0),
        "ffn_gain": jnp.clip(1.0 + 0.18 * jax.random.normal(keys[9], (D,), jnp.float32), 0.1, 1.9),
        "w_gate": centred(keys[10], (D, FF), D ** -0.5, 0.1875, ((0, 32), (1, 4))),
        "w_up": centred(keys[11], (D, FF), D ** -0.5, 0.1875, ((0, 32), (1, 4))),
        "w_down": centred(keys[12], (FF, D), FF ** -0.5, 0.09375, ((0, 4), (1, 32))),
        "cotangent": centred(keys[13], (TOKENS, D), 1.0, 6.0, ((0, 128),)),
    }


@jax.custom_vjp
def low(v):
    return lax.optimization_barrier(v.astype(jnp.bfloat16)).astype(jnp.float32)

@jax.custom_vjp
def low_back(v):
    return v

def low_keep(v):
    return (low(v), None)

def low_pass(kept, grad):
    return (grad,)

def back_keep(v):
    return (v, None)

def back_low(kept, grad):
    return (low(grad),)
low.defvjp(low_keep, low_pass)
low_back.defvjp(back_keep, back_low)
epsilon = 1e-05
rope_base = 1000000.0
highest = lax.Precision.HIGHEST

def mean_norm(values, gain_vec):
    return values * lax.rsqrt(lax.optimization_barrier(jnp.mean(values * values, axis=-1, keepdims=True)) + epsilon) * gain_vec

def rotate(values, seq_positions):
    half_size = values.shape[-1] // 2
    frequency = rope_base ** (-jnp.arange(half_size, dtype=jnp.float32) * 2.0 / values.shape[-1])
    angles = seq_positions.astype(jnp.float32)[:, None] * frequency[None, :]
    cosine = jnp.cos(angles)[:, None, :]
    sine_table = jnp.sin(angles)[:, None, :]
    front_half = values[..., :half_size]
    back_half = values[..., half_size:]
    return jnp.concatenate([front_half * cosine - back_half * sine_table, back_half * cosine + front_half * sine_table], axis=-1)

def attend(queries, key_rows, value_rows, seq_positions):
    length = queries.shape[0]
    block_rows = min(512, length)
    count_blocks = length // block_rows
    row_index = jnp.arange(length, dtype=jnp.int32)
    key_all = jnp.repeat(key_rows, HEADS // KV, axis=1)
    value_all = jnp.repeat(value_rows, HEADS // KV, axis=1)

    def one_block(pieces):
        query_block, query_pos, query_index = pieces
        scores = jnp.einsum('qhd,khd->hqk', query_block, key_all, precision=highest)
        earlier = query_index[:, None] >= row_index[None, :]
        same_doc = query_index[:, None] - row_index[None, :] == query_pos[:, None] - seq_positions[None, :]
        allowed = jnp.logical_and(earlier, same_doc)
        scores = jnp.where(allowed[None], scores, -1e+30)
        scores = low_back(scores)
        row_total = jax.nn.logsumexp(scores, axis=-1, keepdims=True)
        attn_weight = low(jnp.exp(scores - row_total))
        return jnp.einsum('hqk,khd->qhd', attn_weight, value_all, precision=highest)
    result = lax.map(jax.checkpoint(one_block), (queries.reshape(count_blocks, block_rows, HEADS, HSIZE), seq_positions.reshape(count_blocks, block_rows), row_index.reshape(count_blocks, block_rows)))
    return result.reshape(length, HEADS * HSIZE)

def block_forward(sequence, seq_positions, attn_gain, w_query, w_key, w_value, w_output, q_gain, k_gain, ffn_gain, w_gate, w_up, w_down):
    length = sequence.shape[0]
    normed = low(mean_norm(sequence, attn_gain))
    query_pre = low_back(jnp.dot(normed, w_query, precision=highest))
    key_pre = low_back(jnp.dot(normed, w_key, precision=highest))
    value_heads = low(low_back(jnp.dot(normed, w_value, precision=highest)))
    query_rot = low(rotate(mean_norm(query_pre.reshape(length, HEADS, HSIZE), q_gain), seq_positions) * HSIZE ** (-0.5))
    key_rot = low(rotate(mean_norm(key_pre.reshape(length, KV, HSIZE), k_gain), seq_positions))
    mixed_heads = low(low_back(attend(query_rot, key_rot, value_heads.reshape(length, KV, HSIZE), seq_positions)))
    middle = sequence + low_back(jnp.dot(mixed_heads, w_output, precision=highest))
    normed_second = low(mean_norm(middle, ffn_gain))
    gate_value = low_back(jnp.dot(normed_second, w_gate, precision=highest))
    up_value = low_back(jnp.dot(normed_second, w_up, precision=highest))
    activation = low(jax.nn.silu(gate_value) * up_value)
    return middle + low_back(jnp.dot(activation, w_down, precision=highest))

def add_pair(earlier, latest):
    return earlier + latest

def reference(block_input, positions, attn_gain, w_query, w_key, w_value, w_output, q_gain, k_gain, ffn_gain, w_gate, w_up, w_down, cotangent):
    weights = (attn_gain.astype(jnp.float32), w_query.astype(jnp.float32), w_key.astype(jnp.float32), w_value.astype(jnp.float32), w_output.astype(jnp.float32), q_gain.astype(jnp.float32), k_gain.astype(jnp.float32), ffn_gain.astype(jnp.float32), w_gate.astype(jnp.float32), w_up.astype(jnp.float32), w_down.astype(jnp.float32))
    inputs = block_input.astype(jnp.float32).reshape(N_DP, SEQ, D)
    upstream = cotangent.astype(jnp.float32).reshape(N_DP, SEQ, D)
    seq_all = positions.reshape(N_DP, SEQ)

    def one_sequence(totals, pieces):
        sequence, seq_positions, seq_grads = pieces

        def run_block(sequence, *params):
            return block_forward(sequence, seq_positions, *params)
        result, pullback = jax.vjp(run_block, sequence, *weights)
        gradients = pullback(seq_grads)
        totals = jax.tree.map(add_pair, totals, tuple(gradients[1:]))
        return (totals, (result.astype(jnp.bfloat16), gradients[0]))
    initial = jax.tree.map(jnp.zeros_like, weights)
    totals, (outputs, input_grads) = lax.scan(one_sequence, initial, (inputs, seq_all, upstream))
    return (outputs.reshape(TOKENS, D), input_grads.reshape(TOKENS, D), totals[0], totals[1], totals[2], totals[3], totals[4], totals[5], totals[6], totals[7], totals[8], totals[9], totals[10])
```

```python
import functools

import jax
import jax.numpy as jnp
from jax import lax
from jax.experimental import pallas as pl
from jax.experimental.pallas import tpu as pltpu
from jax.sharding import PartitionSpec as P

epsilon = 1e-05
rope_base = 1000000.0
f32 = jnp.float32
bf16 = jnp.bfloat16
MESH = pl.DeviceIdType.MESH
VMEM_SPEC = pl.BlockSpec(memory_space=pltpu.VMEM)
VMEM_LIMIT = 60 * 1024 * 1024
WIDTH = 4224
Q0, K0, V0, O0, G0, U0, D0 = 0, 256, 384, 512, 768, 1920, 3072


class Place:
    def __init__(self):
        d = lax.axis_index("dp")
        t = lax.axis_index("tensor")
        self.z = lax.div(d, 8)
        self.y = lax.rem(lax.div(d, 2), 4)
        self.h = lax.rem(d, 2)
        self.xl = lax.div(t, 2)
        self.core = lax.rem(t, 2)
        self.d = d
        self.t = t

    def at(self, dz=0, dy=0, dh=0):
        z = lax.rem(self.z + (dz + 4), 4)
        y = lax.rem(self.y + (dy + 4), 4)
        h = self.h if dh == 0 else 1 - self.h
        return z * 8 + y * 2 + h

    def dp_device(self, dz=0, dy=0, dh=0):
        return (self.at(dz, dy, dh), self.t)

    def core_device(self):
        return (self.d, self.xl * 2 + (1 - self.core))

    def x_device(self):
        return (self.d, (1 - self.xl) * 2 + self.core)

    def token_block(self, dx=0, dc=0):
        xl = self.xl if dx == 0 else 1 - self.xl
        core = self.core if dc == 0 else 1 - self.core
        return xl * 2 + core


def greet(devices):
    barrier = pltpu.get_barrier_semaphore()
    for device in devices:
        pl.semaphore_signal(barrier, inc=1, device_id=device, device_id_type=MESH)
    pl.semaphore_wait(barrier, len(devices))


def ring_devices(me):
    return [
        me.dp_device(dz=1),
        me.dp_device(dz=-1),
        me.dp_device(dy=1),
        me.dp_device(dy=-1),
        me.dp_device(dh=1),
    ]


def remote(src, dst, send, recv, index, device):
    return pltpu.make_async_remote_copy(
        src_ref=src,
        dst_ref=dst,
        send_sem=send.at[index],
        recv_sem=recv.at[index],
        device_id=device,
        device_id_type=MESH,
    )


def offsets(kind, first, second):
    return (first, second) if kind == 0 else (second, first)


class WeightGather:
    COUNT = 41

    def __init__(self, me, full, send, recv):
        self.me, self.full, self.send, self.recv = me, full, send, recv
        self.started = []

    def block(self, kind, first, second, part=None):
        dz, dy = offsets(kind, first, second)
        row = self.me.at(dz, dy, kind) * 32
        if part is None:
            return self.full.at[pl.ds(pl.multiple_of(row, 32), 32)]
        return self.full.at[pl.ds(pl.multiple_of(row + part * 16, 16), 16)]

    def push(self, ref, index, device):
        copy = remote(ref, ref, self.send, self.recv, index, device)
        copy.start()
        self.started.append(copy)

    def arrived(self, ref, index):
        remote(ref, ref, self.send, self.recv, index, self.me.dp_device(dh=1)).wait_recv()

    def along(self, kind, level, step):
        dz, dy = offsets(kind, step, 0) if level == 0 else offsets(kind, 0, step)
        return self.me.dp_device(dz=dz, dy=dy)

    def base(self, kind, level, chunk):
        return 1 + kind * 4 + chunk * 0 if level == 0 else 9 + kind * 16 + chunk * 4

    def spread(self, kind, level, chunk):
        first = (0, -1, 1, 2)[chunk] if level == 1 else 0
        base = self.base(kind, level, chunk)
        ref = self.block(kind, first, 0)
        self.push(ref, base, self.along(kind, level, 1))
        self.push(ref, base + 1, self.along(kind, level, -1))

    def pass_on(self, kind, level, chunk, side):
        first = (0, -1, 1, 2)[chunk] if level == 1 else 0
        base = self.base(kind, level, chunk)
        step = -1 if side == 0 else 1
        where = (step, 0) if level == 0 else (first, step)
        self.arrived(self.block(kind, *where), base + side)
        self.push(self.block(kind, *where, part=side), base + 2 + side, self.along(kind, level, -step))

    def last(self, kind, level, chunk):
        first = (0, -1, 1, 2)[chunk] if level == 1 else 0
        base = self.base(kind, level, chunk)
        where = (2, 0) if level == 0 else (first, 2)
        for side in range(2):
            self.arrived(self.block(kind, *where, part=side), base + 2 + side)

    def begin(self):
        self.push(self.block(0, 0, 0), 0, self.me.dp_device(dh=1))
        self.spread(0, 0, 0)
        self.spread(0, 1, 0)

    def step1(self):
        self.arrived(self.block(1, 0, 0), 0)
        self.spread(1, 0, 0)
        self.spread(1, 1, 0)

    def step2(self):
        for kind in range(2):
            for side in range(2):
                self.pass_on(kind, 0, 0, side)
                self.spread(kind, 1, 1 + side)

    def step3(self):
        for kind in range(2):
            self.last(kind, 0, 0)
            self.spread(kind, 1, 3)

    def step4(self):
        for chunk in range(4):
            for kind in range(2):
                for side in range(2):
                    self.pass_on(kind, 1, chunk, side)

    def finish(self):
        for chunk in range(4):
            for kind in range(2):
                self.last(kind, 1, chunk)
        for copy in self.started:
            copy.wait_send()


class TokenGather:
    COUNT = 12
    CHUNKS = 4
    ROWS = 64

    def __init__(self, me, rows, send, recv):
        self.me, self.rows, self.send, self.recv = me, rows, send, recv
        self.started = []

    def piece(self, dx, dc, chunk):
        row = self.me.token_block(dx, dc) * 256 + chunk * self.ROWS
        return self.rows.at[pl.ds(pl.multiple_of(row, self.ROWS), self.ROWS)]

    def push(self, ref, index, device):
        copy = remote(ref, ref, self.send, self.recv, index, device)
        copy.start()
        self.started.append(copy)

    def arrived(self, ref, index):
        remote(ref, ref, self.send, self.recv, index, self.me.core_device()).wait_recv()

    def begin(self, chunk):
        own = self.piece(0, 0, chunk)
        self.push(own, chunk, self.me.x_device())
        self.push(own, 4 + chunk, self.me.core_device())

    def pass_on(self, chunk):
        other = self.piece(1, 0, chunk)
        self.arrived(other, chunk)
        self.push(other, 8 + chunk, self.me.core_device())

    def finish(self):
        for chunk in range(self.CHUNKS):
            self.arrived(self.piece(0, 1, chunk), 4 + chunk)
        for chunk in range(self.CHUNKS):
            self.arrived(self.piece(1, 1, chunk), 8 + chunk)
        for copy in self.started:
            copy.wait_send()


class TokenScatter:
    COUNT = 12
    CHUNKS = 4
    ROWS = 64

    def __init__(self, me, part, near, far, relay, send, recv):
        self.me, self.part, self.near, self.far, self.relay = me, part, near, far, relay
        self.send, self.recv = send, recv
        self.started = []

    def piece(self, dx, dc, chunk):
        row = self.me.token_block(dx, dc) * 256 + chunk * self.ROWS
        return pl.ds(pl.multiple_of(row, self.ROWS), self.ROWS)

    def push(self, src, dst, index, device):
        copy = remote(src, dst, self.send, self.recv, index, device)
        copy.start()
        self.started.append(copy)

    def arrived(self, ref, index):
        remote(ref, ref, self.send, self.recv, index, self.me.core_device()).wait_recv()

    def begin_far(self, chunk):
        self.push(
            self.part.at[self.piece(1, 1, chunk)], self.relay.at[chunk], chunk, self.me.core_device()
        )

    def begin_near(self, chunk):
        self.push(
            self.part.at[self.piece(0, 1, chunk)], self.near.at[chunk], 4 + chunk, self.me.core_device()
        )

    def relay_on(self, chunk):
        self.arrived(self.relay.at[chunk], chunk)
        total = self.relay[chunk].astype(f32) + self.part[self.piece(1, 0, chunk), :].astype(f32)
        self.relay[chunk] = total.astype(bf16)
        self.push(self.relay.at[chunk], self.far.at[chunk], 8 + chunk, self.me.x_device())

    def total(self, chunk):
        self.arrived(self.near.at[chunk], 4 + chunk)
        self.arrived(self.far.at[chunk], 8 + chunk)
        return (
            self.part[self.piece(0, 0, chunk), :].astype(f32)
            + self.near[chunk].astype(f32)
            + self.far[chunk].astype(f32)
        )

    def finish(self):
        for copy in self.started:
            copy.wait_send()


def scatter_scratch():
    return [pltpu.VMEM((4, 64, 1024), bf16)] * 3 + [pltpu.SemaphoreType.DMA((12,))] * 2


class GradScatter:
    COUNT = 41

    def __init__(self, me, part, recv_half, recv_full, out_full, sums, last, send, recv):
        self.me, self.part = me, part
        self.recv_half, self.recv_full = recv_half, recv_full
        self.out_full, self.sums, self.last = out_full, sums, last
        self.send, self.recv = send, recv
        self.started = []

    def rows(self, kind, first, second, part=None):
        dz, dy = offsets(kind, first, second)
        row = self.me.at(dz, dy, kind) * 32
        if part is None:
            return pl.ds(pl.multiple_of(row, 32), 32)
        return pl.ds(pl.multiple_of(row + part * 16, 16), 16)

    def push(self, src, dst, index, device):
        copy = remote(src, dst, self.send, self.recv, index, device)
        copy.start()
        self.started.append(copy)

    def arrived(self, ref, index):
        remote(ref, ref, self.send, self.recv, index, self.me.dp_device(dh=1)).wait_recv()

    def along(self, kind, level, step):
        dz, dy = offsets(kind, step, 0) if level == 0 else offsets(kind, 0, step)
        return self.me.dp_device(dz=dz, dy=dy)

    def slot(self, kind, level, chunk):
        return kind * 5 + (4 if level == 0 else chunk)

    def source(self, kind, level, chunk, offset):
        if level == 1:
            first = (0, -1, 1, 2)[chunk]
            return self.part, self.rows(kind, first, offset), [
                self.rows(kind, first, offset, part) for part in range(2)
            ]
        chunk = {0: 0, -1: 1, 1: 2, 2: 3}[offset]
        base = (kind * 4 + chunk) * 32
        return self.sums, pl.ds(base, 32), [pl.ds(base, 16), pl.ds(base + 16, 16)]

    def far(self, kind, level, chunk):
        slot = self.slot(kind, level, chunk)
        ref, _, halves = self.source(kind, level, chunk, 2)
        self.push(ref.at[halves[0]], self.recv_half.at[slot, 0], slot * 4, self.along(kind, level, 1))
        self.push(
            ref.at[halves[1]], self.recv_half.at[slot, 1], slot * 4 + 1, self.along(kind, level, -1)
        )

    def middle(self, kind, level, chunk, side):
        slot = self.slot(kind, level, chunk)
        step = 1 if side == 0 else -1
        ref, _, halves = self.source(kind, level, chunk, step)
        self.arrived(self.recv_half.at[slot, side], slot * 4 + side)
        total = ref[halves[side], :].astype(f32) + self.recv_half[slot, side].astype(f32)
        self.out_full[slot, side, pl.ds(16 * side, 16), :] = total.astype(bf16)
        self.out_full[slot, side, pl.ds(16 * (1 - side), 16), :] = ref[halves[1 - side], :]
        self.push(
            self.out_full.at[slot, side],
            self.recv_full.at[slot, side],
            slot * 4 + 2 + side,
            self.along(kind, level, step),
        )

    def total(self, kind, level, chunk):
        slot = self.slot(kind, level, chunk)
        ref, whole, _ = self.source(kind, level, chunk, 0)
        for side in range(2):
            self.arrived(self.recv_full.at[slot, side], slot * 4 + 2 + side)
        return (
            ref[whole, :].astype(f32)
            + self.recv_full[slot, 0].astype(f32)
            + self.recv_full[slot, 1].astype(f32)
        )

    def begin(self, chunk):
        for kind in range(2):
            self.far(kind, 1, chunk)

    def step1(self, chunk):
        for kind in range(2):
            for side in range(2):
                self.middle(kind, 1, chunk, side)

    def step2(self, chunk):
        for kind in range(2):
            total = self.total(kind, 1, chunk)
            self.sums[pl.ds((kind * 4 + chunk) * 32, 32), :] = total.astype(bf16)

    def step3(self):
        for kind in range(2):
            self.far(kind, 0, 0)

    def step4(self):
        for kind in (1, 0):
            for side in range(2):
                self.middle(kind, 0, 0, side)

    def step5(self):
        self.last[0] = self.total(1, 0, 0).astype(bf16)
        self.push(self.last.at[0], self.last.at[1], 40, self.me.dp_device(dh=1))

    def result(self):
        own = self.total(0, 0, 0)
        self.arrived(self.last.at[1], 40)
        return own + self.last[1].astype(f32)

    def finish(self):
        for copy in self.started:
            copy.wait_send()


def grad_scratch(width):
    return [
        pltpu.VMEM((10, 2, 16, width), bf16),
        pltpu.VMEM((10, 2, 32, width), bf16),
        pltpu.VMEM((10, 2, 32, width), bf16),
        pltpu.VMEM((256, width), bf16),
        pltpu.VMEM((2, 32, width), bf16),
        pltpu.SemaphoreType.DMA((41,)),
        pltpu.SemaphoreType.DMA((41,)),
    ]


def row_scale(values):
    return lax.rsqrt(jnp.mean(values * values, axis=-1, keepdims=True) + epsilon)


def norm_back(values, inverse, gain_vec, upstream):
    weighted = upstream * gain_vec
    row_inner = jnp.mean(weighted * values, axis=-1, keepdims=True)
    return inverse * weighted - values * inverse * inverse * inverse * row_inner


def call(kernel, outs, scratch, number, args, flops=0, moved=0):
    return pl.pallas_call(
        kernel,
        out_shape=outs,
        in_specs=[VMEM_SPEC] * len(args),
        out_specs=[VMEM_SPEC] * len(outs),
        scratch_shapes=scratch,
        cost_estimate=pl.CostEstimate(flops=flops, bytes_accessed=moved, transcendentals=0),
        compiler_params=pltpu.CompilerParams(
            collective_id=number, has_side_effects=True, vmem_limit_bytes=VMEM_LIMIT
        ),
    )(*args)


def gather_kernel(
    x_ref, gain_ref, shard_ref, cot_ref, full_ref, normed_ref, grad_rows_ref,
    w_send, w_recv, n_send, n_recv, c_send, c_recv,
):
    me = Place()
    weights = WeightGather(me, full_ref, w_send, w_recv)
    tokens = TokenGather(me, normed_ref, n_send, n_recv)
    upstream = TokenGather(me, grad_rows_ref, c_send, c_recv)
    own_rows = pl.ds(pl.multiple_of(me.d * 32, 32), 32)
    own_tokens = pl.ds(pl.multiple_of(me.t * 256, 256), 256)
    full_ref[own_rows, :] = shard_ref[...]
    values = x_ref[...].astype(f32)
    normed_ref[own_tokens, :] = (values * row_scale(values) * gain_ref[...]).astype(bf16)
    grad_rows_ref[own_tokens, :] = cot_ref[...]
    greet(ring_devices(me) + [me.core_device(), me.x_device()])
    weights.begin()
    for chunk in range(4):
        tokens.begin(chunk)
    weights.step1()
    weights.step2()
    for chunk in range(4):
        tokens.pass_on(chunk)
    for chunk in range(4):
        upstream.begin(chunk)
    weights.step3()
    weights.step4()
    for chunk in range(4):
        upstream.pass_on(chunk)
    tokens.finish()
    upstream.finish()
    weights.finish()


def middle_kernel(
    part_ref, x_ref, gain_ref, middle_ref, rows_ref,
    near, far, relay, s_send, s_recv, g_send, g_recv,
):
    me = Place()
    scatter = TokenScatter(me, part_ref, near, far, relay, s_send, s_recv)
    gather = TokenGather(me, rows_ref, g_send, g_recv)
    greet([me.core_device(), me.x_device()])
    for chunk in range(4):
        scatter.begin_far(chunk)
    for chunk in range(4):
        scatter.begin_near(chunk)
    for chunk in range(4):
        scatter.relay_on(chunk)
    for chunk in range(4):
        here = pl.ds(chunk * 64, 64)
        values = x_ref[here, :].astype(f32) + scatter.total(chunk)
        middle_ref[here, :] = values
        own = pl.ds(pl.multiple_of(me.t * 256 + chunk * 64, 64), 64)
        rows_ref[own, :] = (values * row_scale(values) * gain_ref[...]).astype(bf16)
        gather.begin(chunk)
    for chunk in range(4):
        gather.pass_on(chunk)
    scatter.finish()
    gather.finish()


def ffn_kernel(
    sum_ref, grad_ref, middle_ref, gain_ref, cot_ref, out_ref, middle_grad_ref, gain_part_ref, rows_ref,
    a_near, a_far, a_relay, a_send, a_recv, b_near, b_far, b_relay, b_send, b_recv, g_send, g_recv,
):
    me = Place()
    first = TokenScatter(me, grad_ref, a_near, a_far, a_relay, a_send, a_recv)
    second = TokenScatter(me, sum_ref, b_near, b_far, b_relay, b_send, b_recv)
    gather = TokenGather(me, rows_ref, g_send, g_recv)
    greet([me.core_device(), me.x_device()])
    for scatter in (first, second):
        for chunk in range(4):
            scatter.begin_far(chunk)
        for chunk in range(4):
            scatter.begin_near(chunk)
    for chunk in range(4):
        first.relay_on(chunk)
    gain_total = jnp.zeros((1, 1024), f32)
    for chunk in range(4):
        here = pl.ds(chunk * 64, 64)
        upstream = first.total(chunk)
        values = middle_ref[here, :]
        inverse = row_scale(values)
        gain_total = gain_total + jnp.sum(upstream * values * inverse, axis=0, keepdims=True)
        total = cot_ref[here, :].astype(f32) + norm_back(values, inverse, gain_ref[...], upstream)
        middle_grad_ref[here, :] = total
        own = pl.ds(pl.multiple_of(me.t * 256 + chunk * 64, 64), 64)
        rows_ref[own, :] = total.astype(bf16)
        gather.begin(chunk)
    gain_part_ref[...] = gain_total
    for chunk in range(4):
        gather.pass_on(chunk)
    for chunk in range(4):
        second.relay_on(chunk)
    for chunk in range(4):
        here = pl.ds(chunk * 64, 64)
        out_ref[here, :] = (middle_ref[here, :] + second.total(chunk)).astype(bf16)
    first.finish()
    second.finish()
    gather.finish()


class GainSum:
    COUNT = 9

    def __init__(self, me, pair, ring_y, ring_z, send, recv):
        self.me, self.pair, self.ring_y, self.ring_z = me, pair, ring_y, ring_z
        self.send, self.recv = send, recv
        self.started = []

    def devices(self):
        return [self.me.dp_device(dy=2), self.me.dp_device(dz=2)]

    def swap(self, index, value, device):
        self.pair[index, 0] = value
        copy = remote(
            self.pair.at[index, 0], self.pair.at[index, 1], self.send, self.recv, index, device
        )
        copy.start()
        copy.wait_recv()
        self.started.append(copy)
        return value + self.pair[index, 1]

    def round(self, ring, index, value, place, device):
        ring[place] = value
        for step in range(3):
            copy = remote(
                ring.at[place], ring.at[place], self.send, self.recv, index + step, device(step + 1)
            )
            copy.start()
            self.started.append(copy)
        for step in range(3):
            source = lax.rem(place + (3 - step), 4)
            remote(
                ring.at[source], ring.at[source], self.send, self.recv, index + step, device(1)
            ).wait_recv()
        return (ring[0] + ring[1]) + (ring[2] + ring[3])

    def run(self, value):
        me = self.me
        value = self.swap(0, value, me.core_device())
        value = self.swap(1, value, me.x_device())
        value = self.swap(2, value, me.dp_device(dh=1))
        value = self.round(self.ring_y, 3, value, me.y, lambda step: me.dp_device(dy=step))
        value = self.round(self.ring_z, 6, value, me.z, lambda step: me.dp_device(dz=step))
        for copy in self.started:
            copy.wait_send()
        return value


def gain_scratch():
    return [
        pltpu.VMEM((3, 2, 8, 1024), f32),
        pltpu.VMEM((4, 8, 1024), f32),
        pltpu.VMEM((4, 8, 1024), f32),
        pltpu.SemaphoreType.DMA((9,)),
        pltpu.SemaphoreType.DMA((9,)),
    ]


def last_kernel(
    part_ref, weight_ref, x_ref, gain_ref, middle_grad_ref, ffn_gain_ref, head_gain_ref,
    input_grad_ref, shard_ref, gains_ref, *scratch,
):
    me = Place()
    tokens = TokenScatter(me, part_ref, *scratch[:5])
    weights = GradScatter(me, weight_ref, *scratch[5:12])
    gains = GainSum(me, *scratch[12:])
    greet(ring_devices(me) + [me.core_device(), me.x_device()] + gains.devices())
    for chunk in range(4):
        tokens.begin_far(chunk)
    for chunk in range(4):
        tokens.begin_near(chunk)
    for chunk in range(4):
        weights.begin(chunk)
    for chunk in range(4):
        tokens.relay_on(chunk)
    weights.step1(0)
    weights.step1(1)
    gain_total = jnp.zeros((1, 1024), f32)
    for chunk in range(4):
        here = pl.ds(chunk * 64, 64)
        upstream = tokens.total(chunk)
        values = x_ref[here, :].astype(f32)
        inverse = row_scale(values)
        gain_total = gain_total + jnp.sum(upstream * values * inverse, axis=0, keepdims=True)
        input_grad_ref[here, :] = middle_grad_ref[here, :] + norm_back(
            values, inverse, gain_ref[...], upstream
        )
    weights.step1(2)
    weights.step1(3)
    for chunk in range(4):
        weights.step2(chunk)
    weights.step3()
    gains_ref[...] = jnp.concatenate(
        [gain_total, ffn_gain_ref[...], head_gain_ref[...], jnp.zeros((5, 1024), f32)], axis=0
    )
    gains_ref[...] = gains.run(gains_ref[...])
    weights.step4()
    weights.step5()
    shard_ref[...] = weights.result()
    weights.finish()
    tokens.finish()


def shape(rows, columns, kind):
    return jax.ShapeDtypeStruct((rows, columns), kind)


def sems(count):
    return [pltpu.SemaphoreType.DMA((count,))] * 2


def rotary_tables(positions, head_size):
    half_size = head_size // 2
    frequency = rope_base ** (-jnp.arange(half_size, dtype=jnp.float32) * 2.0 / head_size)
    angles = positions.astype(jnp.float32)[:, None] * frequency[None, :]
    return (jnp.cos(angles)[:, None, :], jnp.sin(angles)[:, None, :])


def rotate(values, cosine, sine_table):
    half_size = values.shape[-1] // 2
    front_half = values[..., :half_size]
    back_half = values[..., half_size:]
    return jnp.concatenate(
        [
            front_half * cosine - back_half * sine_table,
            back_half * cosine + front_half * sine_table,
        ],
        axis=-1,
    )


def rotate_back(upstream, cosine, sine_table):
    half_size = upstream.shape[-1] // 2
    front_half = upstream[..., :half_size]
    back_half = upstream[..., half_size:]
    return jnp.concatenate(
        [
            front_half * cosine + back_half * sine_table,
            back_half * cosine - front_half * sine_table,
        ],
        axis=-1,
    )


def allowed_mask(row_index, row_pos, col_index, col_pos):
    earlier = row_index[:, None] >= col_index[None, :]
    same_doc = row_index[:, None] - col_index[None, :] == row_pos[:, None] - col_pos[None, :]
    return jnp.logical_and(earlier, same_doc)


def block_scores(query_block, key_part, allowed):
    scores = jnp.einsum("qkgd,skd->kgqs", query_block, key_part, preferred_element_type=jnp.float32)
    return jnp.where(allowed[None, None], scores, -1e30)


def attention_forward(query_rot, key_rot, value_rows, positions):
    length = query_rot.shape[0]
    block_rows = min(512, length)
    row_index = jnp.arange(length, dtype=jnp.int32)
    pieces = []
    totals = []
    for number in range(length // block_rows):
        start_row = number * block_rows
        stop_row = start_row + block_rows
        allowed = allowed_mask(
            row_index[start_row:stop_row],
            positions[start_row:stop_row],
            row_index[:stop_row],
            positions[:stop_row],
        )
        scores = block_scores(query_rot[start_row:stop_row], key_rot[:stop_row], allowed)
        row_peak = jnp.max(scores, axis=-1, keepdims=True)
        row_total = row_peak + jnp.log(jnp.sum(jnp.exp(scores - row_peak), axis=-1, keepdims=True))
        weight_low = jnp.exp(scores - row_total).astype(jnp.bfloat16)
        pieces.append(
            jnp.einsum(
                "kgqs,skd->qkgd",
                weight_low,
                value_rows[:stop_row],
                preferred_element_type=jnp.float32,
            )
        )
        totals.append(row_total)
    return (jnp.concatenate(pieces, axis=0), jnp.concatenate(totals, axis=2))


def attention_backward(query_rot, key_rot, value_rows, positions, totals, mixed_grad):
    length = query_rot.shape[0]
    block_rows = min(512, length)
    row_index = jnp.arange(length, dtype=jnp.int32)
    query_parts = []
    key_grad = jnp.zeros(key_rot.shape, jnp.float32)
    value_grad = jnp.zeros(value_rows.shape, jnp.float32)
    for number in range(length // block_rows):
        start_row = number * block_rows
        stop_row = start_row + block_rows
        query_block = query_rot[start_row:stop_row]
        grad_block = mixed_grad[start_row:stop_row]
        key_part = key_rot[:stop_row]
        value_part = value_rows[:stop_row]
        allowed = allowed_mask(
            row_index[start_row:stop_row],
            positions[start_row:stop_row],
            row_index[:stop_row],
            positions[:stop_row],
        )
        scores = block_scores(query_block, key_part, allowed)
        attn_weight = jnp.exp(scores - totals[:, :, start_row:stop_row])
        weight_grad = jnp.einsum(
            "qkgd,skd->kgqs", grad_block, value_part, preferred_element_type=jnp.float32
        )
        row_inner = jnp.sum(attn_weight * weight_grad, axis=-1, keepdims=True)
        score_grad = (attn_weight * (weight_grad - row_inner)).astype(jnp.bfloat16)
        query_parts.append(
            jnp.einsum("kgqs,skd->qkgd", score_grad, key_part, preferred_element_type=jnp.float32)
        )
        key_grad = key_grad.at[:stop_row].add(
            jnp.einsum(
                "kgqs,qkgd->skd", score_grad, query_block, preferred_element_type=jnp.float32
            )
        )
        value_grad = value_grad.at[:stop_row].add(
            jnp.einsum(
                "kgqs,qkgd->skd",
                attn_weight.astype(jnp.bfloat16),
                grad_block,
                preferred_element_type=jnp.float32,
            )
        )
    return (jnp.concatenate(query_parts, axis=0), key_grad, value_grad)


def body(
    block_input,
    positions,
    attn_gain,
    w_query,
    w_key,
    w_value,
    w_output,
    q_gain,
    k_gain,
    ffn_gain,
    w_gate,
    w_up,
    w_down,
    cotangent,
):
    head_size = q_gain.shape[0]
    query_heads = w_query.shape[1] // head_size
    key_heads = w_key.shape[1] // head_size
    group_size = query_heads // key_heads
    length = positions.shape[0]
    score_scale = head_size ** (-0.5)
    cosine, sine_table = rotary_tables(positions, head_size)
    shard = jnp.concatenate([w_query, w_key, w_value, w_output.T, w_gate, w_up, w_down.T], axis=1)
    full, normed_rows, grad_rows = call(
        gather_kernel,
        [shape(1024, WIDTH, bf16), shape(1024, 1024, bf16), shape(1024, 1024, bf16)],
        sems(41) + sems(12) + sems(12),
        0,
        (block_input, attn_gain[None, :], shard, cotangent),
    )
    query_full = full[:, Q0:K0]
    key_full = full[:, K0:V0]
    value_full = full[:, V0:O0]
    output_full = full[:, O0:G0]
    gate_full = full[:, G0:U0]
    up_full = full[:, U0:D0]
    down_full = full[:, D0:]
    query_pre = jnp.dot(normed_rows, query_full, preferred_element_type=jnp.float32).reshape(
        length, query_heads, head_size
    )
    key_pre = jnp.dot(normed_rows, key_full, preferred_element_type=jnp.float32).reshape(
        length, key_heads, head_size
    )
    value_heads = (
        jnp.dot(normed_rows, value_full, preferred_element_type=jnp.float32)
        .astype(jnp.bfloat16)
        .reshape(length, key_heads, head_size)
    )
    query_scale = row_scale(query_pre)
    key_scale = row_scale(key_pre)
    query_rot = (rotate(query_pre * query_scale * q_gain, cosine, sine_table) * score_scale).astype(
        jnp.bfloat16
    )
    query_rot = query_rot.reshape(length, key_heads, group_size, head_size)
    key_rot = rotate(key_pre * key_scale * k_gain, cosine, sine_table).astype(jnp.bfloat16)
    attended, totals = attention_forward(query_rot, key_rot, value_heads, positions)
    mixed_heads = attended.astype(jnp.bfloat16).reshape(length, query_heads * head_size)
    attn_part = jnp.einsum(
        "rh,dh->rd", mixed_heads, output_full, preferred_element_type=jnp.float32
    ).astype(jnp.bfloat16)
    middle, second_rows = call(
        middle_kernel,
        [shape(256, 1024, f32), shape(1024, 1024, bf16)],
        scatter_scratch() + sems(12),
        1,
        (attn_part, block_input, ffn_gain[None, :]),
    )
    gate_value = jnp.dot(second_rows, gate_full, preferred_element_type=jnp.float32)
    up_value = jnp.dot(second_rows, up_full, preferred_element_type=jnp.float32)
    sigmoid_gate = jax.nn.sigmoid(gate_value)
    silu_value = gate_value * sigmoid_gate
    activation = (silu_value * up_value).astype(jnp.bfloat16)
    ffn_part = jnp.einsum(
        "rf,df->rd", activation, down_full, preferred_element_type=jnp.float32
    ).astype(jnp.bfloat16)
    hidden_grad = jnp.einsum("rd,df->rf", grad_rows, down_full, preferred_element_type=jnp.float32)
    gate_low = (
        hidden_grad * up_value * sigmoid_gate * (1.0 + gate_value * (1.0 - sigmoid_gate))
    ).astype(jnp.bfloat16)
    up_low = (hidden_grad * silu_value).astype(jnp.bfloat16)
    down_grad = jnp.einsum("rf,rd->df", activation, grad_rows, preferred_element_type=jnp.float32)
    gate_grad = jnp.einsum("rd,rf->df", second_rows, gate_low, preferred_element_type=jnp.float32)
    up_grad = jnp.einsum("rd,rf->df", second_rows, up_low, preferred_element_type=jnp.float32)
    second_part = (
        jnp.einsum("rf,df->rd", gate_low, gate_full, preferred_element_type=jnp.float32)
        + jnp.einsum("rf,df->rd", up_low, up_full, preferred_element_type=jnp.float32)
    ).astype(jnp.bfloat16)
    layer_output, middle_grad, ffn_gain_part, middle_rows = call(
        ffn_kernel,
        [
            shape(256, 1024, bf16),
            shape(256, 1024, f32),
            shape(1, 1024, f32),
            shape(1024, 1024, bf16),
        ],
        scatter_scratch() + scatter_scratch() + sems(12),
        2,
        (ffn_part, second_part, middle, ffn_gain[None, :], cotangent),
    )
    output_grad = jnp.einsum(
        "rh,rd->dh", mixed_heads, middle_rows, preferred_element_type=jnp.float32
    )
    mixed_grad = jnp.einsum(
        "rd,dh->rh", middle_rows, output_full, preferred_element_type=jnp.float32
    ).astype(jnp.bfloat16)
    mixed_grad = mixed_grad.reshape(length, key_heads, group_size, head_size)
    query_rot_grad, key_rot_grad, value_grad = attention_backward(
        query_rot, key_rot, value_heads, positions, totals, mixed_grad
    )
    query_norm_grad = rotate_back(
        query_rot_grad.reshape(length, query_heads, head_size) * score_scale, cosine, sine_table
    )
    key_norm_grad = rotate_back(key_rot_grad, cosine, sine_table)
    q_gain_part = jnp.sum(query_norm_grad * query_pre * query_scale, axis=(0, 1))
    k_gain_part = jnp.sum(key_norm_grad * key_pre * key_scale, axis=(0, 1))
    query_low = (
        norm_back(query_pre, query_scale, q_gain, query_norm_grad)
        .astype(jnp.bfloat16)
        .reshape(length, query_heads * head_size)
    )
    key_low = (
        norm_back(key_pre, key_scale, k_gain, key_norm_grad)
        .astype(jnp.bfloat16)
        .reshape(length, key_heads * head_size)
    )
    value_low = value_grad.astype(jnp.bfloat16).reshape(length, key_heads * head_size)
    query_grad = jnp.einsum("rd,rh->dh", normed_rows, query_low, preferred_element_type=jnp.float32)
    key_grad = jnp.einsum("rd,rh->dh", normed_rows, key_low, preferred_element_type=jnp.float32)
    value_weight = jnp.einsum(
        "rd,rh->dh", normed_rows, value_low, preferred_element_type=jnp.float32
    )
    total_part = jnp.einsum("rh,dh->rd", query_low, query_full, preferred_element_type=jnp.float32)
    total_part = total_part + jnp.einsum(
        "rh,dh->rd", key_low, key_full, preferred_element_type=jnp.float32
    )
    first_part = (
        total_part
        + jnp.einsum("rh,dh->rd", value_low, value_full, preferred_element_type=jnp.float32)
    ).astype(jnp.bfloat16)
    weight_part = jnp.concatenate(
        [
            part.astype(jnp.bfloat16)
            for part in (query_grad, key_grad, value_weight, output_grad, gate_grad, up_grad, down_grad)
        ],
        axis=1,
    )
    head_gains = jnp.pad(jnp.concatenate([q_gain_part, k_gain_part])[None, :], ((0, 0), (0, 896)))
    input_grad, shards, gains = call(
        last_kernel,
        [shape(256, 1024, f32), shape(32, WIDTH, f32), shape(8, 1024, f32)],
        scatter_scratch() + grad_scratch(WIDTH) + gain_scratch(),
        3,
        (
            first_part,
            weight_part,
            block_input,
            attn_gain[None, :],
            middle_grad,
            ffn_gain_part,
            head_gains,
        ),
    )
    return (
        layer_output,
        input_grad,
        gains[0],
        shards[:, Q0:K0],
        shards[:, K0:V0],
        shards[:, V0:O0],
        shards[:, O0:G0].T,
        gains[2, :64],
        gains[2, 64:128],
        gains[1],
        shards[:, G0:U0],
        shards[:, U0:D0],
        shards[:, D0:].T,
    )


def solution(mesh):
    placed = (
        P(("dp", "tensor"), None),
        P("dp"),
        P(),
        P("dp", "tensor"),
        P("dp", "tensor"),
        P("dp", "tensor"),
        P("tensor", "dp"),
        P(),
        P(),
        P(),
        P("dp", "tensor"),
        P("dp", "tensor"),
        P("tensor", "dp"),
        P(("dp", "tensor"), None),
    )
    return jax.shard_map(
        body,
        mesh=mesh,
        in_specs=placed,
        out_specs=(
            P(("dp", "tensor"), None),
            P(("dp", "tensor"), None),
            P(),
            P("dp", "tensor"),
            P("dp", "tensor"),
            P("dp", "tensor"),
            P("tensor", "dp"),
            P(),
            P(),
            P(),
            P("dp", "tensor"),
            P("dp", "tensor"),
            P("tensor", "dp"),
        ),
        check_vma=False,
    )
```

```python
import functools

import jax
import jax.numpy as jnp
from jax import lax
from jax.experimental import pallas as pl
from jax.experimental.pallas import tpu as pltpu
from jax.sharding import PartitionSpec as P

epsilon = 1e-05
rope_base = 1000000.0
f32 = jnp.float32
bf16 = jnp.bfloat16
MESH = pl.DeviceIdType.MESH
VMEM_SPEC = pl.BlockSpec(memory_space=pltpu.VMEM)
VMEM_LIMIT = 60 * 1024 * 1024


class Place:
    def __init__(self):
        d = lax.axis_index("dp")
        t = lax.axis_index("tensor")
        self.z = lax.div(d, 8)
        self.y = lax.rem(lax.div(d, 2), 4)
        self.h = lax.rem(d, 2)
        self.xl = lax.div(t, 2)
        self.core = lax.rem(t, 2)
        self.d = d
        self.t = t

    def at(self, dz=0, dy=0, dh=0):
        z = lax.rem(self.z + (dz + 4), 4)
        y = lax.rem(self.y + (dy + 4), 4)
        h = self.h if dh == 0 else 1 - self.h
        return z * 8 + y * 2 + h

    def dp_device(self, dz=0, dy=0, dh=0):
        return (self.at(dz, dy, dh), self.t)

    def core_device(self):
        return (self.d, self.xl * 2 + (1 - self.core))

    def x_device(self):
        return (self.d, (1 - self.xl) * 2 + self.core)

    def token_block(self, dx=0, dc=0):
        xl = self.xl if dx == 0 else 1 - self.xl
        core = self.core if dc == 0 else 1 - self.core
        return xl * 2 + core


def greet(devices):
    barrier = pltpu.get_barrier_semaphore()
    for device in devices:
        pl.semaphore_signal(barrier, inc=1, device_id=device, device_id_type=MESH)
    pl.semaphore_wait(barrier, len(devices))


def ring_devices(me):
    return [
        me.dp_device(dz=1),
        me.dp_device(dz=-1),
        me.dp_device(dy=1),
        me.dp_device(dy=-1),
        me.dp_device(dh=1),
    ]


def remote(src, dst, send, recv, index, device):
    return pltpu.make_async_remote_copy(
        src_ref=src,
        dst_ref=dst,
        send_sem=send.at[index],
        recv_sem=recv.at[index],
        device_id=device,
        device_id_type=MESH,
    )


def offsets(kind, first, second):
    return (first, second) if kind == 0 else (second, first)


class WeightGather:
    COUNT = 41

    def __init__(self, me, full, send, recv):
        self.me, self.full, self.send, self.recv = me, full, send, recv
        self.started = []

    def block(self, kind, first, second, part=None):
        dz, dy = offsets(kind, first, second)
        row = self.me.at(dz, dy, kind) * 32
        if part is None:
            return self.full.at[pl.ds(pl.multiple_of(row, 32), 32)]
        return self.full.at[pl.ds(pl.multiple_of(row + part * 16, 16), 16)]

    def push(self, ref, index, device):
        copy = remote(ref, ref, self.send, self.recv, index, device)
        copy.start()
        self.started.append(copy)

    def arrived(self, ref, index):
        remote(ref, ref, self.send, self.recv, index, self.me.dp_device(dh=1)).wait_recv()

    def along(self, kind, level, step):
        dz, dy = offsets(kind, step, 0) if level == 0 else offsets(kind, 0, step)
        return self.me.dp_device(dz=dz, dy=dy)

    def base(self, kind, level, chunk):
        return 1 + kind * 4 + chunk * 0 if level == 0 else 9 + kind * 16 + chunk * 4

    def spread(self, kind, level, chunk):
        first = (0, -1, 1, 2)[chunk] if level == 1 else 0
        base = self.base(kind, level, chunk)
        ref = self.block(kind, first, 0)
        self.push(ref, base, self.along(kind, level, 1))
        self.push(ref, base + 1, self.along(kind, level, -1))

    def pass_on(self, kind, level, chunk, side):
        first = (0, -1, 1, 2)[chunk] if level == 1 else 0
        base = self.base(kind, level, chunk)
        step = -1 if side == 0 else 1
        where = (step, 0) if level == 0 else (first, step)
        self.arrived(self.block(kind, *where), base + side)
        self.push(self.block(kind, *where, part=side), base + 2 + side, self.along(kind, level, -step))

    def last(self, kind, level, chunk):
        first = (0, -1, 1, 2)[chunk] if level == 1 else 0
        base = self.base(kind, level, chunk)
        where = (2, 0) if level == 0 else (first, 2)
        for side in range(2):
            self.arrived(self.block(kind, *where, part=side), base + 2 + side)

    def begin(self):
        self.push(self.block(0, 0, 0), 0, self.me.dp_device(dh=1))
        self.spread(0, 0, 0)
        self.spread(0, 1, 0)

    def step1(self):
        self.arrived(self.block(1, 0, 0), 0)
        self.spread(1, 0, 0)
        self.spread(1, 1, 0)

    def step2(self):
        for kind in range(2):
            for side in range(2):
                self.pass_on(kind, 0, 0, side)
                self.spread(kind, 1, 1 + side)

    def step3(self):
        for kind in range(2):
            self.last(kind, 0, 0)
            self.spread(kind, 1, 3)

    def step4(self):
        for chunk in range(4):
            for kind in range(2):
                for side in range(2):
                    self.pass_on(kind, 1, chunk, side)

    def finish(self):
        for chunk in range(4):
            for kind in range(2):
                self.last(kind, 1, chunk)
        for copy in self.started:
            copy.wait_send()


class TokenGather:
    COUNT = 12
    CHUNKS = 4
    ROWS = 64

    def __init__(self, me, rows, send, recv):
        self.me, self.rows, self.send, self.recv = me, rows, send, recv
        self.started = []

    def piece(self, dx, dc, chunk):
        row = self.me.token_block(dx, dc) * 256 + chunk * self.ROWS
        return self.rows.at[pl.ds(pl.multiple_of(row, self.ROWS), self.ROWS)]

    def push(self, ref, index, device):
        copy = remote(ref, ref, self.send, self.recv, index, device)
        copy.start()
        self.started.append(copy)

    def arrived(self, ref, index):
        remote(ref, ref, self.send, self.recv, index, self.me.core_device()).wait_recv()

    def begin(self, chunk):
        own = self.piece(0, 0, chunk)
        self.push(own, chunk, self.me.x_device())
        self.push(own, 4 + chunk, self.me.core_device())

    def pass_on(self, chunk):
        other = self.piece(1, 0, chunk)
        self.arrived(other, chunk)
        self.push(other, 8 + chunk, self.me.core_device())

    def finish(self):
        for chunk in range(self.CHUNKS):
            self.arrived(self.piece(0, 1, chunk), 4 + chunk)
        for chunk in range(self.CHUNKS):
            self.arrived(self.piece(1, 1, chunk), 8 + chunk)
        for copy in self.started:
            copy.wait_send()


class TokenScatter:
    COUNT = 12
    CHUNKS = 4
    ROWS = 64

    def __init__(self, me, part, near, far, relay, send, recv):
        self.me, self.part, self.near, self.far, self.relay = me, part, near, far, relay
        self.send, self.recv = send, recv
        self.started = []

    def piece(self, dx, dc, chunk):
        row = self.me.token_block(dx, dc) * 256 + chunk * self.ROWS
        return pl.ds(pl.multiple_of(row, self.ROWS), self.ROWS)

    def push(self, src, dst, index, device):
        copy = remote(src, dst, self.send, self.recv, index, device)
        copy.start()
        self.started.append(copy)

    def arrived(self, ref, index):
        remote(ref, ref, self.send, self.recv, index, self.me.core_device()).wait_recv()

    def begin_far(self, chunk):
        self.push(
            self.part.at[self.piece(1, 1, chunk)], self.relay.at[chunk], chunk, self.me.core_device()
        )

    def begin_near(self, chunk):
        self.push(
            self.part.at[self.piece(0, 1, chunk)], self.near.at[chunk], 4 + chunk, self.me.core_device()
        )

    def relay_on(self, chunk):
        self.arrived(self.relay.at[chunk], chunk)
        total = self.relay[chunk].astype(f32) + self.part[self.piece(1, 0, chunk), :].astype(f32)
        self.relay[chunk] = total.astype(bf16)
        self.push(self.relay.at[chunk], self.far.at[chunk], 8 + chunk, self.me.x_device())

    def total(self, chunk):
        self.arrived(self.near.at[chunk], 4 + chunk)
        self.arrived(self.far.at[chunk], 8 + chunk)
        return (
            self.part[self.piece(0, 0, chunk), :].astype(f32)
            + self.near[chunk].astype(f32)
            + self.far[chunk].astype(f32)
        )

    def finish(self):
        for copy in self.started:
            copy.wait_send()


def scatter_scratch():
    return [pltpu.VMEM((4, 64, 1024), bf16)] * 3 + [pltpu.SemaphoreType.DMA((12,))] * 2


class GradScatter:
    COUNT = 61

    def __init__(self, me, part, recv_half, recv_full, out_half, sums, last, send, recv):
        self.me, self.part = me, part
        self.recv_half, self.recv_full = recv_half, recv_full
        self.out_half, self.sums, self.last = out_half, sums, last
        self.send, self.recv = send, recv
        self.started = []

    def rows(self, kind, first, second, part=None):
        dz, dy = offsets(kind, first, second)
        row = self.me.at(dz, dy, kind) * 32
        if part is None:
            return pl.ds(pl.multiple_of(row, 32), 32)
        return pl.ds(pl.multiple_of(row + part * 16, 16), 16)

    def push(self, src, dst, index, device):
        copy = remote(src, dst, self.send, self.recv, index, device)
        copy.start()
        self.started.append(copy)

    def arrived(self, ref, index):
        remote(ref, ref, self.send, self.recv, index, self.me.dp_device(dh=1)).wait_recv()

    def along(self, kind, level, step):
        dz, dy = offsets(kind, step, 0) if level == 0 else offsets(kind, 0, step)
        return self.me.dp_device(dz=dz, dy=dy)

    def slot(self, kind, level, chunk):
        return kind * 5 + (4 if level == 0 else chunk)

    def source(self, kind, level, chunk, offset):
        if level == 1:
            first = (0, -1, 1, 2)[chunk]
            return self.part, self.rows(kind, first, offset), [
                self.rows(kind, first, offset, part) for part in range(2)
            ]
        chunk = {0: 0, -1: 1, 1: 2, 2: 3}[offset]
        base = (kind * 4 + chunk) * 32
        return self.sums, pl.ds(base, 32), [pl.ds(base, 16), pl.ds(base + 16, 16)]

    def far(self, kind, level, chunk):
        slot = self.slot(kind, level, chunk)
        ref, _, halves = self.source(kind, level, chunk, 2)
        self.push(ref.at[halves[0]], self.recv_half.at[slot, 0], slot * 6, self.along(kind, level, 1))
        self.push(
            ref.at[halves[1]], self.recv_half.at[slot, 1], slot * 6 + 1, self.along(kind, level, -1)
        )

    def near(self, kind, level, chunk):
        slot = self.slot(kind, level, chunk)
        for side in range(2):
            step = 1 if side == 0 else -1
            ref, _, halves = self.source(kind, level, chunk, step)
            self.push(
                ref.at[halves[1 - side]],
                self.recv_full.at[slot, side, pl.ds(16 * (1 - side), 16)],
                slot * 6 + 4 + side,
                self.along(kind, level, step),
            )

    def middle(self, kind, level, chunk, side):
        slot = self.slot(kind, level, chunk)
        step = 1 if side == 0 else -1
        ref, _, halves = self.source(kind, level, chunk, step)
        self.arrived(self.recv_half.at[slot, side], slot * 6 + side)
        total = ref[halves[side], :].astype(f32) + self.recv_half[slot, side].astype(f32)
        self.out_half[slot, side] = total.astype(bf16)
        self.push(
            self.out_half.at[slot, side],
            self.recv_full.at[slot, side, pl.ds(16 * side, 16)],
            slot * 6 + 2 + side,
            self.along(kind, level, step),
        )

    def total(self, kind, level, chunk):
        slot = self.slot(kind, level, chunk)
        ref, whole, _ = self.source(kind, level, chunk, 0)
        for side in range(2):
            full = self.recv_full.at[slot, side]
            self.arrived(full.at[pl.ds(16 * side, 16)], slot * 6 + 2 + side)
            self.arrived(full.at[pl.ds(16 * (1 - side), 16)], slot * 6 + 4 + side)
        return (
            ref[whole, :].astype(f32)
            + self.recv_full[slot, 0].astype(f32)
            + self.recv_full[slot, 1].astype(f32)
        )

    def begin(self):
        for push in (self.far, self.near):
            for chunk in range(4):
                for kind in range(2):
                    push(kind, 1, chunk)

    def step1(self, chunk):
        for kind in range(2):
            for side in range(2):
                self.middle(kind, 1, chunk, side)

    def step2(self, chunk):
        for kind in range(2):
            total = self.total(kind, 1, chunk)
            self.sums[pl.ds((kind * 4 + chunk) * 32, 32), :] = total.astype(bf16)

    def step3(self):
        for push in (self.far, self.near):
            for kind in range(2):
                push(kind, 0, 0)

    def step4(self):
        for kind in (1, 0):
            for side in range(2):
                self.middle(kind, 0, 0, side)

    def step5(self):
        self.last[0] = self.total(1, 0, 0).astype(bf16)
        self.push(self.last.at[0], self.last.at[1], 60, self.me.dp_device(dh=1))

    def result(self):
        own = self.total(0, 0, 0)
        self.arrived(self.last.at[1], 60)
        return own + self.last[1].astype(f32)

    def finish(self):
        for copy in self.started:
            copy.wait_send()


def grad_scratch(width):
    return [
        pltpu.VMEM((10, 2, 16, width), bf16),
        pltpu.VMEM((10, 2, 32, width), bf16),
        pltpu.VMEM((10, 2, 16, width), bf16),
        pltpu.VMEM((256, width), bf16),
        pltpu.VMEM((2, 32, width), bf16),
        pltpu.SemaphoreType.DMA((61,)),
        pltpu.SemaphoreType.DMA((61,)),
    ]


def row_scale(values):
    return lax.rsqrt(jnp.mean(values * values, axis=-1, keepdims=True) + epsilon)


def norm_back(values, inverse, gain_vec, upstream):
    weighted = upstream * gain_vec
    row_inner = jnp.mean(weighted * values, axis=-1, keepdims=True)
    return inverse * weighted - values * inverse * inverse * inverse * row_inner


def call(kernel, outs, scratch, number, args, flops=0, moved=0):
    return pl.pallas_call(
        kernel,
        out_shape=outs,
        in_specs=[VMEM_SPEC] * len(args),
        out_specs=[VMEM_SPEC] * len(outs),
        scratch_shapes=scratch,
        cost_estimate=pl.CostEstimate(flops=flops, bytes_accessed=moved, transcendentals=0),
        compiler_params=pltpu.CompilerParams(
            collective_id=number, has_side_effects=True, vmem_limit_bytes=VMEM_LIMIT
        ),
    )(*args)


def dot(a, b):
    return jnp.dot(a, b, preferred_element_type=f32)


def dot_tb(a, b):
    return lax.dot_general(a, b, (((1,), (1,)), ((), ())), preferred_element_type=f32)


def head_scale(values):
    return lax.rsqrt(jnp.mean(values * values, axis=0, keepdims=True) + epsilon)


def rotate(values, cosine, sine):
    front, back = values[:32], values[32:]
    return jnp.concatenate([front * cosine - back * sine, back * cosine + front * sine], axis=0)


def rotate_back(values, cosine, sine):
    front, back = values[:32], values[32:]
    return jnp.concatenate([front * cosine + back * sine, back * cosine - front * sine], axis=0)


def project_block(block, rows_ref, weight_ref, pre_ref, low):
    here = pl.ds(pl.multiple_of(block * 256, 256), 256)
    flat = dot(rows_ref[here, :], weight_ref[:, 0:512])
    turned = flat.T
    pre_ref[:, here] = turned[:384]
    cosine, sine = low.cos[:, here], low.sin[:, here]
    for head in range(4):
        u = turned[64 * head : 64 * head + 64]
        u = u * head_scale(u) * low.q_gain[...]
        low.q[pl.ds(64 * head, 64), here] = (rotate(u, cosine, sine) * 0.125).astype(bf16)
    for head in range(2):
        u = turned[256 + 64 * head : 320 + 64 * head]
        u = rotate(u * head_scale(u) * low.k_gain[...], cosine, sine)
        low.kt[head, block] = u.astype(bf16)
        low.k[head, here, :] = u.T.astype(bf16)
        u = turned[384 + 64 * head : 448 + 64 * head]
        low.vt[head, block, 0:64, :] = u.astype(bf16)
        low.vt[head, block, 64:80, :] = jnp.ones((16, 256), bf16)
        low.v[head, here, :] = u.T.astype(bf16)


def pair_lanes(ref, head, here):
    return jnp.concatenate(
        [ref[pl.ds(128 * head, 64), here], ref[pl.ds(128 * head + 64, 64), here]], axis=1
    )


def seen(low, number, key_block, diagonal):
    here = pl.ds(number * 256, 256)
    key_row = lax.broadcasted_iota(jnp.int32, (256, 256), 0) + key_block * 256
    mask = key_row >= low.start[:, here]
    if diagonal:
        query_row = lax.broadcasted_iota(jnp.int32, (256, 256), 1) + number * 256
        mask = jnp.logical_and(mask, key_row <= query_row)
    return jnp.concatenate([mask, mask], axis=1)


def forward_block(low, head, number, acc):
    here = pl.ds(number * 256, 256)
    queries = pair_lanes(low.q, head, here)

    def step(key_block, diagonal):
        keys = low.k[head, pl.ds(pl.multiple_of(key_block * 256, 256), 256), :]
        weight = jnp.exp(dot(keys, queries))
        weight = jnp.where(seen(low, number, key_block, diagonal), weight, 0.0).astype(bf16)
        return dot(low.vt[head, key_block], weight)

    acc[...] = step(number, True)
    if number > 0:

        @pl.loop(0, number)
        def _(key_block):
            acc[...] += step(key_block, False)

    total = acc[64:65, :]
    mixed = acc[0:64, :] / total
    low.lse[2 * head : 2 * head + 1, here] = jnp.log(total[:, 0:256])
    low.lse[2 * head + 1 : 2 * head + 2, here] = jnp.log(total[:, 256:512])
    low.mixed[pl.ds(128 * head, 64), here] = mixed[:, 0:256]
    low.mixed[pl.ds(128 * head + 64, 64), here] = mixed[:, 256:512]


def backward_prepare(block, rows_ref, weight_ref, low):
    here = pl.ds(pl.multiple_of(block * 256, 256), 256)
    turned = dot(rows_ref[here, :], weight_ref[:, 512:768]).T.astype(bf16)
    low.gt[:, here] = turned
    for head in range(4):
        part = turned[64 * head : 64 * head + 64].astype(f32)
        low.g[head, here, :] = part.T.astype(bf16)
        mixed = low.mixed[pl.ds(64 * head, 64), here]
        low.inner[head : head + 1, here] = jnp.sum(part * mixed, axis=0, keepdims=True)
        low.qn[head, here, :] = low.q[pl.ds(64 * head, 64), here].astype(f32).T.astype(bf16)


def backward_block(low, head, number, acc):
    here = pl.ds(number * 256, 256)
    queries = pair_lanes(low.q, head, here)
    upstream = pair_lanes(low.gt, head, here)
    query_rows = jnp.concatenate([low.qn[2 * head, here, :], low.qn[2 * head + 1, here, :]], axis=0)
    upstream_rows = jnp.concatenate([low.g[2 * head, here, :], low.g[2 * head + 1, here, :]], axis=0)

    def both(ref):
        return jnp.concatenate(
            [ref[2 * head : 2 * head + 1, here], ref[2 * head + 1 : 2 * head + 2, here]], axis=1
        )

    lse = both(low.lse)
    inner = both(low.inner)

    def step(key_block, diagonal):
        rows = pl.ds(pl.multiple_of(key_block * 256, 256), 256)
        weight = jnp.exp(dot(low.k[head, rows, :], queries) - lse)
        weight = jnp.where(seen(low, number, key_block, diagonal), weight, 0.0)
        score = weight * (dot(low.v[head, rows, :], upstream) - inner)
        score = score.astype(bf16)
        value_part = dot(weight.astype(bf16), upstream_rows)
        key_part = dot(score, query_rows)
        if diagonal:
            low.dv[head, rows, :] = value_part
            low.dk[head, rows, :] = key_part
        else:
            low.dv[head, rows, :] += value_part
            low.dk[head, rows, :] += key_part
        return dot(low.kt[head, key_block], score)

    acc[0:64, :] = step(number, True)
    if number > 0:

        @pl.loop(0, number)
        def _(key_block):
            acc[0:64, :] += step(key_block, False)

    low.dq[pl.ds(128 * head, 64), here] = acc[0:64, 0:256]
    low.dq[pl.ds(128 * head + 64, 64), here] = acc[0:64, 256:512]


def head_norm_back(values, gain, upstream):
    inverse = head_scale(values)
    weighted = upstream * gain
    inner = jnp.mean(weighted * values, axis=0, keepdims=True)
    return inverse * weighted - values * inverse * inverse * inverse * inner, inverse


def backward_finish(block, low, pre_ref, turned_ref, flat_ref):
    here = pl.ds(pl.multiple_of(block * 256, 256), 256)
    cosine, sine = low.cos[:, here], low.sin[:, here]
    q_part = jnp.zeros((64, 1), f32)
    k_part = jnp.zeros((64, 1), f32)
    for head in range(4):
        rows = pl.ds(64 * head, 64)
        upstream = rotate_back(low.dq[rows, here] * 0.125, cosine, sine)
        values = pre_ref[rows, here]
        grad, inverse = head_norm_back(values, low.q_gain[...], upstream)
        q_part = q_part + jnp.sum(upstream * values * inverse, axis=1, keepdims=True)
        turned_ref[rows, here] = grad.astype(bf16)
    for head in range(2):
        rows = pl.ds(256 + 64 * head, 64)
        upstream = rotate_back(low.dk[head, here, :].T, cosine, sine)
        values = pre_ref[rows, here]
        grad, inverse = head_norm_back(values, low.k_gain[...], upstream)
        k_part = k_part + jnp.sum(upstream * values * inverse, axis=1, keepdims=True)
        turned_ref[rows, here] = grad.astype(bf16)
        turned_ref[pl.ds(384 + 64 * head, 64), here] = low.dv[head, here, :].T.astype(bf16)
    flat_ref[here, :] = turned_ref[:, here].astype(f32).T.astype(bf16)
    return q_part, k_part


class GainSum:
    COUNT = 9

    def __init__(self, me, pair, ring_y, ring_z, send, recv):
        self.me, self.pair, self.ring_y, self.ring_z = me, pair, ring_y, ring_z
        self.send, self.recv = send, recv
        self.started = []

    def devices(self):
        return [self.me.dp_device(dy=2), self.me.dp_device(dz=2)]

    def swap(self, index, value, device):
        self.pair[index, 0] = value
        copy = remote(
            self.pair.at[index, 0], self.pair.at[index, 1], self.send, self.recv, index, device
        )
        copy.start()
        copy.wait_recv()
        self.started.append(copy)
        return value + self.pair[index, 1]

    def round(self, ring, index, value, place, device):
        ring[place] = value
        for step in range(3):
            copy = remote(
                ring.at[place], ring.at[place], self.send, self.recv, index + step, device(step + 1)
            )
            copy.start()
            self.started.append(copy)
        for step in range(3):
            source = lax.rem(place + (3 - step), 4)
            remote(
                ring.at[source], ring.at[source], self.send, self.recv, index + step, device(1)
            ).wait_recv()
        return (ring[0] + ring[1]) + (ring[2] + ring[3])

    def run(self, value):
        me = self.me
        value = self.swap(0, value, me.core_device())
        value = self.swap(1, value, me.x_device())
        value = self.swap(2, value, me.dp_device(dh=1))
        value = self.round(self.ring_y, 3, value, me.y, lambda step: me.dp_device(dy=step))
        value = self.round(self.ring_z, 6, value, me.z, lambda step: me.dp_device(dz=step))
        for copy in self.started:
            copy.wait_send()
        return value


def gain_scratch():
    return [
        pltpu.VMEM((3, 2, 8, 1024), f32),
        pltpu.VMEM((4, 8, 1024), f32),
        pltpu.VMEM((4, 8, 1024), f32),
        pltpu.SemaphoreType.DMA((9,)),
        pltpu.SemaphoreType.DMA((9,)),
    ]


class Fields:
    def __init__(self, **refs):
        self.__dict__.update(refs)


def gather_services(gather):
    steps = [gather.step1]
    for kind in range(2):
        for side in range(2):

            def hand_on(kind=kind, side=side):
                gather.pass_on(kind, 0, 0, side)
                gather.spread(kind, 1, 1 + side)

            steps.append(hand_on)
    steps.append(gather.step3)
    for chunk in range(4):

        def hand_bulk(chunk=chunk):
            for kind in range(2):
                for side in range(2):
                    gather.pass_on(kind, 1, chunk, side)

        steps.append(hand_bulk)
    return steps


def front_kernel(
    x_ref, gain_ref, ffn_gain_ref, attn_shard_ref, ffn_shard_ref, cot_ref,
    cos_ref, sin_ref, q_gain_ref, k_gain_ref, start_ref,
    attn_full, ffn_full, normed_ref, grad_rows_ref, pre_ref, mixed_ref, lse_ref, q_ref, kt_ref, k_ref, v_ref,
    middle_ref, rows_ref,
    vt, acc, part, near, far, relay, s_send, s_recv,
    a_send, a_recv, f_send, f_recv, n_send, n_recv, c_send, c_recv, g_send, g_recv,
):
    me = Place()
    attn = WeightGather(me, attn_full, a_send, a_recv)
    ffn = WeightGather(me, ffn_full, f_send, f_recv)
    tokens = TokenGather(me, normed_ref, n_send, n_recv)
    upstream = TokenGather(me, grad_rows_ref, c_send, c_recv)
    scatter = TokenScatter(me, part, near, far, relay, s_send, s_recv)
    second = TokenGather(me, rows_ref, g_send, g_recv)
    low = Fields(
        cos=cos_ref, sin=sin_ref, q_gain=q_gain_ref, k_gain=k_gain_ref, start=start_ref,
        q=q_ref, kt=kt_ref, k=k_ref, vt=vt, v=v_ref, lse=lse_ref, mixed=mixed_ref,
    )
    own_rows = pl.ds(pl.multiple_of(me.d * 32, 32), 32)
    own_tokens = pl.ds(pl.multiple_of(me.t * 256, 256), 256)
    attn_full[own_rows, :] = attn_shard_ref[...]
    ffn_full[own_rows, :] = ffn_shard_ref[...]
    values = x_ref[...].astype(f32)
    normed_ref[own_tokens, :] = (values * row_scale(values) * gain_ref[...]).astype(bf16)
    grad_rows_ref[own_tokens, :] = cot_ref[...]
    lse_ref[...] = jnp.zeros((8, 1024), f32)
    greet(ring_devices(me) + [me.core_device(), me.x_device()])
    attn.begin()
    for chunk in range(4):
        tokens.begin(chunk)
    attn.step1()
    attn.step2()
    attn.step3()
    attn.step4()
    ffn.begin()
    for chunk in range(4):
        tokens.pass_on(chunk)
    tokens.finish()
    attn.finish()
    services = gather_services(ffn)

    def serve(count=1):
        for _ in range(count):
            if services:
                services.pop(0)()

    serve()
    for chunk in range(4):
        upstream.begin(chunk)

    @pl.loop(0, 4)
    def _(block):
        project_block(block, normed_ref, attn_full, pre_ref, low)

    for number in range(4):
        for head in range(2):
            forward_block(low, head, number, acc)
            if number == 1 or number == 3:
                serve()
    for chunk in range(4):
        upstream.pass_on(chunk)

    def output_part(dx, dc):
        here = pl.ds(pl.multiple_of(me.token_block(dx, dc) * 256, 256), 256)
        flat = mixed_ref[:, here].T.astype(bf16)
        part[here, :] = dot_tb(flat, attn_full[:, 512:768]).astype(bf16)

    output_part(1, 1)
    for chunk in range(4):
        scatter.begin_far(chunk)
    output_part(1, 0)
    output_part(0, 1)
    for chunk in range(4):
        scatter.begin_near(chunk)
    output_part(0, 0)
    for chunk in range(4):
        scatter.relay_on(chunk)
    serve(2)
    for chunk in range(4):
        here = pl.ds(chunk * 64, 64)
        values = x_ref[here, :].astype(f32) + scatter.total(chunk)
        middle_ref[here, :] = values
        own = pl.ds(pl.multiple_of(me.t * 256 + chunk * 64, 64), 64)
        rows_ref[own, :] = (values * row_scale(values) * ffn_gain_ref[...]).astype(bf16)
        second.begin(chunk)
    serve()
    for chunk in range(4):
        second.pass_on(chunk)
    serve(10)
    upstream.finish()
    scatter.finish()
    second.finish()
    ffn.finish()


def scatter_services(scatter):
    steps = []
    for chunk in range(4):
        steps.append(functools.partial(scatter.step1, chunk))
    for chunk in range(4):
        steps.append(functools.partial(scatter.step2, chunk))
    steps.append(scatter.step3)
    steps.append(scatter.step4)
    steps.append(scatter.step5)
    return steps


def back_kernel(
    grad_ref, sum_ref, ffn_grad_ref, middle_ref, x_ref, gain_ref, ffn_gain_ref, cot_ref,
    cos_ref, sin_ref, q_gain_ref, k_gain_ref, start_ref,
    attn_full, normed_ref, pre_ref, mixed_ref, lse_ref, q_ref, kt_ref, k_ref, v_ref,
    out_ref, input_grad_ref, attn_shard_ref, ffn_shard_ref, gains_ref,
    middle_grad, rows, part, attn_grad, acc, gt, g, inner, qn, dk, dv, dq, turned, flat, *scratch,
):
    me = Place()
    scratch = list(scratch)

    def take(count):
        taken = scratch[:count]
        del scratch[:count]
        return taken

    first = TokenScatter(me, grad_ref, *take(5))
    second = TokenScatter(me, sum_ref, *take(5))
    third = TokenScatter(me, part, *take(5))
    gather = TokenGather(me, rows, *take(2))
    ffn = GradScatter(me, ffn_grad_ref, *take(7))
    attn = GradScatter(me, attn_grad, *take(7))
    gains = GainSum(me, *take(5))
    low = Fields(
        cos=cos_ref, sin=sin_ref, q_gain=q_gain_ref, k_gain=k_gain_ref, start=start_ref,
        q=q_ref, kt=kt_ref, k=k_ref, v=v_ref, lse=lse_ref, mixed=mixed_ref,
        gt=gt, g=g, inner=inner, qn=qn, dk=dk, dv=dv, dq=dq,
    )
    greet(ring_devices(me) + [me.core_device(), me.x_device()] + gains.devices())
    for chunk in range(4):
        first.begin_far(chunk)
    for chunk in range(4):
        first.begin_near(chunk)
    ffn.begin()
    for chunk in range(4):
        first.relay_on(chunk)
    for chunk in range(4):
        second.begin_far(chunk)
    for chunk in range(4):
        second.begin_near(chunk)
    services = scatter_services(ffn)

    def serve(count=1):
        for _ in range(count):
            if services:
                services.pop(0)()

    ffn_gain_total = jnp.zeros((1, 1024), f32)
    for chunk in range(4):
        here = pl.ds(chunk * 64, 64)
        upstream = first.total(chunk)
        values = middle_ref[here, :]
        inverse = row_scale(values)
        ffn_gain_total = ffn_gain_total + jnp.sum(upstream * values * inverse, axis=0, keepdims=True)
        total = cot_ref[here, :].astype(f32) + norm_back(values, inverse, ffn_gain_ref[...], upstream)
        middle_grad[here, :] = total
        own = pl.ds(pl.multiple_of(me.t * 256 + chunk * 64, 64), 64)
        rows[own, :] = total.astype(bf16)
        gather.begin(chunk)
    serve(2)
    for chunk in range(4):
        gather.pass_on(chunk)
    for chunk in range(4):
        second.relay_on(chunk)
    gather.finish()

    @pl.loop(0, 4)
    def _(block):
        backward_prepare(block, rows, attn_full, low)

    serve()
    for number in range(4):
        for head in range(2):
            backward_block(low, head, number, acc)
            if number >= 1 and head == 1 or number == 3:
                serve()
    for chunk in range(4):
        here = pl.ds(chunk * 64, 64)
        out_ref[here, :] = (middle_ref[here, :] + second.total(chunk)).astype(bf16)
    q_part = jnp.zeros((64, 1), f32)
    k_part = jnp.zeros((64, 1), f32)
    for block in range(4):
        q_more, k_more = backward_finish(block, low, pre_ref, turned, flat)
        q_part = q_part + q_more
        k_part = k_part + k_more
    gains_ref[...] = jnp.zeros((8, 1024), f32)
    gains_ref[1:2, :] = ffn_gain_total
    gains_ref[2:3, 0:64] = jnp.broadcast_to(q_part, (64, 128)).T[0:1, :]
    gains_ref[3:4, 0:64] = jnp.broadcast_to(k_part, (64, 128)).T[0:1, :]

    def first_part(dx, dc):
        here = pl.ds(pl.multiple_of(me.token_block(dx, dc) * 256, 256), 256)
        part[here, :] = dot_tb(flat[here, :], attn_full[:, 0:512]).astype(bf16)

    first_part(1, 1)
    for chunk in range(4):
        third.begin_far(chunk)
    first_part(1, 0)
    for chunk in range(4):
        third.relay_on(chunk)
    mixed_low = mixed_ref[...].astype(bf16)
    for tile in range(4):
        here = pl.ds(tile * 256, 256)
        attn_grad[here, 0:512] = dot(turned[...], normed_ref[:, here]).T.astype(bf16)
        attn_grad[here, 512:768] = dot(mixed_low, rows[:, here]).T.astype(bf16)
    attn.begin()
    first_part(0, 1)
    for chunk in range(4):
        third.begin_near(chunk)
    first_part(0, 0)
    serve(20)
    for chunk in range(4):
        attn.step1(chunk)
    attn_gain_total = jnp.zeros((1, 1024), f32)
    for chunk in range(4):
        here = pl.ds(chunk * 64, 64)
        upstream = third.total(chunk)
        values = x_ref[here, :].astype(f32)
        inverse = row_scale(values)
        attn_gain_total = attn_gain_total + jnp.sum(upstream * values * inverse, axis=0, keepdims=True)
        input_grad_ref[here, :] = middle_grad[here, :] + norm_back(
            values, inverse, gain_ref[...], upstream
        )
    gains_ref[0:1, :] = attn_gain_total
    for chunk in range(4):
        attn.step2(chunk)
    attn.step3()
    gains_ref[...] = gains.run(gains_ref[...])
    attn.step4()
    attn.step5()
    ffn_shard_ref[...] = ffn.result()
    attn_shard_ref[...] = attn.result()
    for transfer in (first, second, third, ffn, attn):
        transfer.finish()


def shape(rows, columns, kind):
    return jax.ShapeDtypeStruct((rows, columns), kind)


def sems(count):
    return [pltpu.SemaphoreType.DMA((count,))] * 2


def body(
    block_input,
    positions,
    attn_gain,
    w_query,
    w_key,
    w_value,
    w_output,
    q_gain,
    k_gain,
    ffn_gain,
    w_gate,
    w_up,
    w_down,
    cotangent,
):
    frequency = rope_base ** (-jnp.arange(32, dtype=f32) * 2.0 / 64)
    angles = frequency[:, None] * positions.astype(f32)[None, :]
    cosine, sine = jnp.cos(angles), jnp.sin(angles)
    start = (jnp.arange(1024, dtype=jnp.int32) - positions)[None, :]
    attn_shard = jnp.concatenate([w_query, w_key, w_value, w_output.T], axis=1)
    ffn_shard = jnp.concatenate([w_gate, w_up, w_down.T], axis=1)
    tables = (cosine, sine, q_gain[:, None], k_gain[:, None], start)
    square = shape(1024, 1024, bf16)
    (
        attn_full, ffn_full, normed_rows, grad_rows, pre, mixed, lse, q_low, kt_low, k_low, v_low,
        middle, second_rows,
    ) = call(
        front_kernel,
        [
            shape(1024, 768, bf16),
            shape(1024, 3456, bf16),
            square,
            square,
            shape(384, 1024, f32),
            shape(256, 1024, f32),
            shape(8, 1024, f32),
            shape(256, 1024, bf16),
            jax.ShapeDtypeStruct((2, 4, 64, 256), bf16),
            jax.ShapeDtypeStruct((2, 1024, 64), bf16),
            jax.ShapeDtypeStruct((2, 1024, 64), bf16),
            shape(256, 1024, f32),
            square,
        ],
        [pltpu.VMEM((2, 4, 80, 256), bf16), pltpu.VMEM((80, 512), f32), pltpu.VMEM((1024, 1024), bf16)]
        + scatter_scratch()
        + sems(41)
        + sems(41)
        + sems(12) * 3,
        0,
        (
            block_input, attn_gain[None, :], ffn_gain[None, :], attn_shard, ffn_shard, cotangent,
            *tables,
        ),
    )
    gate_full = ffn_full[:, 0:1152]
    up_full = ffn_full[:, 1152:2304]
    down_full = ffn_full[:, 2304:3456]
    gate_value = jnp.dot(second_rows, gate_full, preferred_element_type=f32)
    up_value = jnp.dot(second_rows, up_full, preferred_element_type=f32)
    sigmoid_gate = jax.nn.sigmoid(gate_value)
    silu_value = gate_value * sigmoid_gate
    activation = (silu_value * up_value).astype(bf16)
    ffn_part = jnp.einsum(
        "rf,df->rd", activation, down_full, preferred_element_type=f32
    ).astype(bf16)
    hidden_grad = jnp.einsum("rd,df->rf", grad_rows, down_full, preferred_element_type=f32)
    gate_low = (
        hidden_grad * up_value * sigmoid_gate * (1.0 + gate_value * (1.0 - sigmoid_gate))
    ).astype(bf16)
    up_low = (hidden_grad * silu_value).astype(bf16)
    second_part = (
        jnp.einsum("rf,df->rd", gate_low, gate_full, preferred_element_type=f32)
        + jnp.einsum("rf,df->rd", up_low, up_full, preferred_element_type=f32)
    ).astype(bf16)
    ffn_grad = jnp.concatenate(
        [
            jnp.einsum("rd,rf->df", second_rows, gate_low, preferred_element_type=f32).astype(bf16),
            jnp.einsum("rd,rf->df", second_rows, up_low, preferred_element_type=f32).astype(bf16),
            jnp.einsum("rf,rd->df", activation, grad_rows, preferred_element_type=f32).astype(bf16),
        ],
        axis=1,
    )
    layer_output, input_grad, attn_out, ffn_out, gains = call(
        back_kernel,
        [
            shape(256, 1024, bf16),
            shape(256, 1024, f32),
            shape(32, 768, f32),
            shape(32, 3456, f32),
            shape(8, 1024, f32),
        ],
        [
            pltpu.VMEM((256, 1024), f32),
            pltpu.VMEM((1024, 1024), bf16),
            pltpu.VMEM((1024, 1024), bf16),
            pltpu.VMEM((1024, 768), bf16),
            pltpu.VMEM((80, 512), f32),
            pltpu.VMEM((256, 1024), bf16),
            pltpu.VMEM((4, 1024, 64), bf16),
            pltpu.VMEM((8, 1024), f32),
            pltpu.VMEM((4, 1024, 64), bf16),
            pltpu.VMEM((2, 1024, 64), f32),
            pltpu.VMEM((2, 1024, 64), f32),
            pltpu.VMEM((256, 1024), f32),
            pltpu.VMEM((512, 1024), bf16),
            pltpu.VMEM((1024, 512), bf16),
        ]
        + scatter_scratch() * 3
        + sems(12)
        + grad_scratch(3456)
        + grad_scratch(768)
        + gain_scratch(),
        1,
        (
            second_part, ffn_part, ffn_grad, middle, block_input, attn_gain[None, :], ffn_gain[None, :],
            cotangent, *tables,
            attn_full, normed_rows, pre, mixed, lse, q_low, kt_low, k_low, v_low,
        ),
    )
    return (
        layer_output,
        input_grad,
        gains[0],
        attn_out[:, 0:256],
        attn_out[:, 256:384],
        attn_out[:, 384:512],
        attn_out[:, 512:768].T,
        gains[2, :64],
        gains[3, :64],
        gains[1],
        ffn_out[:, 0:1152],
        ffn_out[:, 1152:2304],
        ffn_out[:, 2304:3456].T,
    )


def solution(mesh):
    placed = (
        P(("dp", "tensor"), None),
        P("dp"),
        P(),
        P("dp", "tensor"),
        P("dp", "tensor"),
        P("dp", "tensor"),
        P("tensor", "dp"),
        P(),
        P(),
        P(),
        P("dp", "tensor"),
        P("dp", "tensor"),
        P("tensor", "dp"),
        P(("dp", "tensor"), None),
    )
    return jax.shard_map(
        body,
        mesh=mesh,
        in_specs=placed,
        out_specs=(
            P(("dp", "tensor"), None),
            P(("dp", "tensor"), None),
            P(),
            P("dp", "tensor"),
            P("dp", "tensor"),
            P("dp", "tensor"),
            P("tensor", "dp"),
            P(),
            P(),
            P(),
            P("dp", "tensor"),
            P("dp", "tensor"),
            P("tensor", "dp"),
        ),
        check_vma=False,
    )
```

```python
import functools
import math

import jax
import jax.numpy as jnp
from jax import lax
from jax.experimental import pallas as pl
from jax.experimental.pallas import tpu as pltpu
from jax.sharding import PartitionSpec as P

epsilon = 1e-05
rope_base = 1000000.0
f32 = jnp.float32
bf16 = jnp.bfloat16
MESH = pl.DeviceIdType.MESH
VMEM_SPEC = pl.BlockSpec(memory_space=pltpu.VMEM)
VMEM_LIMIT = 60 * 1024 * 1024


class Place:
    def __init__(self):
        d = lax.axis_index("dp")
        t = lax.axis_index("tensor")
        self.z = lax.div(d, 8)
        self.y = lax.rem(lax.div(d, 2), 4)
        self.h = lax.rem(d, 2)
        self.xl = lax.div(t, 2)
        self.core = lax.rem(t, 2)
        self.d = d
        self.t = t

    def at(self, dz=0, dy=0, dh=0):
        z = lax.rem(self.z + (dz + 4), 4)
        y = lax.rem(self.y + (dy + 4), 4)
        h = self.h if dh == 0 else 1 - self.h
        return z * 8 + y * 2 + h

    def dp_device(self, dz=0, dy=0, dh=0):
        return (self.at(dz, dy, dh), self.t)

    def core_device(self):
        return (self.d, self.xl * 2 + (1 - self.core))

    def x_device(self):
        return (self.d, (1 - self.xl) * 2 + self.core)

    def token_block(self, dx=0, dc=0):
        xl = self.xl if dx == 0 else 1 - self.xl
        core = self.core if dc == 0 else 1 - self.core
        return xl * 2 + core


def greet(devices):
    barrier = pltpu.get_barrier_semaphore()
    for device in devices:
        pl.semaphore_signal(barrier, inc=1, device_id=device, device_id_type=MESH)
    pl.semaphore_wait(barrier, len(devices))


def ring_devices(me):
    return [
        me.dp_device(dz=1),
        me.dp_device(dz=-1),
        me.dp_device(dy=1),
        me.dp_device(dy=-1),
        me.dp_device(dh=1),
    ]


def remote(src, dst, send, recv, index, device):
    return pltpu.make_async_remote_copy(
        src_ref=src,
        dst_ref=dst,
        send_sem=send.at[index],
        recv_sem=recv.at[index],
        device_id=device,
        device_id_type=MESH,
    )


def offsets(kind, first, second):
    return (first, second) if kind == 0 else (second, first)


class WeightGather:
    COUNT = 41

    def __init__(self, me, full, send, recv):
        self.me, self.full, self.send, self.recv = me, full, send, recv
        self.started = []

    def block(self, kind, first, second, part=None):
        dz, dy = offsets(kind, first, second)
        row = self.me.at(dz, dy, kind) * 32
        if part is None:
            return self.full.at[pl.ds(pl.multiple_of(row, 32), 32)]
        return self.full.at[pl.ds(pl.multiple_of(row + part * 16, 16), 16)]

    def push(self, ref, index, device):
        copy = remote(ref, ref, self.send, self.recv, index, device)
        copy.start()
        self.started.append(copy)

    def arrived(self, ref, index):
        remote(ref, ref, self.send, self.recv, index, self.me.dp_device(dh=1)).wait_recv()

    def along(self, kind, level, step):
        dz, dy = offsets(kind, step, 0) if level == 0 else offsets(kind, 0, step)
        return self.me.dp_device(dz=dz, dy=dy)

    def base(self, kind, level, chunk):
        return 1 + kind * 4 + chunk * 0 if level == 0 else 9 + kind * 16 + chunk * 4

    def spread(self, kind, level, chunk):
        first = (0, -1, 1, 2)[chunk] if level == 1 else 0
        base = self.base(kind, level, chunk)
        ref = self.block(kind, first, 0)
        self.push(ref, base, self.along(kind, level, 1))
        self.push(ref, base + 1, self.along(kind, level, -1))

    def pass_on(self, kind, level, chunk, side):
        first = (0, -1, 1, 2)[chunk] if level == 1 else 0
        base = self.base(kind, level, chunk)
        step = -1 if side == 0 else 1
        where = (step, 0) if level == 0 else (first, step)
        self.arrived(self.block(kind, *where), base + side)
        self.push(self.block(kind, *where, part=side), base + 2 + side, self.along(kind, level, -step))

    def last(self, kind, level, chunk):
        first = (0, -1, 1, 2)[chunk] if level == 1 else 0
        base = self.base(kind, level, chunk)
        where = (2, 0) if level == 0 else (first, 2)
        for side in range(2):
            self.arrived(self.block(kind, *where, part=side), base + 2 + side)

    def begin(self):
        self.push(self.block(0, 0, 0), 0, self.me.dp_device(dh=1))
        self.spread(0, 0, 0)
        self.spread(0, 1, 0)

    def step1(self):
        self.arrived(self.block(1, 0, 0), 0)
        self.spread(1, 0, 0)
        self.spread(1, 1, 0)

    def step2(self):
        for kind in range(2):
            for side in range(2):
                self.pass_on(kind, 0, 0, side)
                self.spread(kind, 1, 1 + side)

    def step3(self):
        for kind in range(2):
            self.last(kind, 0, 0)
            self.spread(kind, 1, 3)

    def step4(self):
        for chunk in range(4):
            for kind in range(2):
                for side in range(2):
                    self.pass_on(kind, 1, chunk, side)

    def finish(self):
        for chunk in range(4):
            for kind in range(2):
                self.last(kind, 1, chunk)
        for copy in self.started:
            copy.wait_send()


class TokenGather:
    COUNT = 12
    CHUNKS = 4
    ROWS = 64

    def __init__(self, me, rows, send, recv):
        self.me, self.rows, self.send, self.recv = me, rows, send, recv
        self.started = []

    def piece(self, dx, dc, chunk):
        row = self.me.token_block(dx, dc) * 256 + chunk * self.ROWS
        return self.rows.at[pl.ds(pl.multiple_of(row, self.ROWS), self.ROWS)]

    def push(self, ref, index, device):
        copy = remote(ref, ref, self.send, self.recv, index, device)
        copy.start()
        self.started.append(copy)

    def arrived(self, ref, index):
        remote(ref, ref, self.send, self.recv, index, self.me.core_device()).wait_recv()

    def begin(self, chunk):
        own = self.piece(0, 0, chunk)
        self.push(own, chunk, self.me.x_device())
        self.push(own, 4 + chunk, self.me.core_device())

    def pass_on(self, chunk):
        other = self.piece(1, 0, chunk)
        self.arrived(other, chunk)
        self.push(other, 8 + chunk, self.me.core_device())

    def finish(self):
        for chunk in range(self.CHUNKS):
            self.arrived(self.piece(0, 1, chunk), 4 + chunk)
        for chunk in range(self.CHUNKS):
            self.arrived(self.piece(1, 1, chunk), 8 + chunk)
        for copy in self.started:
            copy.wait_send()


class TokenScatter:
    COUNT = 12
    CHUNKS = 4
    ROWS = 64

    def __init__(self, me, part, near, far, relay, send, recv):
        self.me, self.part, self.near, self.far, self.relay = me, part, near, far, relay
        self.send, self.recv = send, recv
        self.started = []

    def piece(self, dx, dc, chunk):
        row = self.me.token_block(dx, dc) * 256 + chunk * self.ROWS
        return pl.ds(pl.multiple_of(row, self.ROWS), self.ROWS)

    def push(self, src, dst, index, device):
        copy = remote(src, dst, self.send, self.recv, index, device)
        copy.start()
        self.started.append(copy)

    def arrived(self, ref, index):
        remote(ref, ref, self.send, self.recv, index, self.me.core_device()).wait_recv()

    def begin_far(self, chunk):
        self.push(
            self.part.at[self.piece(1, 1, chunk)], self.relay.at[chunk], chunk, self.me.core_device()
        )

    def begin_near(self, chunk):
        self.push(
            self.part.at[self.piece(0, 1, chunk)], self.near.at[chunk], 4 + chunk, self.me.core_device()
        )

    def relay_on(self, chunk):
        self.arrived(self.relay.at[chunk], chunk)
        total = self.relay[chunk].astype(f32) + self.part[self.piece(1, 0, chunk), :].astype(f32)
        self.relay[chunk] = total.astype(bf16)
        self.push(self.relay.at[chunk], self.far.at[chunk], 8 + chunk, self.me.x_device())

    def total(self, chunk):
        self.arrived(self.near.at[chunk], 4 + chunk)
        self.arrived(self.far.at[chunk], 8 + chunk)
        return (
            self.part[self.piece(0, 0, chunk), :].astype(f32)
            + self.near[chunk].astype(f32)
            + self.far[chunk].astype(f32)
        )

    def finish(self):
        for copy in self.started:
            copy.wait_send()


def scatter_scratch():
    return [pltpu.VMEM((4, 64, 1024), bf16)] * 3 + [pltpu.SemaphoreType.DMA((12,))] * 2


class GradScatter:
    COUNT = 61

    def __init__(self, me, part, recv_half, recv_full, out_half, sums, last, send, recv):
        self.me, self.part = me, part
        self.recv_half, self.recv_full = recv_half, recv_full
        self.out_half, self.sums, self.last = out_half, sums, last
        self.send, self.recv = send, recv
        self.started = []

    def rows(self, kind, first, second, part=None):
        dz, dy = offsets(kind, first, second)
        row = self.me.at(dz, dy, kind) * 32
        if part is None:
            return pl.ds(pl.multiple_of(row, 32), 32)
        return pl.ds(pl.multiple_of(row + part * 16, 16), 16)

    def push(self, src, dst, index, device):
        copy = remote(src, dst, self.send, self.recv, index, device)
        copy.start()
        self.started.append(copy)

    def arrived(self, ref, index):
        remote(ref, ref, self.send, self.recv, index, self.me.dp_device(dh=1)).wait_recv()

    def along(self, kind, level, step):
        dz, dy = offsets(kind, step, 0) if level == 0 else offsets(kind, 0, step)
        return self.me.dp_device(dz=dz, dy=dy)

    def slot(self, kind, level, chunk):
        return kind * 5 + (4 if level == 0 else chunk)

    def source(self, kind, level, chunk, offset):
        if level == 1:
            first = (0, -1, 1, 2)[chunk]
            return self.part, self.rows(kind, first, offset), [
                self.rows(kind, first, offset, part) for part in range(2)
            ]
        chunk = {0: 0, -1: 1, 1: 2, 2: 3}[offset]
        base = (kind * 4 + chunk) * 32
        return self.sums, pl.ds(base, 32), [pl.ds(base, 16), pl.ds(base + 16, 16)]

    def far(self, kind, level, chunk):
        slot = self.slot(kind, level, chunk)
        ref, _, halves = self.source(kind, level, chunk, 2)
        self.push(ref.at[halves[0]], self.recv_half.at[slot, 0], slot * 6, self.along(kind, level, 1))
        self.push(
            ref.at[halves[1]], self.recv_half.at[slot, 1], slot * 6 + 1, self.along(kind, level, -1)
        )

    def near(self, kind, level, chunk):
        slot = self.slot(kind, level, chunk)
        for side in range(2):
            step = 1 if side == 0 else -1
            ref, _, halves = self.source(kind, level, chunk, step)
            self.push(
                ref.at[halves[1 - side]],
                self.recv_full.at[slot, side, pl.ds(16 * (1 - side), 16)],
                slot * 6 + 4 + side,
                self.along(kind, level, step),
            )

    def middle(self, kind, level, chunk, side):
        slot = self.slot(kind, level, chunk)
        step = 1 if side == 0 else -1
        ref, _, halves = self.source(kind, level, chunk, step)
        self.arrived(self.recv_half.at[slot, side], slot * 6 + side)
        total = ref[halves[side], :].astype(f32) + self.recv_half[slot, side].astype(f32)
        self.out_half[slot, side] = total.astype(bf16)
        self.push(
            self.out_half.at[slot, side],
            self.recv_full.at[slot, side, pl.ds(16 * side, 16)],
            slot * 6 + 2 + side,
            self.along(kind, level, step),
        )

    def total(self, kind, level, chunk):
        slot = self.slot(kind, level, chunk)
        ref, whole, _ = self.source(kind, level, chunk, 0)
        for side in range(2):
            full = self.recv_full.at[slot, side]
            self.arrived(full.at[pl.ds(16 * side, 16)], slot * 6 + 2 + side)
            self.arrived(full.at[pl.ds(16 * (1 - side), 16)], slot * 6 + 4 + side)
        return (
            ref[whole, :].astype(f32)
            + self.recv_full[slot, 0].astype(f32)
            + self.recv_full[slot, 1].astype(f32)
        )

    def begin(self):
        for push in (self.far, self.near):
            for chunk in range(4):
                for kind in range(2):
                    push(kind, 1, chunk)

    def step1(self, chunk):
        for kind in range(2):
            for side in range(2):
                self.middle(kind, 1, chunk, side)

    def step2(self, chunk):
        for kind in range(2):
            total = self.total(kind, 1, chunk)
            self.sums[pl.ds((kind * 4 + chunk) * 32, 32), :] = total.astype(bf16)

    def step3(self):
        for push in (self.far, self.near):
            for kind in range(2):
                push(kind, 0, 0)

    def step4(self):
        for kind in (1, 0):
            for side in range(2):
                self.middle(kind, 0, 0, side)

    def step5(self):
        self.last[0] = self.total(1, 0, 0).astype(bf16)
        self.push(self.last.at[0], self.last.at[1], 60, self.me.dp_device(dh=1))

    def result(self):
        own = self.total(0, 0, 0)
        self.arrived(self.last.at[1], 60)
        return own + self.last[1].astype(f32)

    def finish(self):
        for copy in self.started:
            copy.wait_send()


def grad_scratch(width):
    return [
        pltpu.VMEM((10, 2, 16, width), bf16),
        pltpu.VMEM((10, 2, 32, width), bf16),
        pltpu.VMEM((10, 2, 16, width), bf16),
        pltpu.VMEM((256, width), bf16),
        pltpu.VMEM((2, 32, width), bf16),
        pltpu.SemaphoreType.DMA((61,)),
        pltpu.SemaphoreType.DMA((61,)),
    ]


def row_scale(values):
    return lax.rsqrt(jnp.mean(values * values, axis=-1, keepdims=True) + epsilon)


def norm_back(values, inverse, gain_vec, upstream):
    weighted = upstream * gain_vec
    row_inner = jnp.mean(weighted * values, axis=-1, keepdims=True)
    return inverse * weighted - values * inverse * inverse * inverse * row_inner


def call(kernel, outs, scratch, number, args, flops=0, moved=0):
    return pl.pallas_call(
        kernel,
        out_shape=outs,
        in_specs=[VMEM_SPEC] * len(args),
        out_specs=[VMEM_SPEC] * len(outs),
        scratch_shapes=scratch,
        cost_estimate=pl.CostEstimate(flops=flops, bytes_accessed=moved, transcendentals=0),
        compiler_params=pltpu.CompilerParams(
            collective_id=number, has_side_effects=True, vmem_limit_bytes=VMEM_LIMIT
        ),
    )(*args)


def dot(a, b):
    return jnp.dot(a, b, preferred_element_type=f32)


def dot_tb(a, b):
    return lax.dot_general(a, b, (((1,), (1,)), ((), ())), preferred_element_type=f32)


def head_scale(values):
    return lax.rsqrt(jnp.mean(values * values, axis=0, keepdims=True) + epsilon)


def rotate(values, cosine, sine):
    front, back = values[:32], values[32:]
    return jnp.concatenate([front * cosine - back * sine, back * cosine + front * sine], axis=0)


def rotate_back(values, cosine, sine):
    front, back = values[:32], values[32:]
    return jnp.concatenate([front * cosine + back * sine, back * cosine - front * sine], axis=0)


def project_block(block, rows_ref, weight_ref, pre_ref, low):
    here = pl.ds(pl.multiple_of(block * 256, 256), 256)
    flat = dot(rows_ref[here, :], weight_ref[:, 0:512])
    turned = flat.T
    pre_ref[:, here] = turned[:384]
    cosine, sine = low.cos[:, here], low.sin[:, here]
    for head in range(4):
        u = turned[64 * head : 64 * head + 64]
        u = u * head_scale(u) * low.q_gain[...]
        low.q[pl.ds(64 * head, 64), here] = (rotate(u, cosine, sine) * 0.125).astype(bf16)
    for head in range(2):
        u = turned[256 + 64 * head : 320 + 64 * head]
        u = rotate(u * head_scale(u) * low.k_gain[...], cosine, sine)
        low.kt[head, block] = u.astype(bf16)
        low.k[head, here, :] = u.T.astype(bf16)
        u = turned[384 + 64 * head : 448 + 64 * head]
        low.vt[head, block, 0:64, :] = u.astype(bf16)
        low.vt[head, block, 64:80, :] = jnp.ones((16, 256), bf16)
        low.v[head, here, :] = u.T.astype(bf16)


def pair_lanes(ref, head, here):
    return jnp.concatenate(
        [ref[pl.ds(128 * head, 64), here], ref[pl.ds(128 * head + 64, 64), here]], axis=1
    )


def seen(low, number, key_block, diagonal):
    here = pl.ds(number * 256, 256)
    key_row = lax.broadcasted_iota(jnp.int32, (256, 256), 0) + key_block * 256
    mask = key_row >= low.start[:, here]
    if diagonal:
        query_row = lax.broadcasted_iota(jnp.int32, (256, 256), 1) + number * 256
        mask = jnp.logical_and(mask, key_row <= query_row)
    return jnp.concatenate([mask, mask], axis=1)


def forward_block(low, head, number, acc):
    here = pl.ds(number * 256, 256)
    queries = pair_lanes(low.q, head, here)

    def step(key_block, diagonal):
        keys = low.k[head, pl.ds(pl.multiple_of(key_block * 256, 256), 256), :]
        weight = jnp.exp(dot(keys, queries))
        weight = jnp.where(seen(low, number, key_block, diagonal), weight, 0.0).astype(bf16)
        return dot(low.vt[head, key_block], weight)

    acc[...] = step(number, True)
    if number > 0:

        @pl.loop(0, number)
        def _(key_block):
            acc[...] += step(key_block, False)

    total = acc[64:65, :]
    mixed = acc[0:64, :] / total
    low.lse[2 * head : 2 * head + 1, here] = jnp.log(total[:, 0:256])
    low.lse[2 * head + 1 : 2 * head + 2, here] = jnp.log(total[:, 256:512])
    low.mixed[pl.ds(128 * head, 64), here] = mixed[:, 0:256]
    low.mixed[pl.ds(128 * head + 64, 64), here] = mixed[:, 256:512]


def backward_prepare(block, rows_ref, weight_ref, low):
    here = pl.ds(pl.multiple_of(block * 256, 256), 256)
    turned = dot(rows_ref[here, :], weight_ref[:, 512:768]).T.astype(bf16)
    low.gt[:, here] = turned
    for head in range(4):
        part = turned[64 * head : 64 * head + 64].astype(f32)
        low.g[head, here, :] = part.T.astype(bf16)
        mixed = low.mixed[pl.ds(64 * head, 64), here]
        low.inner[head : head + 1, here] = jnp.sum(part * mixed, axis=0, keepdims=True)
        low.qn[head, here, :] = low.q[pl.ds(64 * head, 64), here].astype(f32).T.astype(bf16)


def backward_block(low, head, number, acc):
    here = pl.ds(number * 256, 256)
    queries = pair_lanes(low.q, head, here)
    upstream = pair_lanes(low.gt, head, here)
    query_rows = jnp.concatenate([low.qn[2 * head, here, :], low.qn[2 * head + 1, here, :]], axis=0)
    upstream_rows = jnp.concatenate([low.g[2 * head, here, :], low.g[2 * head + 1, here, :]], axis=0)

    def both(ref):
        return jnp.concatenate(
            [ref[2 * head : 2 * head + 1, here], ref[2 * head + 1 : 2 * head + 2, here]], axis=1
        )

    lse = both(low.lse)
    inner = both(low.inner)

    def step(key_block, diagonal):
        rows = pl.ds(pl.multiple_of(key_block * 256, 256), 256)
        weight = jnp.exp(dot(low.k[head, rows, :], queries) - lse)
        weight = jnp.where(seen(low, number, key_block, diagonal), weight, 0.0)
        score = weight * (dot(low.v[head, rows, :], upstream) - inner)
        score = score.astype(bf16)
        value_part = dot(weight.astype(bf16), upstream_rows)
        key_part = dot(score, query_rows)
        if diagonal:
            low.dv[head, rows, :] = value_part
            low.dk[head, rows, :] = key_part
        else:
            low.dv[head, rows, :] += value_part
            low.dk[head, rows, :] += key_part
        return dot(low.kt[head, key_block], score)

    acc[0:64, :] = step(number, True)
    if number > 0:

        @pl.loop(0, number)
        def _(key_block):
            acc[0:64, :] += step(key_block, False)

    low.dq[pl.ds(128 * head, 64), here] = acc[0:64, 0:256]
    low.dq[pl.ds(128 * head + 64, 64), here] = acc[0:64, 256:512]


def head_norm_back(values, gain, upstream):
    inverse = head_scale(values)
    weighted = upstream * gain
    inner = jnp.mean(weighted * values, axis=0, keepdims=True)
    return inverse * weighted - values * inverse * inverse * inverse * inner, inverse


def backward_finish(block, low, pre_ref, turned_ref, flat_ref):
    here = pl.ds(pl.multiple_of(block * 256, 256), 256)
    cosine, sine = low.cos[:, here], low.sin[:, here]
    q_part = jnp.zeros((64, 1), f32)
    k_part = jnp.zeros((64, 1), f32)
    for head in range(4):
        rows = pl.ds(64 * head, 64)
        upstream = rotate_back(low.dq[rows, here] * 0.125, cosine, sine)
        values = pre_ref[rows, here]
        grad, inverse = head_norm_back(values, low.q_gain[...], upstream)
        q_part = q_part + jnp.sum(upstream * values * inverse, axis=1, keepdims=True)
        turned_ref[rows, here] = grad.astype(bf16)
    for head in range(2):
        rows = pl.ds(256 + 64 * head, 64)
        upstream = rotate_back(low.dk[head, here, :].T, cosine, sine)
        values = pre_ref[rows, here]
        grad, inverse = head_norm_back(values, low.k_gain[...], upstream)
        k_part = k_part + jnp.sum(upstream * values * inverse, axis=1, keepdims=True)
        turned_ref[rows, here] = grad.astype(bf16)
        turned_ref[pl.ds(384 + 64 * head, 64), here] = low.dv[head, here, :].T.astype(bf16)
    flat_ref[here, :] = turned_ref[:, here].astype(f32).T.astype(bf16)
    return q_part, k_part


class GainSum:
    def __init__(self, me, row, plane, send, recv):
        self.me, self.row, self.plane = me, row, plane
        self.send, self.recv = send, recv
        self.started = []

    def row_devices(self):
        me = self.me
        return [
            (me.at(dh=step // 4), lax.rem(me.t + step % 4, 4)) for step in range(1, 8)
        ]

    def plane_devices(self):
        return [self.me.dp_device(dz=step // 4, dy=step % 4) for step in range(1, 16)]

    def exchange(self, slots, place, value, devices, base):
        slots[place] = value
        for step, device in enumerate(devices):
            copy = remote(
                slots.at[place], slots.at[place], self.send, self.recv, base + step, device
            )
            copy.start()
            self.started.append(copy)
        for step, device in enumerate(devices):
            remote(
                slots.at[place], slots.at[place], self.send, self.recv, base + step, device
            ).wait_recv()
        total = slots[0]
        for slot in range(1, len(devices) + 1):
            total = total + slots[slot]
        return total

    def run(self, value):
        me = self.me
        value = self.exchange(self.row, me.h * 4 + me.t, value, self.row_devices(), 0)
        value = self.exchange(self.plane, me.z * 4 + me.y, value, self.plane_devices(), 7)
        for copy in self.started:
            copy.wait_send()
        return value


def gain_scratch():
    return [
        pltpu.VMEM((8, 24, 128), f32),
        pltpu.VMEM((16, 24, 128), f32),
        pltpu.SemaphoreType.DMA((22,)),
        pltpu.SemaphoreType.DMA((22,)),
    ]


class Fields:
    def __init__(self, **refs):
        self.__dict__.update(refs)


def gather_services(gather):
    steps = [gather.step1]
    for kind in range(2):
        for side in range(2):

            def hand_on(kind=kind, side=side):
                gather.pass_on(kind, 0, 0, side)
                gather.spread(kind, 1, 1 + side)

            steps.append(hand_on)
    steps.append(gather.step3)
    for chunk in range(4):

        def hand_bulk(chunk=chunk):
            for kind in range(2):
                for side in range(2):
                    gather.pass_on(kind, 1, chunk, side)

        steps.append(hand_bulk)
    return steps


def column(row_ref):
    return jnp.broadcast_to(row_ref[...], (128, 64)).T[:, 0:1]


def tables(position_ref, q_gain_ref, k_gain_ref, cos, sin, start, q_gain, k_gain):
    place = lax.broadcasted_iota(jnp.int32, (32, 1024), 0).astype(f32)
    frequency = jnp.exp(place * (-math.log(rope_base) * 2.0 / 64))
    angles = frequency * position_ref[...].astype(f32)
    cos[...] = jnp.cos(angles)
    sin[...] = jnp.sin(angles)
    start[...] = lax.broadcasted_iota(jnp.int32, (1, 1024), 1) - position_ref[...]
    q_gain[...] = column(q_gain_ref)
    k_gain[...] = column(k_gain_ref)


def table_scratch():
    return [
        pltpu.VMEM((32, 1024), f32),
        pltpu.VMEM((32, 1024), f32),
        pltpu.VMEM((1, 1024), jnp.int32),
        pltpu.VMEM((64, 1), f32),
        pltpu.VMEM((64, 1), f32),
    ]


def turn(values):
    return values.astype(f32).T.astype(bf16)


def ffn_block(here, low):
    rows = low.rows[here, :]
    gate = dot(rows, low.full[:, 0:1152])
    up = dot(rows, low.full[:, 1152:2304])
    sigmoid = jax.nn.sigmoid(gate)
    silu = gate * sigmoid
    activation = (silu * up).astype(bf16)
    low.activation[here, :] = activation
    hidden = dot(low.grad_rows[here, :], low.full[:, 2304:3456])
    gate_low = (hidden * up * sigmoid * (1.0 + gate * (1.0 - sigmoid))).astype(bf16)
    up_low = (hidden * silu).astype(bf16)
    low.gate_low[here, :] = gate_low
    low.up_low[here, :] = up_low
    low.ffn_part[here, :] = dot_tb(activation, low.full[:, 2304:3456]).astype(bf16)
    low.part[here, :] = (
        dot_tb(gate_low, low.full[:, 0:1152]) + dot_tb(up_low, low.full[:, 1152:2304])
    ).astype(bf16)
    low.rows_t[:, here] = turn(rows)


def front_kernel(
    x_ref, position_ref, gain_ref, wq_ref, wk_ref, wv_ref, wo_ref, q_gain_ref, k_gain_ref, ffn_gain_ref,
    wg_ref, wu_ref, wd_ref, cot_ref,
    attn_full, normed_ref, pre_ref, mixed_ref, lse_ref, q_ref, kt_ref, k_ref, v_ref,
    ffn_grad, middle_grad, out_ref, ffn_gain_part,
    ffn_full, grad_rows, grad_rows_t, rows_ref, rows_t, middle, vt, acc, part, ffn_part,
    activation, gate_low, up_low, *scratch,
):
    me = Place()
    scratch = list(scratch)

    def take(count):
        taken = scratch[:count]
        del scratch[:count]
        return taken

    cos, sin, start, q_gain, k_gain = take(5)
    buffers = take(5)
    scatter = TokenScatter(me, part, *buffers)
    first = TokenScatter(me, part, *buffers)
    last = TokenScatter(me, ffn_part, *take(5))
    attn = WeightGather(me, attn_full, *take(2))
    ffn = WeightGather(me, ffn_full, *take(2))
    tokens = TokenGather(me, normed_ref, *take(2))
    upstream = TokenGather(me, grad_rows, *take(2))
    second = TokenGather(me, rows_ref, *take(2))
    low = Fields(
        cos=cos, sin=sin, q_gain=q_gain, k_gain=k_gain, start=start,
        q=q_ref, kt=kt_ref, k=k_ref, vt=vt, v=v_ref, lse=lse_ref, mixed=mixed_ref,
        rows=rows_ref, rows_t=rows_t, full=ffn_full, grad_rows=grad_rows, part=part, ffn_part=ffn_part,
        activation=activation, gate_low=gate_low, up_low=up_low,
    )
    own_rows = pl.ds(pl.multiple_of(me.d * 32, 32), 32)
    own_tokens = pl.ds(pl.multiple_of(me.t * 256, 256), 256)
    attn_full[own_rows, 0:256] = wq_ref[...]
    attn_full[own_rows, 256:384] = wk_ref[...]
    attn_full[own_rows, 384:512] = wv_ref[...]
    attn_full[own_rows, 512:768] = turn(wo_ref[...])
    values = x_ref[...].astype(f32)
    normed_ref[own_tokens, :] = (values * row_scale(values) * gain_ref[...]).astype(bf16)
    greet(ring_devices(me) + [me.core_device(), me.x_device()])
    attn.begin()
    for chunk in range(4):
        tokens.begin(chunk)
    ffn_full[own_rows, 0:1152] = wg_ref[...]
    ffn_full[own_rows, 1152:2304] = wu_ref[...]
    ffn_full[own_rows, 2304:3456] = turn(wd_ref[...])
    grad_rows[own_tokens, :] = cot_ref[...]
    attn.step1()
    lse_ref[...] = jnp.zeros((8, 1024), f32)
    tables(position_ref, q_gain_ref, k_gain_ref, cos, sin, start, q_gain, k_gain)
    attn.step2()
    attn.step3()
    attn.step4()
    ffn.begin()
    for chunk in range(4):
        tokens.pass_on(chunk)
    tokens.finish()
    attn.finish()
    services = gather_services(ffn)

    def serve(count=1):
        for _ in range(count):
            if services:
                services.pop(0)()

    serve()
    for chunk in range(4):
        upstream.begin(chunk)

    @pl.loop(0, 4)
    def _(block):
        project_block(block, normed_ref, attn_full, pre_ref, low)

    for number in range(4):
        for head in range(2):
            forward_block(low, head, number, acc)
            if number == 1 or number == 3:
                serve()
    for chunk in range(4):
        upstream.pass_on(chunk)

    def output_part(dx, dc):
        here = pl.ds(pl.multiple_of(me.token_block(dx, dc) * 256, 256), 256)
        flat = mixed_ref[:, here].T.astype(bf16)
        part[here, :] = dot_tb(flat, attn_full[:, 512:768]).astype(bf16)

    output_part(1, 1)
    for chunk in range(4):
        scatter.begin_far(chunk)
    output_part(1, 0)
    output_part(0, 1)
    for chunk in range(4):
        scatter.begin_near(chunk)
    output_part(0, 0)
    for chunk in range(4):
        scatter.relay_on(chunk)
    serve(2)
    upstream.finish()
    grad_rows_t[...] = turn(grad_rows[...])
    for chunk in range(4):
        here = pl.ds(chunk * 64, 64)
        values = x_ref[here, :].astype(f32) + scatter.total(chunk)
        middle[here, :] = values
        own = pl.ds(pl.multiple_of(me.t * 256 + chunk * 64, 64), 64)
        rows_ref[own, :] = (values * row_scale(values) * ffn_gain_ref[...]).astype(bf16)
        if chunk == 3:
            scatter.finish()
        second.begin(chunk)
    serve(20)
    ffn.finish()

    passes = [
        remote(piece, piece, second.send, second.recv, 8 + chunk, me.core_device())
        for chunk, piece in enumerate(second.piece(1, 0, chunk) for chunk in range(4))
    ]

    @pl.loop(0, 4)
    def _(turn_number):
        @pl.when(turn_number == 1)
        def _():
            for chunk in range(4):
                second.arrived(second.piece(0, 1, chunk), 4 + chunk)

        @pl.when(turn_number == 2)
        def _():
            for chunk in range(4):
                second.arrived(second.piece(1, 0, chunk), chunk)
                passes[chunk].start()

        @pl.when(turn_number == 3)
        def _():
            for chunk in range(4):
                second.arrived(second.piece(1, 1, chunk), 8 + chunk)

        block = lax.rem(me.xl + lax.div(turn_number, 2), 2) * 2 + lax.rem(me.core + lax.rem(turn_number, 2), 2)
        ffn_block(pl.ds(pl.multiple_of(block * 256, 256), 256), low)

    for copy in second.started + passes:
        copy.wait_send()

    def weight_tile(tile):
        here = pl.ds(tile * 256, 256)
        ffn_grad[here, 0:1152] = dot(rows_t[here, :], gate_low[...]).astype(bf16)
        ffn_grad[here, 1152:2304] = dot(rows_t[here, :], up_low[...]).astype(bf16)
        ffn_grad[here, 2304:3456] = dot(grad_rows_t[here, :], activation[...]).astype(bf16)

    for chunk in range(4):
        first.begin_far(chunk)
    for chunk in range(4):
        first.begin_near(chunk)
    weight_tile(0)
    for chunk in range(4):
        first.relay_on(chunk)
    for chunk in range(4):
        last.begin_far(chunk)
    for chunk in range(4):
        last.begin_near(chunk)
    weight_tile(1)
    for chunk in range(4):
        last.relay_on(chunk)
    weight_tile(2)
    weight_tile(3)
    gain_total = jnp.zeros((1, 1024), f32)
    for chunk in range(4):
        here = pl.ds(chunk * 64, 64)
        grad = first.total(chunk)
        values = middle[here, :]
        inverse = row_scale(values)
        gain_total = gain_total + jnp.sum(grad * values * inverse, axis=0, keepdims=True)
        middle_grad[here, :] = cot_ref[here, :].astype(f32) + norm_back(
            values, inverse, ffn_gain_ref[...], grad
        )
    ffn_gain_part[...] = gain_total
    for chunk in range(4):
        here = pl.ds(chunk * 64, 64)
        out_ref[here, :] = (middle[here, :] + last.total(chunk)).astype(bf16)
    first.finish()
    last.finish()


def scatter_services(scatter):
    steps = []
    for chunk in range(4):
        steps.append(functools.partial(scatter.step1, chunk))
    for chunk in range(4):
        steps.append(functools.partial(scatter.step2, chunk))
    steps.append(scatter.step3)
    steps.append(scatter.step4)
    steps.append(scatter.step5)
    return steps


def back_kernel(
    ffn_grad, middle_grad, ffn_gain_part, x_ref, position_ref, gain_ref, q_gain_ref, k_gain_ref,
    attn_full, normed_ref, pre_ref, mixed_ref, lse_ref, q_ref, kt_ref, k_ref, v_ref,
    input_grad_ref, attn_shard_ref, ffn_shard_ref, gains_ref,
    rows, part, attn_grad, acc, gt, g, inner, qn, dk, dv, dq, turned, flat, gain_rows, *scratch,
):
    me = Place()
    scratch = list(scratch)

    def take(count):
        taken = scratch[:count]
        del scratch[:count]
        return taken

    cos, sin, start, q_gain, k_gain = take(5)
    third = TokenScatter(me, part, *take(5))
    gather = TokenGather(me, rows, *take(2))
    ffn = GradScatter(me, ffn_grad, *take(7))
    attn = GradScatter(me, attn_grad, *take(7))
    gains = GainSum(me, *take(4))
    low = Fields(
        cos=cos, sin=sin, q_gain=q_gain, k_gain=k_gain, start=start,
        q=q_ref, kt=kt_ref, k=k_ref, v=v_ref, lse=lse_ref, mixed=mixed_ref,
        gt=gt, g=g, inner=inner, qn=qn, dk=dk, dv=dv, dq=dq,
    )
    own_tokens = pl.ds(pl.multiple_of(me.t * 256, 256), 256)
    rows[own_tokens, :] = middle_grad[...].astype(bf16)
    greet(gains.row_devices() + gains.plane_devices())
    for chunk in range(4):
        gather.begin(chunk)
    ffn.begin()
    tables(position_ref, q_gain_ref, k_gain_ref, cos, sin, start, q_gain, k_gain)
    services = scatter_services(ffn)

    def serve(count=1):
        for _ in range(count):
            if services:
                services.pop(0)()

    for chunk in range(4):
        gather.pass_on(chunk)
    serve(1)
    gather.finish()

    @pl.loop(0, 4)
    def _(block):
        backward_prepare(block, rows, attn_full, low)

    serve(2)
    for number in range(4):
        for head in range(2):
            backward_block(low, head, number, acc)
            if number >= 1 and head == 1 or number == 3:
                serve()
    q_part = jnp.zeros((64, 1), f32)
    k_part = jnp.zeros((64, 1), f32)
    for block in range(4):
        q_more, k_more = backward_finish(block, low, pre_ref, turned, flat)
        q_part = q_part + q_more
        k_part = k_part + k_more

    def first_part(dx, dc):
        here = pl.ds(pl.multiple_of(me.token_block(dx, dc) * 256, 256), 256)
        part[here, :] = dot_tb(flat[here, :], attn_full[:, 0:512]).astype(bf16)

    first_part(1, 1)
    for chunk in range(4):
        third.begin_far(chunk)
    first_part(1, 0)
    for chunk in range(4):
        third.relay_on(chunk)
    mixed_low = mixed_ref[...].astype(bf16)
    for tile in range(4):
        here = pl.ds(tile * 256, 256)
        attn_grad[here, 0:512] = dot(turned[...], normed_ref[:, here]).T.astype(bf16)
        attn_grad[here, 512:768] = dot(mixed_low, rows[:, here]).T.astype(bf16)
    attn.begin()
    first_part(0, 1)
    for chunk in range(4):
        third.begin_near(chunk)
    first_part(0, 0)
    gain_rows[16:24, :] = jnp.zeros((8, 128), f32)
    gain_rows[16:17, 0:64] = jnp.broadcast_to(q_part, (64, 128)).T[0:1, :]
    gain_rows[17:18, 0:64] = jnp.broadcast_to(k_part, (64, 128)).T[0:1, :]
    serve(20)
    for chunk in range(4):
        attn.step1(chunk)
    gain_total = jnp.zeros((1, 1024), f32)
    for chunk in range(4):
        here = pl.ds(chunk * 64, 64)
        upstream = third.total(chunk)
        values = x_ref[here, :].astype(f32)
        inverse = row_scale(values)
        gain_total = gain_total + jnp.sum(upstream * values * inverse, axis=0, keepdims=True)
        input_grad_ref[here, :] = middle_grad[here, :] + norm_back(
            values, inverse, gain_ref[...], upstream
        )
    for part_number in range(8):
        lanes = slice(128 * part_number, 128 * part_number + 128)
        gain_rows[part_number : part_number + 1, :] = gain_total[:, lanes]
        gain_rows[8 + part_number : 9 + part_number, :] = ffn_gain_part[:, lanes]
    for chunk in range(4):
        attn.step2(chunk)
    attn.step3()
    gains_ref[...] = gains.run(gain_rows[...])
    attn.step4()
    attn.step5()
    ffn_shard_ref[...] = ffn.result()
    attn_shard_ref[...] = attn.result()
    for transfer in (third, ffn, attn):
        transfer.finish()


def unpack_kernel(
    out_ref, input_grad_ref, attn_ref, ffn_ref, gains_ref,
    out, input_grad, attn_gain, wq, wk, wv, wo, q_gain, k_gain, ffn_gain, wg, wu, wd,
):
    out[...] = out_ref[...]
    input_grad[...] = input_grad_ref[...]
    for part in range(8):
        lanes = slice(128 * part, 128 * part + 128)
        attn_gain[:, lanes] = gains_ref[part : part + 1, :]
        ffn_gain[:, lanes] = gains_ref[8 + part : 9 + part, :]
    q_gain[...] = gains_ref[16:17, 0:64]
    k_gain[...] = gains_ref[17:18, 0:64]
    wq[...] = attn_ref[:, 0:256]
    wk[...] = attn_ref[:, 256:384]
    wv[...] = attn_ref[:, 384:512]
    wo[...] = attn_ref[:, 512:768].T
    wg[...] = ffn_ref[:, 0:1152]
    wu[...] = ffn_ref[:, 1152:2304]
    wd[...] = ffn_ref[:, 2304:3456].T


def shape(rows, columns, kind):
    return jax.ShapeDtypeStruct((rows, columns), kind)


def sems(count):
    return [pltpu.SemaphoreType.DMA((count,))] * 2


def body(
    block_input,
    positions,
    attn_gain,
    w_query,
    w_key,
    w_value,
    w_output,
    q_gain,
    k_gain,
    ffn_gain,
    w_gate,
    w_up,
    w_down,
    cotangent,
):
    square = shape(1024, 1024, bf16)
    position_row = positions[None, :]
    (
        attn_full, normed_rows, pre, mixed, lse, q_low, kt_low, k_low, v_low,
        ffn_grad, middle_grad, layer_output, ffn_gain_part,
    ) = call(
        front_kernel,
        [
            shape(1024, 768, bf16),
            square,
            shape(384, 1024, f32),
            shape(256, 1024, f32),
            shape(8, 1024, f32),
            shape(256, 1024, bf16),
            jax.ShapeDtypeStruct((2, 4, 64, 256), bf16),
            jax.ShapeDtypeStruct((2, 1024, 64), bf16),
            jax.ShapeDtypeStruct((2, 1024, 64), bf16),
            shape(1024, 3456, bf16),
            shape(256, 1024, f32),
            shape(256, 1024, bf16),
            shape(1, 1024, f32),
        ],
        [
            pltpu.VMEM((1024, 3456), bf16),
            pltpu.VMEM((1024, 1024), bf16),
            pltpu.VMEM((1024, 1024), bf16),
            pltpu.VMEM((1024, 1024), bf16),
            pltpu.VMEM((1024, 1024), bf16),
            pltpu.VMEM((256, 1024), f32),
            pltpu.VMEM((2, 4, 80, 256), bf16),
            pltpu.VMEM((80, 512), f32),
            pltpu.VMEM((1024, 1024), bf16),
            pltpu.VMEM((1024, 1024), bf16),
            pltpu.VMEM((1024, 1152), bf16),
            pltpu.VMEM((1024, 1152), bf16),
            pltpu.VMEM((1024, 1152), bf16),
        ]
        + table_scratch()
        + scatter_scratch() * 2
        + sems(41) * 2
        + sems(12) * 3,
        0,
        (
            block_input, position_row, attn_gain[None, :], w_query, w_key, w_value, w_output,
            q_gain[None, :], k_gain[None, :], ffn_gain[None, :], w_gate, w_up, w_down, cotangent,
        ),
    )
    input_grad, attn_out, ffn_out, gains = call(
        back_kernel,
        [
            shape(256, 1024, f32),
            shape(32, 768, f32),
            shape(32, 3456, f32),
            shape(24, 128, f32),
        ],
        [
            pltpu.VMEM((1024, 1024), bf16),
            pltpu.VMEM((1024, 1024), bf16),
            pltpu.VMEM((1024, 768), bf16),
            pltpu.VMEM((80, 512), f32),
            pltpu.VMEM((256, 1024), bf16),
            pltpu.VMEM((4, 1024, 64), bf16),
            pltpu.VMEM((8, 1024), f32),
            pltpu.VMEM((4, 1024, 64), bf16),
            pltpu.VMEM((2, 1024, 64), f32),
            pltpu.VMEM((2, 1024, 64), f32),
            pltpu.VMEM((256, 1024), f32),
            pltpu.VMEM((512, 1024), bf16),
            pltpu.VMEM((1024, 512), bf16),
            pltpu.VMEM((24, 128), f32),
        ]
        + table_scratch()
        + scatter_scratch()
        + sems(12)
        + grad_scratch(3456)
        + grad_scratch(768)
        + gain_scratch(),
        1,
        (
            ffn_grad, middle_grad, ffn_gain_part, block_input, position_row, attn_gain[None, :],
            q_gain[None, :], k_gain[None, :],
            attn_full, normed_rows, pre, mixed, lse, q_low, kt_low, k_low, v_low,
        ),
    )
    outs = pl.pallas_call(
        unpack_kernel,
        out_shape=[
            shape(256, 1024, bf16),
            shape(256, 1024, f32),
            shape(1, 1024, f32),
            shape(32, 256, f32),
            shape(32, 128, f32),
            shape(32, 128, f32),
            shape(256, 32, f32),
            shape(1, 64, f32),
            shape(1, 64, f32),
            shape(1, 1024, f32),
            shape(32, 1152, f32),
            shape(32, 1152, f32),
            shape(1152, 32, f32),
        ],
        in_specs=[VMEM_SPEC] * 5,
        out_specs=[VMEM_SPEC] * 13,
        compiler_params=pltpu.CompilerParams(vmem_limit_bytes=VMEM_LIMIT),
    )(layer_output, input_grad, attn_out, ffn_out, gains)
    return tuple(out[0] if out.shape[0] == 1 else out for out in outs)


def solution(mesh):
    placed = (
        P(("dp", "tensor"), None),
        P("dp"),
        P(),
        P("dp", "tensor"),
        P("dp", "tensor"),
        P("dp", "tensor"),
        P("tensor", "dp"),
        P(),
        P(),
        P(),
        P("dp", "tensor"),
        P("dp", "tensor"),
        P("tensor", "dp"),
        P(("dp", "tensor"), None),
    )
    return jax.shard_map(
        body,
        mesh=mesh,
        in_specs=placed,
        out_specs=(
            P(("dp", "tensor"), None),
            P(("dp", "tensor"), None),
            P(),
            P("dp", "tensor"),
            P("dp", "tensor"),
            P("dp", "tensor"),
            P("tensor", "dp"),
            P(),
            P(),
            P(),
            P("dp", "tensor"),
            P("dp", "tensor"),
            P("tensor", "dp"),
        ),
        check_vma=False,
    )
```

```python
import functools
import math

import jax
import jax.numpy as jnp
from jax import lax
from jax.experimental import pallas as pl
from jax.experimental.pallas import tpu as pltpu
from jax.sharding import PartitionSpec as P

epsilon = 1e-05
rope_base = 1000000.0
f32 = jnp.float32
bf16 = jnp.bfloat16
MESH = pl.DeviceIdType.MESH
VMEM_SPEC = pl.BlockSpec(memory_space=pltpu.VMEM)
VMEM_LIMIT = 62 * 1024 * 1024


class Place:
    def __init__(self):
        d = lax.axis_index("dp")
        t = lax.axis_index("tensor")
        self.z = lax.div(d, 8)
        self.y = lax.rem(lax.div(d, 2), 4)
        self.h = lax.rem(d, 2)
        self.xl = lax.div(t, 2)
        self.core = lax.rem(t, 2)
        self.d = d
        self.t = t

    def at(self, dz=0, dy=0, dh=0):
        z = lax.rem(self.z + (dz + 4), 4)
        y = lax.rem(self.y + (dy + 4), 4)
        h = self.h if dh == 0 else 1 - self.h
        return z * 8 + y * 2 + h

    def dp_device(self, dz=0, dy=0, dh=0):
        return (self.at(dz, dy, dh), self.t)

    def core_device(self):
        return (self.d, self.xl * 2 + (1 - self.core))

    def x_device(self):
        return (self.d, (1 - self.xl) * 2 + self.core)

    def token_block(self, dx=0, dc=0):
        xl = self.xl if dx == 0 else 1 - self.xl
        core = self.core if dc == 0 else 1 - self.core
        return xl * 2 + core


def greet(devices):
    barrier = pltpu.get_barrier_semaphore()
    for device in devices:
        pl.semaphore_signal(barrier, inc=1, device_id=device, device_id_type=MESH)
    pl.semaphore_wait(barrier, len(devices))


def ring_devices(me):
    return [
        me.dp_device(dz=1),
        me.dp_device(dz=-1),
        me.dp_device(dy=1),
        me.dp_device(dy=-1),
        me.dp_device(dh=1),
    ]


def remote(src, dst, send, recv, index, device):
    return pltpu.make_async_remote_copy(
        src_ref=src,
        dst_ref=dst,
        send_sem=send.at[index],
        recv_sem=recv.at[index],
        device_id=device,
        device_id_type=MESH,
    )


def offsets(kind, first, second):
    return (first, second) if kind == 0 else (second, first)


class WeightGather:
    COUNT = 41

    def __init__(self, me, full, send, recv):
        self.me, self.full, self.send, self.recv = me, full, send, recv
        self.started = []

    def block(self, kind, first, second, part=None):
        dz, dy = offsets(kind, first, second)
        row = self.me.at(dz, dy, kind) * 32
        if part is None:
            return self.full.at[pl.ds(pl.multiple_of(row, 32), 32)]
        return self.full.at[pl.ds(pl.multiple_of(row + part * 16, 16), 16)]

    def push(self, ref, index, device):
        copy = remote(ref, ref, self.send, self.recv, index, device)
        copy.start()
        self.started.append(copy)

    def arrived(self, ref, index):
        remote(ref, ref, self.send, self.recv, index, self.me.dp_device(dh=1)).wait_recv()

    def along(self, kind, level, step):
        dz, dy = offsets(kind, step, 0) if level == 0 else offsets(kind, 0, step)
        return self.me.dp_device(dz=dz, dy=dy)

    def base(self, kind, level, chunk):
        return 1 + kind * 4 + chunk * 0 if level == 0 else 9 + kind * 16 + chunk * 4

    def spread(self, kind, level, chunk):
        first = (0, -1, 1, 2)[chunk] if level == 1 else 0
        base = self.base(kind, level, chunk)
        ref = self.block(kind, first, 0)
        self.push(ref, base, self.along(kind, level, 1))
        self.push(ref, base + 1, self.along(kind, level, -1))

    def pass_on(self, kind, level, chunk, side):
        first = (0, -1, 1, 2)[chunk] if level == 1 else 0
        base = self.base(kind, level, chunk)
        step = -1 if side == 0 else 1
        where = (step, 0) if level == 0 else (first, step)
        self.arrived(self.block(kind, *where), base + side)
        self.push(self.block(kind, *where, part=side), base + 2 + side, self.along(kind, level, -step))

    def last(self, kind, level, chunk):
        first = (0, -1, 1, 2)[chunk] if level == 1 else 0
        base = self.base(kind, level, chunk)
        where = (2, 0) if level == 0 else (first, 2)
        for side in range(2):
            self.arrived(self.block(kind, *where, part=side), base + 2 + side)

    def begin(self):
        self.push(self.block(0, 0, 0), 0, self.me.dp_device(dh=1))
        self.spread(0, 0, 0)
        self.spread(0, 1, 0)

    def step1(self):
        self.arrived(self.block(1, 0, 0), 0)
        self.spread(1, 0, 0)
        self.spread(1, 1, 0)

    def step2(self):
        for kind in range(2):
            for side in range(2):
                self.pass_on(kind, 0, 0, side)
                self.spread(kind, 1, 1 + side)

    def step3(self):
        for kind in range(2):
            self.last(kind, 0, 0)
            self.spread(kind, 1, 3)

    def step4(self):
        for chunk in range(4):
            for kind in range(2):
                for side in range(2):
                    self.pass_on(kind, 1, chunk, side)

    def finish(self):
        for chunk in range(4):
            for kind in range(2):
                self.last(kind, 1, chunk)
        for copy in self.started:
            copy.wait_send()


class TokenGather:
    COUNT = 12
    CHUNKS = 4
    ROWS = 64

    def __init__(self, me, rows, send, recv):
        self.me, self.rows, self.send, self.recv = me, rows, send, recv
        self.started = []

    def piece(self, dx, dc, chunk):
        row = self.me.token_block(dx, dc) * 256 + chunk * self.ROWS
        return self.rows.at[pl.ds(pl.multiple_of(row, self.ROWS), self.ROWS)]

    def push(self, ref, index, device):
        copy = remote(ref, ref, self.send, self.recv, index, device)
        copy.start()
        self.started.append(copy)

    def arrived(self, ref, index):
        remote(ref, ref, self.send, self.recv, index, self.me.core_device()).wait_recv()

    def begin(self, chunk):
        own = self.piece(0, 0, chunk)
        self.push(own, chunk, self.me.x_device())
        self.push(own, 4 + chunk, self.me.core_device())

    def pass_on(self, chunk):
        other = self.piece(1, 0, chunk)
        self.arrived(other, chunk)
        self.push(other, 8 + chunk, self.me.core_device())

    def finish(self):
        for chunk in range(self.CHUNKS):
            self.arrived(self.piece(0, 1, chunk), 4 + chunk)
        for chunk in range(self.CHUNKS):
            self.arrived(self.piece(1, 1, chunk), 8 + chunk)
        for copy in self.started:
            copy.wait_send()


class TokenScatter:
    COUNT = 12
    CHUNKS = 4
    ROWS = 64

    def __init__(self, me, part, near, far, relay, send, recv):
        self.me, self.part, self.near, self.far, self.relay = me, part, near, far, relay
        self.send, self.recv = send, recv
        self.started = []

    def piece(self, dx, dc, chunk):
        row = self.me.token_block(dx, dc) * 256 + chunk * self.ROWS
        return pl.ds(pl.multiple_of(row, self.ROWS), self.ROWS)

    def push(self, src, dst, index, device):
        copy = remote(src, dst, self.send, self.recv, index, device)
        copy.start()
        self.started.append(copy)

    def arrived(self, ref, index):
        remote(ref, ref, self.send, self.recv, index, self.me.core_device()).wait_recv()

    def begin_far(self, chunk):
        self.push(
            self.part.at[self.piece(1, 1, chunk)], self.relay.at[chunk], chunk, self.me.core_device()
        )

    def begin_near(self, chunk):
        self.push(
            self.part.at[self.piece(0, 1, chunk)], self.near.at[chunk], 4 + chunk, self.me.core_device()
        )

    def relay_on(self, chunk):
        self.arrived(self.relay.at[chunk], chunk)
        total = self.relay[chunk].astype(f32) + self.part[self.piece(1, 0, chunk), :].astype(f32)
        self.relay[chunk] = total.astype(bf16)
        self.push(self.relay.at[chunk], self.far.at[chunk], 8 + chunk, self.me.x_device())

    def total(self, chunk):
        self.arrived(self.near.at[chunk], 4 + chunk)
        self.arrived(self.far.at[chunk], 8 + chunk)
        return (
            self.part[self.piece(0, 0, chunk), :].astype(f32)
            + self.near[chunk].astype(f32)
            + self.far[chunk].astype(f32)
        )

    def finish(self):
        for copy in self.started:
            copy.wait_send()


def scatter_scratch():
    return [pltpu.VMEM((4, 64, 1024), bf16)] * 3 + [pltpu.SemaphoreType.DMA((12,))] * 2


class GradScatter:
    COUNT = 61

    def __init__(self, me, part, recv_half, recv_full, sums, last, send, recv):
        self.me, self.part = me, part
        self.recv_half, self.recv_full = recv_half, recv_full
        self.sums, self.last = sums, last
        self.send, self.recv = send, recv
        self.started = []

    def rows(self, kind, first, second, part=None):
        dz, dy = offsets(kind, first, second)
        row = self.me.at(dz, dy, kind) * 32
        if part is None:
            return pl.ds(pl.multiple_of(row, 32), 32)
        return pl.ds(pl.multiple_of(row + part * 16, 16), 16)

    def push(self, src, dst, index, device):
        copy = remote(src, dst, self.send, self.recv, index, device)
        copy.start()
        self.started.append(copy)

    def arrived(self, ref, index):
        remote(ref, ref, self.send, self.recv, index, self.me.dp_device(dh=1)).wait_recv()

    def along(self, kind, level, step):
        dz, dy = offsets(kind, step, 0) if level == 0 else offsets(kind, 0, step)
        return self.me.dp_device(dz=dz, dy=dy)

    def slot(self, kind, level, chunk):
        return kind * 5 + (4 if level == 0 else chunk)

    def source(self, kind, level, chunk, offset):
        if level == 1:
            first = (0, -1, 1, 2)[chunk]
            return self.part, self.rows(kind, first, offset), [
                self.rows(kind, first, offset, part) for part in range(2)
            ]
        chunk = {0: 0, -1: 1, 1: 2, 2: 3}[offset]
        base = (kind * 4 + chunk) * 32
        return self.sums, pl.ds(base, 32), [pl.ds(base, 16), pl.ds(base + 16, 16)]

    def far(self, kind, level, chunk):
        slot = self.slot(kind, level, chunk)
        ref, _, halves = self.source(kind, level, chunk, 2)
        self.push(ref.at[halves[0]], self.recv_half.at[slot, 0], slot * 6, self.along(kind, level, 1))
        self.push(
            ref.at[halves[1]], self.recv_half.at[slot, 1], slot * 6 + 1, self.along(kind, level, -1)
        )

    def near(self, kind, level, chunk):
        slot = self.slot(kind, level, chunk)
        for side in range(2):
            step = 1 if side == 0 else -1
            ref, _, halves = self.source(kind, level, chunk, step)
            self.push(
                ref.at[halves[1 - side]],
                self.recv_full.at[slot, side, pl.ds(16 * (1 - side), 16)],
                slot * 6 + 4 + side,
                self.along(kind, level, step),
            )

    def middle(self, kind, level, chunk, side):
        slot = self.slot(kind, level, chunk)
        step = 1 if side == 0 else -1
        ref, _, halves = self.source(kind, level, chunk, step)
        self.arrived(self.recv_half.at[slot, side], slot * 6 + side)
        total = ref[halves[side], :].astype(f32) + self.recv_half[slot, side].astype(f32)
        ref[halves[side], :] = total.astype(bf16)
        self.push(
            ref.at[halves[side]],
            self.recv_full.at[slot, side, pl.ds(16 * side, 16)],
            slot * 6 + 2 + side,
            self.along(kind, level, step),
        )

    def total(self, kind, level, chunk):
        slot = self.slot(kind, level, chunk)
        ref, whole, _ = self.source(kind, level, chunk, 0)
        for side in range(2):
            full = self.recv_full.at[slot, side]
            self.arrived(full.at[pl.ds(16 * side, 16)], slot * 6 + 2 + side)
            self.arrived(full.at[pl.ds(16 * (1 - side), 16)], slot * 6 + 4 + side)
        return (
            ref[whole, :].astype(f32)
            + self.recv_full[slot, 0].astype(f32)
            + self.recv_full[slot, 1].astype(f32)
        )

    def begin(self):
        for push in (self.far, self.near):
            for chunk in range(4):
                for kind in range(2):
                    push(kind, 1, chunk)

    def step1(self, chunk):
        for kind in range(2):
            for side in range(2):
                self.middle(kind, 1, chunk, side)

    def step2(self, chunk):
        for kind in range(2):
            total = self.total(kind, 1, chunk)
            self.sums[pl.ds((kind * 4 + chunk) * 32, 32), :] = total.astype(bf16)

    def step3(self):
        for push in (self.far, self.near):
            for kind in range(2):
                push(kind, 0, 0)

    def step4(self):
        for kind in (1, 0):
            for side in range(2):
                self.middle(kind, 0, 0, side)

    def step5(self):
        self.last[0] = self.total(1, 0, 0).astype(bf16)
        self.push(self.last.at[0], self.last.at[1], 60, self.me.dp_device(dh=1))

    def result(self):
        own = self.total(0, 0, 0)
        self.arrived(self.last.at[1], 60)
        return own + self.last[1].astype(f32)

    def finish(self):
        for copy in self.started:
            copy.wait_send()


def grad_scratch(width):
    return [
        pltpu.VMEM((10, 2, 16, width), bf16),
        pltpu.VMEM((10, 2, 32, width), bf16),
        pltpu.VMEM((256, width), bf16),
        pltpu.VMEM((2, 32, width), bf16),
        pltpu.SemaphoreType.DMA((61,)),
        pltpu.SemaphoreType.DMA((61,)),
    ]


def row_scale(values):
    return lax.rsqrt(jnp.mean(values * values, axis=-1, keepdims=True) + epsilon)


def norm_back(values, inverse, gain_vec, upstream):
    weighted = upstream * gain_vec
    row_inner = jnp.mean(weighted * values, axis=-1, keepdims=True)
    return inverse * weighted - values * inverse * inverse * inverse * row_inner


def call(kernel, outs, scratch, number, args, flops=0, moved=0):
    return pl.pallas_call(
        kernel,
        out_shape=outs,
        in_specs=[VMEM_SPEC] * len(args),
        out_specs=[VMEM_SPEC] * len(outs),
        scratch_shapes=scratch,
        cost_estimate=pl.CostEstimate(flops=flops, bytes_accessed=moved, transcendentals=0),
        compiler_params=pltpu.CompilerParams(
            collective_id=number, has_side_effects=True, vmem_limit_bytes=VMEM_LIMIT
        ),
    )(*args)


def dot(a, b):
    return jnp.dot(a, b, preferred_element_type=f32)


def dot_tb(a, b):
    return lax.dot_general(a, b, (((1,), (1,)), ((), ())), preferred_element_type=f32)


def head_scale(values):
    return lax.rsqrt(jnp.mean(values * values, axis=0, keepdims=True) + epsilon)


def rotate(values, cosine, sine):
    front, back = values[:32], values[32:]
    return jnp.concatenate([front * cosine - back * sine, back * cosine + front * sine], axis=0)


def rotate_back(values, cosine, sine):
    front, back = values[:32], values[32:]
    return jnp.concatenate([front * cosine + back * sine, back * cosine - front * sine], axis=0)


def project_block(block, rows_ref, weight_ref, pre_ref, low):
    here = pl.ds(pl.multiple_of(block * 256, 256), 256)
    flat = dot(rows_ref[here, :], weight_ref[:, 0:512])
    turned = flat.T
    pre_ref[:, here] = turned[:384]
    cosine, sine = low.cos[:, here], low.sin[:, here]
    for head in range(4):
        u = turned[64 * head : 64 * head + 64]
        u = u * head_scale(u) * low.q_gain[...]
        low.q[pl.ds(64 * head, 64), here] = (rotate(u, cosine, sine) * 0.125).astype(bf16)
    for head in range(2):
        u = turned[256 + 64 * head : 320 + 64 * head]
        u = rotate(u * head_scale(u) * low.k_gain[...], cosine, sine)
        low.kt[head, block] = u.astype(bf16)
        low.k[head, here, :] = u.T.astype(bf16)
        u = turned[384 + 64 * head : 448 + 64 * head]
        low.vt[head, block, 0:64, :] = u.astype(bf16)
        low.vt[head, block, 64:80, :] = jnp.ones((16, 256), bf16)
        low.v[head, here, :] = u.T.astype(bf16)


def pair_lanes(ref, head, here):
    return jnp.concatenate(
        [ref[pl.ds(128 * head, 64), here], ref[pl.ds(128 * head + 64, 64), here]], axis=1
    )


def seen(low, number, key_block, diagonal):
    here = pl.ds(number * 256, 256)
    key_row = lax.broadcasted_iota(jnp.int32, (256, 256), 0) + key_block * 256
    mask = key_row >= low.start[:, here]
    if diagonal:
        query_row = lax.broadcasted_iota(jnp.int32, (256, 256), 1) + number * 256
        mask = jnp.logical_and(mask, key_row <= query_row)
    return jnp.concatenate([mask, mask], axis=1)


def forward_block(low, head, number, acc):
    here = pl.ds(number * 256, 256)
    queries = pair_lanes(low.q, head, here)

    def step(key_block, diagonal):
        keys = low.k[head, pl.ds(pl.multiple_of(key_block * 256, 256), 256), :]
        weight = jnp.exp(dot(keys, queries))
        weight = jnp.where(seen(low, number, key_block, diagonal), weight, 0.0).astype(bf16)
        return dot(low.vt[head, key_block], weight)

    acc[...] = step(number, True)
    if number > 0:

        @pl.loop(0, number)
        def _(key_block):
            acc[...] += step(key_block, False)

    total = acc[64:65, :]
    mixed = acc[0:64, :] / total
    low.lse[2 * head : 2 * head + 1, here] = jnp.log(total[:, 0:256])
    low.lse[2 * head + 1 : 2 * head + 2, here] = jnp.log(total[:, 256:512])
    low.mixed[pl.ds(128 * head, 64), here] = mixed[:, 0:256]
    low.mixed[pl.ds(128 * head + 64, 64), here] = mixed[:, 256:512]


def backward_prepare(block, rows_ref, weight_ref, low):
    here = pl.ds(pl.multiple_of(block * 256, 256), 256)
    turned = dot(rows_ref[here, :], weight_ref[:, 512:768]).T.astype(bf16)
    low.gt[:, here] = turned
    for head in range(4):
        part = turned[64 * head : 64 * head + 64].astype(f32)
        low.g[head, here, :] = part.T.astype(bf16)
        mixed = low.mixed[pl.ds(64 * head, 64), here]
        low.inner[head : head + 1, here] = jnp.sum(part * mixed, axis=0, keepdims=True)
        low.qn[head, here, :] = low.q[pl.ds(64 * head, 64), here].astype(f32).T.astype(bf16)


def backward_block(low, head, number, acc):
    here = pl.ds(number * 256, 256)
    queries = pair_lanes(low.q, head, here)
    upstream = pair_lanes(low.gt, head, here)
    query_rows = jnp.concatenate([low.qn[2 * head, here, :], low.qn[2 * head + 1, here, :]], axis=0)
    upstream_rows = jnp.concatenate([low.g[2 * head, here, :], low.g[2 * head + 1, here, :]], axis=0)

    def both(ref):
        return jnp.concatenate(
            [ref[2 * head : 2 * head + 1, here], ref[2 * head + 1 : 2 * head + 2, here]], axis=1
        )

    lse = both(low.lse)
    inner = both(low.inner)

    def step(key_block, diagonal):
        rows = pl.ds(pl.multiple_of(key_block * 256, 256), 256)
        weight = jnp.exp(dot(low.k[head, rows, :], queries) - lse)
        weight = jnp.where(seen(low, number, key_block, diagonal), weight, 0.0)
        score = weight * (dot(low.v[head, rows, :], upstream) - inner)
        score = score.astype(bf16)
        value_part = dot(weight.astype(bf16), upstream_rows)
        key_part = dot(score, query_rows)
        if diagonal:
            low.dv[head, rows, :] = value_part
            low.dk[head, rows, :] = key_part
        else:
            low.dv[head, rows, :] += value_part
            low.dk[head, rows, :] += key_part
        return dot(low.kt[head, key_block], score)

    acc[0:64, :] = step(number, True)
    if number > 0:

        @pl.loop(0, number)
        def _(key_block):
            acc[0:64, :] += step(key_block, False)

    low.dq[pl.ds(128 * head, 64), here] = acc[0:64, 0:256]
    low.dq[pl.ds(128 * head + 64, 64), here] = acc[0:64, 256:512]


def head_norm_back(values, gain, upstream):
    inverse = head_scale(values)
    weighted = upstream * gain
    inner = jnp.mean(weighted * values, axis=0, keepdims=True)
    return inverse * weighted - values * inverse * inverse * inverse * inner, inverse


def backward_finish(block, low, pre_ref, turned_ref, flat_ref):
    here = pl.ds(pl.multiple_of(block * 256, 256), 256)
    cosine, sine = low.cos[:, here], low.sin[:, here]
    q_part = jnp.zeros((64, 1), f32)
    k_part = jnp.zeros((64, 1), f32)
    for head in range(4):
        rows = pl.ds(64 * head, 64)
        upstream = rotate_back(low.dq[rows, here] * 0.125, cosine, sine)
        values = pre_ref[rows, here]
        grad, inverse = head_norm_back(values, low.q_gain[...], upstream)
        q_part = q_part + jnp.sum(upstream * values * inverse, axis=1, keepdims=True)
        turned_ref[rows, here] = grad.astype(bf16)
    for head in range(2):
        rows = pl.ds(256 + 64 * head, 64)
        upstream = rotate_back(low.dk[head, here, :].T, cosine, sine)
        values = pre_ref[rows, here]
        grad, inverse = head_norm_back(values, low.k_gain[...], upstream)
        k_part = k_part + jnp.sum(upstream * values * inverse, axis=1, keepdims=True)
        turned_ref[rows, here] = grad.astype(bf16)
        turned_ref[pl.ds(384 + 64 * head, 64), here] = low.dv[head, here, :].T.astype(bf16)
    flat_ref[here, :] = turned_ref[:, here].astype(f32).T.astype(bf16)
    return q_part, k_part


class GainSum:
    def __init__(self, me, row, plane, send, recv):
        self.me, self.row, self.plane = me, row, plane
        self.send, self.recv = send, recv
        self.started = []

    def row_devices(self):
        me = self.me
        return [
            (me.at(dh=step // 4), lax.rem(me.t + step % 4, 4)) for step in range(1, 8)
        ]

    def plane_devices(self):
        return [self.me.dp_device(dz=step // 4, dy=step % 4) for step in range(1, 16)]

    def exchange(self, slots, place, value, devices, base):
        slots[place] = value
        for step, device in enumerate(devices):
            copy = remote(
                slots.at[place], slots.at[place], self.send, self.recv, base + step, device
            )
            copy.start()
            self.started.append(copy)
        for step, device in enumerate(devices):
            remote(
                slots.at[place], slots.at[place], self.send, self.recv, base + step, device
            ).wait_recv()
        total = slots[0]
        for slot in range(1, len(devices) + 1):
            total = total + slots[slot]
        return total

    def run(self, value):
        me = self.me
        value = self.exchange(self.row, me.h * 4 + me.t, value, self.row_devices(), 0)
        value = self.exchange(self.plane, me.z * 4 + me.y, value, self.plane_devices(), 7)
        for copy in self.started:
            copy.wait_send()
        return value


def gain_scratch():
    return [
        pltpu.VMEM((8, 24, 128), f32),
        pltpu.VMEM((16, 24, 128), f32),
        pltpu.SemaphoreType.DMA((22,)),
        pltpu.SemaphoreType.DMA((22,)),
    ]


class Fields:
    def __init__(self, **refs):
        self.__dict__.update(refs)


def gather_services(gather):
    steps = [gather.step1]
    for kind in range(2):
        for side in range(2):

            def hand_on(kind=kind, side=side):
                gather.pass_on(kind, 0, 0, side)
                gather.spread(kind, 1, 1 + side)

            steps.append(hand_on)
    steps.append(gather.step3)
    for chunk in range(4):

        def hand_bulk(chunk=chunk):
            for kind in range(2):
                for side in range(2):
                    gather.pass_on(kind, 1, chunk, side)

        steps.append(hand_bulk)
    return steps


def column(row_ref):
    return jnp.broadcast_to(row_ref[...], (128, 64)).T[:, 0:1]


def tables(position_ref, q_gain_ref, k_gain_ref, cos, sin, start, q_gain, k_gain):
    place = lax.broadcasted_iota(jnp.int32, (32, 1024), 0).astype(f32)
    frequency = jnp.exp(place * (-math.log(rope_base) * 2.0 / 64))
    angles = frequency * position_ref[...].astype(f32)
    cos[...] = jnp.cos(angles)
    sin[...] = jnp.sin(angles)
    start[...] = lax.broadcasted_iota(jnp.int32, (1, 1024), 1) - position_ref[...]
    q_gain[...] = column(q_gain_ref)
    k_gain[...] = column(k_gain_ref)


def table_scratch():
    return [
        pltpu.VMEM((32, 1024), f32),
        pltpu.VMEM((32, 1024), f32),
        pltpu.VMEM((1, 1024), jnp.int32),
        pltpu.VMEM((64, 1), f32),
        pltpu.VMEM((64, 1), f32),
    ]


def turn(values):
    return values.astype(f32).T.astype(bf16)


def ffn_block(here, low):
    rows = low.rows[here, :]
    grads = low.grad_rows[here, :]
    for first, count in ((0, 512), (512, 640)):
        columns = pl.ds(first, count)
        gate = dot(rows, low.full[:, pl.ds(first, count)])
        up = dot(rows, low.full[:, pl.ds(1152 + first, count)])
        hidden = dot(grads, low.full[:, pl.ds(2304 + first, count)])
        sigmoid = jax.nn.sigmoid(gate)
        silu = gate * sigmoid
        low.activation[here, columns] = (silu * up).astype(bf16)
        low.gate_low[here, columns] = (hidden * up * sigmoid * (1.0 + gate * (1.0 - sigmoid))).astype(bf16)
        low.up_low[here, columns] = (hidden * silu).astype(bf16)
    low.ffn_part[here, :] = dot_tb(low.activation[here, :], low.full[:, 2304:3456]).astype(bf16)
    low.part[here, :] = (
        dot_tb(low.gate_low[here, :], low.full[:, 0:1152]) + dot_tb(low.up_low[here, :], low.full[:, 1152:2304])
    ).astype(bf16)


def scatter_services(scatter):
    steps = []
    for chunk in range(4):
        steps.append(functools.partial(scatter.step1, chunk))
    for chunk in range(4):
        steps.append(functools.partial(scatter.step2, chunk))
    steps.append(scatter.step3)
    steps.append(scatter.step4)
    steps.append(scatter.step5)
    return steps


class Heads:
    def __init__(self, ref, first):
        self.ref, self.first = ref, first

    def lanes(self, head):
        return pl.ds((self.first + head) * 128, 64)

    def __getitem__(self, index):
        return self.ref[index[1], self.lanes(index[0])]

    def __setitem__(self, index, value):
        self.ref[index[1], self.lanes(index[0])] = value


def block_kernel(
    x_ref, position_ref, gain_ref, wq_ref, wk_ref, wv_ref, wo_ref, q_gain_ref, k_gain_ref, ffn_gain_ref,
    wg_ref, wu_ref, wd_ref, cot_ref,
    out_ref, input_grad_ref, attn_shard_ref, ffn_shard_ref, gains_ref,
    attn_full, ffn_full, normed_ref, grad_rows, grad_rows_t, rows_ref, back_rows, middle, part, ffn_part,
    activation, gate_low, up_low,
    pre_ref, mixed_ref, lse_ref, q_ref, kt_ref, k_ref, vt, v_ref, acc, inner, dk, dv, dq, gain_rows,
    *scratch,
):
    me = Place()
    scratch = list(scratch)

    def take(count):
        taken = scratch[:count]
        del scratch[:count]
        return taken

    cos, sin, start, q_gain, k_gain = take(5)
    buffers = take(5)
    scatter = TokenScatter(me, part, *buffers)
    first = TokenScatter(me, part, *buffers)
    third = TokenScatter(me, part, *buffers)
    last = TokenScatter(me, ffn_part, *take(5))
    attn = WeightGather(me, attn_full, *take(2))
    ffn = WeightGather(me, ffn_full, *take(2))
    tokens = TokenGather(me, normed_ref, *take(2))
    upstream = TokenGather(me, grad_rows, *take(2))
    second = TokenGather(me, rows_ref, *take(2))
    back = TokenGather(me, back_rows, *take(2))
    attn_grad = grad_rows_t.at[:, pl.ds(0, 768)]
    ffn_grad = GradScatter(me, ffn_full, *take(6))
    weight_grad = GradScatter(me, attn_grad, *take(6))
    gains = GainSum(me, *take(4))
    middle_grad = input_grad_ref
    turned = gate_low.at[pl.ds(0, 512), pl.ds(0, 1024)]
    flat = up_low.at[:, pl.ds(0, 512)]
    gt = gate_low.at[pl.ds(512, 256), pl.ds(0, 1024)]
    low = Fields(
        cos=cos, sin=sin, q_gain=q_gain, k_gain=k_gain, start=start,
        q=q_ref, kt=kt_ref, k=k_ref, vt=vt, v=v_ref, lse=lse_ref, mixed=mixed_ref,
        rows=rows_ref, full=ffn_full, grad_rows=grad_rows, part=part, ffn_part=ffn_part,
        activation=activation, gate_low=gate_low, up_low=up_low,
        gt=gt, g=Heads(activation, 0), inner=inner, qn=Heads(activation, 4), dk=dk, dv=dv, dq=dq,
    )
    own_rows = pl.ds(pl.multiple_of(me.d * 32, 32), 32)
    own_tokens = pl.ds(pl.multiple_of(me.t * 256, 256), 256)
    attn_full[own_rows, 0:256] = wq_ref[...]
    attn_full[own_rows, 256:384] = wk_ref[...]
    attn_full[own_rows, 384:512] = wv_ref[...]
    attn_full[own_rows, 512:768] = wo_ref[...]
    values = x_ref[...].astype(f32)
    normed_ref[own_tokens, :] = (values * row_scale(values) * gain_ref[...]).astype(bf16)
    greet(gains.row_devices() + gains.plane_devices())
    attn.begin()
    for chunk in range(4):
        tokens.begin(chunk)
    ffn_full[own_rows, 0:1152] = wg_ref[...]
    ffn_full[own_rows, 1152:2304] = wu_ref[...]
    ffn_full[own_rows, 2304:3456] = wd_ref[...]
    grad_rows[own_tokens, :] = cot_ref[...]
    attn.step1()
    lse_ref[...] = jnp.zeros((8, 1024), f32)
    tables(position_ref, q_gain_ref, k_gain_ref, cos, sin, start, q_gain, k_gain)
    attn.step2()
    attn.step3()
    attn.step4()
    ffn.begin()
    for chunk in range(4):
        tokens.pass_on(chunk)
    tokens.finish()
    attn.finish()
    services = gather_services(ffn)

    def serve(count=1):
        for _ in range(count):
            if services:
                services.pop(0)()

    serve()
    for chunk in range(4):
        upstream.begin(chunk)

    @pl.loop(0, 4)
    def _(block):
        project_block(block, normed_ref, attn_full, pre_ref, low)

    for number in range(4):
        for head in range(2):
            forward_block(low, head, number, acc)
            if number == 1 or number == 3:
                serve()
    for chunk in range(4):
        upstream.pass_on(chunk)

    def output_part(dx, dc):
        here = pl.ds(pl.multiple_of(me.token_block(dx, dc) * 256, 256), 256)
        flat = mixed_ref[:, here].T.astype(bf16)
        part[here, :] = dot_tb(flat, attn_full[:, 512:768]).astype(bf16)

    output_part(1, 1)
    for chunk in range(4):
        scatter.begin_far(chunk)
    output_part(1, 0)
    output_part(0, 1)
    for chunk in range(4):
        scatter.begin_near(chunk)
    output_part(0, 0)
    for chunk in range(4):
        scatter.relay_on(chunk)
    serve(2)
    upstream.finish()

    @pl.loop(0, 4)
    def _(block):
        here = pl.ds(pl.multiple_of(block * 256, 256), 256)
        grad_rows_t[:, here] = turn(grad_rows[here, :])

    for chunk in range(4):
        here = pl.ds(chunk * 64, 64)
        values = x_ref[here, :].astype(f32) + scatter.total(chunk)
        middle[here, :] = values
        own = pl.ds(pl.multiple_of(me.t * 256 + chunk * 64, 64), 64)
        rows_ref[own, :] = (values * row_scale(values) * ffn_gain_ref[...]).astype(bf16)
        if chunk == 3:
            scatter.finish()
        second.begin(chunk)
    serve(20)
    ffn.finish()

    passes = [
        remote(piece, piece, second.send, second.recv, 8 + chunk, me.core_device())
        for chunk, piece in enumerate(second.piece(1, 0, chunk) for chunk in range(4))
    ]

    @pl.loop(0, 4)
    def _(turn_number):
        @pl.when(turn_number == 1)
        def _():
            for chunk in range(4):
                second.arrived(second.piece(0, 1, chunk), 4 + chunk)

        @pl.when(turn_number == 2)
        def _():
            for chunk in range(4):
                second.arrived(second.piece(1, 0, chunk), chunk)
                passes[chunk].start()

        @pl.when(turn_number == 3)
        def _():
            for chunk in range(4):
                second.arrived(second.piece(1, 1, chunk), 8 + chunk)

        block = lax.rem(me.xl + lax.div(turn_number, 2), 2) * 2 + lax.rem(me.core + lax.rem(turn_number, 2), 2)
        ffn_block(pl.ds(pl.multiple_of(block * 256, 256), 256), low)

    for copy in second.started + passes:
        copy.wait_send()

    for chunk in range(4):
        first.begin_far(chunk)
    for chunk in range(4):
        first.begin_near(chunk)

    def weight_tile(tile):
        here = pl.ds(pl.multiple_of(tile * 256, 256), 256)
        rows_t = turn(rows_ref[:, here])
        ffn_full[here, 0:1152] = dot(rows_t, gate_low[...]).astype(bf16)
        ffn_full[here, 1152:2304] = dot(rows_t, up_low[...]).astype(bf16)
        ffn_full[here, 2304:3456] = dot(grad_rows_t[here, :], activation[...]).astype(bf16)

    pl.loop(0, 1)(weight_tile)
    for chunk in range(4):
        first.relay_on(chunk)
    pl.loop(1, 4)(weight_tile)
    ffn_grad.begin()
    ffn_gain_total = jnp.zeros((1, 1024), f32)
    for chunk in range(4):
        here = pl.ds(chunk * 64, 64)
        grad = first.total(chunk)
        values = middle[here, :]
        inverse = row_scale(values)
        ffn_gain_total = ffn_gain_total + jnp.sum(grad * values * inverse, axis=0, keepdims=True)
        total = cot_ref[here, :].astype(f32) + norm_back(values, inverse, ffn_gain_ref[...], grad)
        middle_grad[here, :] = total
        own = pl.ds(pl.multiple_of(me.t * 256 + chunk * 64, 64), 64)
        back_rows[own, :] = total.astype(bf16)
        if chunk == 3:
            first.finish()
        back.begin(chunk)
    for chunk in range(4):
        last.begin_far(chunk)
    for chunk in range(4):
        last.begin_near(chunk)
    services.extend(scatter_services(ffn_grad))
    serve(3)
    for chunk in range(4):
        back.pass_on(chunk)
    for chunk in range(4):
        last.relay_on(chunk)
    serve(1)
    back.finish()

    @pl.loop(0, 4)
    def _(block):
        backward_prepare(block, back_rows, attn_full, low)


    @pl.loop(0, 4)
    def _(tile):
        here = pl.ds(pl.multiple_of(tile * 256, 256), 256)
        attn_grad[here, 512:768] = dot(mixed_ref[...].astype(bf16), back_rows[:, here]).T.astype(bf16)

    for number in range(4):
        for head in range(2):
            backward_block(low, head, number, acc)
            if number == 3:
                serve()
    for chunk in range(4):
        here = pl.ds(chunk * 64, 64)
        out_ref[here, :] = (middle[here, :] + last.total(chunk)).astype(bf16)
    q_part = jnp.zeros((64, 1), f32)
    k_part = jnp.zeros((64, 1), f32)
    for block in range(4):
        q_more, k_more = backward_finish(block, low, pre_ref, turned, flat)
        q_part = q_part + q_more
        k_part = k_part + k_more

    serve(2)

    def first_part(dx, dc):
        here = pl.ds(pl.multiple_of(me.token_block(dx, dc) * 256, 256), 256)
        part[here, :] = dot_tb(flat[here, :], attn_full[:, 0:512]).astype(bf16)

    first_part(1, 1)
    for chunk in range(4):
        third.begin_far(chunk)
    first_part(1, 0)
    for chunk in range(4):
        third.relay_on(chunk)

    @pl.loop(0, 4)
    def _(tile):
        here = pl.ds(pl.multiple_of(tile * 256, 256), 256)
        attn_grad[here, 0:512] = dot(turned[...], normed_ref[:, here]).T.astype(bf16)

    weight_grad.begin()
    first_part(0, 1)
    for chunk in range(4):
        third.begin_near(chunk)
    first_part(0, 0)
    gain_rows[16:24, :] = jnp.zeros((8, 128), f32)
    gain_rows[16:17, 0:64] = jnp.broadcast_to(q_part, (64, 128)).T[0:1, :]
    gain_rows[17:18, 0:64] = jnp.broadcast_to(k_part, (64, 128)).T[0:1, :]
    serve(20)
    for chunk in range(4):
        weight_grad.step1(chunk)
    gain_total = jnp.zeros((1, 1024), f32)
    for chunk in range(4):
        here = pl.ds(chunk * 64, 64)
        upstream = third.total(chunk)
        values = x_ref[here, :].astype(f32)
        inverse = row_scale(values)
        gain_total = gain_total + jnp.sum(upstream * values * inverse, axis=0, keepdims=True)
        input_grad_ref[here, :] = middle_grad[here, :] + norm_back(
            values, inverse, gain_ref[...], upstream
        )
    for part_number in range(8):
        lanes = slice(128 * part_number, 128 * part_number + 128)
        gain_rows[part_number : part_number + 1, :] = gain_total[:, lanes]
        gain_rows[8 + part_number : 9 + part_number, :] = ffn_gain_total[:, lanes]
    for chunk in range(4):
        weight_grad.step2(chunk)
    weight_grad.step3()
    gains_ref[...] = gains.run(gain_rows[...])
    weight_grad.step4()
    weight_grad.step5()
    ffn_shard_ref[...] = ffn_grad.result()
    attn_shard_ref[...] = weight_grad.result()
    for transfer in (third, last, ffn_grad, weight_grad):
        transfer.finish()


def unpack_kernel(
    out_ref, input_grad_ref, attn_ref, ffn_ref, gains_ref,
    out, input_grad, attn_gain, wq, wk, wv, wo, q_gain, k_gain, ffn_gain, wg, wu, wd,
):
    out[...] = out_ref[...]
    input_grad[...] = input_grad_ref[...]
    for part in range(8):
        lanes = slice(128 * part, 128 * part + 128)
        attn_gain[:, lanes] = gains_ref[part : part + 1, :]
        ffn_gain[:, lanes] = gains_ref[8 + part : 9 + part, :]
    q_gain[...] = gains_ref[16:17, 0:64]
    k_gain[...] = gains_ref[17:18, 0:64]
    wq[...] = attn_ref[:, 0:256]
    wk[...] = attn_ref[:, 256:384]
    wv[...] = attn_ref[:, 384:512]
    wo[...] = attn_ref[:, 512:768]
    wg[...] = ffn_ref[:, 0:1152]
    wu[...] = ffn_ref[:, 1152:2304]
    wd[...] = ffn_ref[:, 2304:3456]


def shape(rows, columns, kind):
    return jax.ShapeDtypeStruct((rows, columns), kind)


def sems(count):
    return [pltpu.SemaphoreType.DMA((count,))] * 2


def body(
    block_input,
    positions,
    attn_gain,
    w_query,
    w_key,
    w_value,
    w_output,
    q_gain,
    k_gain,
    ffn_gain,
    w_gate,
    w_up,
    w_down,
    cotangent,
):
    square = pltpu.VMEM((1024, 1024), bf16)
    hidden = pltpu.VMEM((1024, 1152), bf16)
    layer_output, input_grad, attn_out, ffn_out, gains = call(
        block_kernel,
        [
            shape(256, 1024, bf16),
            shape(256, 1024, f32),
            shape(32, 768, f32),
            shape(32, 3456, f32),
            shape(24, 128, f32),
        ],
        [
            pltpu.VMEM((1024, 768), bf16),
            pltpu.VMEM((1024, 3456), bf16),
            square,
            square,
            square,
            square,
            square,
            pltpu.VMEM((256, 1024), f32),
            square,
            square,
            hidden,
            hidden,
            hidden,
            pltpu.VMEM((384, 1024), f32),
            pltpu.VMEM((256, 1024), f32),
            pltpu.VMEM((8, 1024), f32),
            pltpu.VMEM((256, 1024), bf16),
            pltpu.VMEM((2, 4, 64, 256), bf16),
            pltpu.VMEM((2, 1024, 64), bf16),
            pltpu.VMEM((2, 4, 80, 256), bf16),
            pltpu.VMEM((2, 1024, 64), bf16),
            pltpu.VMEM((80, 512), f32),
            pltpu.VMEM((8, 1024), f32),
            pltpu.VMEM((2, 1024, 64), f32),
            pltpu.VMEM((2, 1024, 64), f32),
            pltpu.VMEM((256, 1024), f32),
            pltpu.VMEM((24, 128), f32),
        ]
        + table_scratch()
        + scatter_scratch() * 2
        + sems(41) * 2
        + sems(12) * 4
        + grad_scratch(3456)
        + grad_scratch(768)
        + gain_scratch(),
        0,
        (
            block_input, positions[None, :], attn_gain[None, :], w_query, w_key, w_value, w_output.T,
            q_gain[None, :], k_gain[None, :], ffn_gain[None, :], w_gate, w_up, w_down.T, cotangent,
        ),
    )
    outs = pl.pallas_call(
        unpack_kernel,
        out_shape=[
            shape(256, 1024, bf16),
            shape(256, 1024, f32),
            shape(1, 1024, f32),
            shape(32, 256, f32),
            shape(32, 128, f32),
            shape(32, 128, f32),
            shape(32, 256, f32),
            shape(1, 64, f32),
            shape(1, 64, f32),
            shape(1, 1024, f32),
            shape(32, 1152, f32),
            shape(32, 1152, f32),
            shape(32, 1152, f32),
        ],
        in_specs=[VMEM_SPEC] * 5,
        out_specs=[VMEM_SPEC] * 13,
        compiler_params=pltpu.CompilerParams(vmem_limit_bytes=VMEM_LIMIT),
    )(layer_output, input_grad, attn_out, ffn_out, gains)
    outs = [out[0] if out.shape[0] == 1 else out for out in outs]
    return (*outs[:6], outs[6].T, *outs[7:12], outs[12].T)


def solution(mesh):
    placed = (
        P(("dp", "tensor"), None),
        P("dp"),
        P(),
        P("dp", "tensor"),
        P("dp", "tensor"),
        P("dp", "tensor"),
        P("tensor", "dp"),
        P(),
        P(),
        P(),
        P("dp", "tensor"),
        P("dp", "tensor"),
        P("tensor", "dp"),
        P(("dp", "tensor"), None),
    )
    return jax.shard_map(
        body,
        mesh=mesh,
        in_specs=placed,
        out_specs=(
            P(("dp", "tensor"), None),
            P(("dp", "tensor"), None),
            P(),
            P("dp", "tensor"),
            P("dp", "tensor"),
            P("dp", "tensor"),
            P("tensor", "dp"),
            P(),
            P(),
            P(),
            P("dp", "tensor"),
            P("dp", "tensor"),
            P("tensor", "dp"),
        ),
        check_vma=False,
    )
```

```python
import functools
import math

import jax
import jax.numpy as jnp
from jax import lax
from jax.experimental import pallas as pl
from jax.experimental.pallas import tpu as pltpu
from jax.sharding import PartitionSpec as P

epsilon = 1e-05
rope_base = 1000000.0
f32 = jnp.float32
bf16 = jnp.bfloat16
MESH = pl.DeviceIdType.MESH
VMEM_SPEC = pl.BlockSpec(memory_space=pltpu.VMEM)
VMEM_LIMIT = 62 * 1024 * 1024


class Place:
    def __init__(self):
        d = lax.axis_index("dp")
        t = lax.axis_index("tensor")
        self.z = lax.div(d, 8)
        self.y = lax.rem(lax.div(d, 2), 4)
        self.h = lax.rem(d, 2)
        self.xl = lax.div(t, 2)
        self.core = lax.rem(t, 2)
        self.d = d
        self.t = t

    def at(self, dz=0, dy=0, dh=0):
        z = lax.rem(self.z + (dz + 4), 4)
        y = lax.rem(self.y + (dy + 4), 4)
        h = self.h if dh == 0 else 1 - self.h
        return z * 8 + y * 2 + h

    def dp_device(self, dz=0, dy=0, dh=0):
        return (self.at(dz, dy, dh), self.t)

    def core_device(self):
        return (self.d, self.xl * 2 + (1 - self.core))

    def x_device(self):
        return (self.d, (1 - self.xl) * 2 + self.core)

    def token_block(self, dx=0, dc=0):
        xl = self.xl if dx == 0 else 1 - self.xl
        core = self.core if dc == 0 else 1 - self.core
        return xl * 2 + core


def greet(devices):
    barrier = pltpu.get_barrier_semaphore()
    for device in devices:
        pl.semaphore_signal(barrier, inc=1, device_id=device, device_id_type=MESH)
    pl.semaphore_wait(barrier, len(devices))


def ring_devices(me):
    return [
        me.dp_device(dz=1),
        me.dp_device(dz=-1),
        me.dp_device(dy=1),
        me.dp_device(dy=-1),
        me.dp_device(dh=1),
    ]


def remote(src, dst, send, recv, index, device):
    return pltpu.make_async_remote_copy(
        src_ref=src,
        dst_ref=dst,
        send_sem=send.at[index],
        recv_sem=recv.at[index],
        device_id=device,
        device_id_type=MESH,
    )


def offsets(kind, first, second):
    return (first, second) if kind == 0 else (second, first)


class WeightGather:
    COUNT = 41

    def __init__(self, me, full, direct, send, recv):
        self.me, self.full, self.direct, self.send, self.recv = me, full, direct, send, recv
        self.started = []

    def block(self, kind, first, second, part=None):
        dz, dy = offsets(kind, first, second)
        row = self.me.at(dz, dy, kind) * 32
        if part is None:
            return self.full.at[pl.ds(pl.multiple_of(row, 32), 32)]
        return self.full.at[pl.ds(pl.multiple_of(row + part * 16, 16), 16)]

    def push(self, ref, index, device):
        copy = remote(ref, ref, self.send, self.recv, index, device)
        copy.start()
        self.started.append(copy)

    def arrived(self, ref, index):
        remote(ref, ref, self.send, self.recv, index, self.me.dp_device(dh=1)).wait_recv()

    def along(self, kind, level, step):
        dz, dy = offsets(kind, step, 0) if level == 0 else offsets(kind, 0, step)
        return self.me.dp_device(dz=dz, dy=dy)

    def base(self, kind, level, chunk):
        return 1 + kind * 4 + chunk * 0 if level == 0 else 9 + kind * 16 + chunk * 4

    def spread(self, kind, level, chunk):
        first = (0, -1, 1, 2)[chunk] if level == 1 else 0
        base = self.base(kind, level, chunk)
        ref = self.block(kind, first, 0)
        self.push(ref, base, self.along(kind, level, 1))
        self.push(ref, base + 1, self.along(kind, level, -1))
        if level == 0 and self.direct:
            self.push(ref, base + 2, self.along(kind, level, 2))

    def pass_on(self, kind, level, chunk, side):
        first = (0, -1, 1, 2)[chunk] if level == 1 else 0
        base = self.base(kind, level, chunk)
        step = -1 if side == 0 else 1
        where = (step, 0) if level == 0 else (first, step)
        self.arrived(self.block(kind, *where), base + side)
        self.push(self.block(kind, *where, part=side), base + 2 + side, self.along(kind, level, -step))

    def last(self, kind, level, chunk):
        first = (0, -1, 1, 2)[chunk] if level == 1 else 0
        base = self.base(kind, level, chunk)
        where = (2, 0) if level == 0 else (first, 2)
        for side in range(2):
            self.arrived(self.block(kind, *where, part=side), base + 2 + side)

    def exchange(self):
        self.push(self.block(0, 0, 0), 0, self.me.dp_device(dh=1))

    def begin(self):
        self.exchange()
        self.spread(0, 0, 0)
        self.spread(0, 1, 0)

    def step1(self):
        self.arrived(self.block(1, 0, 0), 0)
        self.spread(1, 0, 0)
        self.spread(1, 1, 0)

    def hand_on(self, kind, number):
        if self.direct:
            self.arrived(self.block(kind, (-1, 1, 2)[number], 0), self.base(kind, 0, 0) + number)
        elif number < 2:
            self.pass_on(kind, 0, 0, number)
        else:
            self.last(kind, 0, 0)
        self.spread(kind, 1, 1 + number)

    def step2(self):
        for kind in range(2):
            for number in range(2):
                self.hand_on(kind, number)

    def step3(self):
        for kind in range(2):
            self.hand_on(kind, 2)

    def step4(self):
        for chunk in range(4):
            for kind in range(2):
                for side in range(2):
                    self.pass_on(kind, 1, chunk, side)

    def finish(self):
        for chunk in range(4):
            for kind in range(2):
                self.last(kind, 1, chunk)
        for copy in self.started:
            copy.wait_send()


class TokenGather:
    COUNT = 12
    CHUNKS = 4
    ROWS = 64

    def __init__(self, me, rows, send, recv):
        self.me, self.rows, self.send, self.recv = me, rows, send, recv
        self.started = []

    def piece(self, dx, dc, chunk):
        row = self.me.token_block(dx, dc) * 256 + chunk * self.ROWS
        return self.rows.at[pl.ds(pl.multiple_of(row, self.ROWS), self.ROWS)]

    def push(self, ref, index, device):
        copy = remote(ref, ref, self.send, self.recv, index, device)
        copy.start()
        self.started.append(copy)

    def arrived(self, ref, index):
        remote(ref, ref, self.send, self.recv, index, self.me.core_device()).wait_recv()

    def begin(self, chunk):
        own = self.piece(0, 0, chunk)
        self.push(own, chunk, self.me.x_device())
        self.push(own, 4 + chunk, self.me.core_device())

    def pass_on(self, chunk):
        other = self.piece(1, 0, chunk)
        self.arrived(other, chunk)
        self.push(other, 8 + chunk, self.me.core_device())

    def finish(self):
        for chunk in range(self.CHUNKS):
            self.arrived(self.piece(0, 1, chunk), 4 + chunk)
        for chunk in range(self.CHUNKS):
            self.arrived(self.piece(1, 1, chunk), 8 + chunk)
        for copy in self.started:
            copy.wait_send()


class TokenScatter:
    COUNT = 12
    CHUNKS = 4
    ROWS = 64

    def __init__(self, me, part, near, far, relay, send, recv):
        self.me, self.part, self.near, self.far, self.relay = me, part, near, far, relay
        self.send, self.recv = send, recv
        self.started = []

    def piece(self, dx, dc, chunk):
        row = self.me.token_block(dx, dc) * 256 + chunk * self.ROWS
        return pl.ds(pl.multiple_of(row, self.ROWS), self.ROWS)

    def push(self, src, dst, index, device):
        copy = remote(src, dst, self.send, self.recv, index, device)
        copy.start()
        self.started.append(copy)

    def arrived(self, ref, index):
        remote(ref, ref, self.send, self.recv, index, self.me.core_device()).wait_recv()

    def begin_far(self, chunk):
        self.push(
            self.part.at[self.piece(1, 1, chunk)], self.relay.at[chunk], chunk, self.me.core_device()
        )

    def begin_near(self, chunk):
        self.push(
            self.part.at[self.piece(0, 1, chunk)], self.near.at[chunk], 4 + chunk, self.me.core_device()
        )

    def relay_on(self, chunk):
        self.arrived(self.relay.at[chunk], chunk)
        total = self.relay[chunk].astype(f32) + self.part[self.piece(1, 0, chunk), :].astype(f32)
        self.relay[chunk] = total.astype(bf16)
        self.push(self.relay.at[chunk], self.far.at[chunk], 8 + chunk, self.me.x_device())

    def total(self, chunk):
        self.arrived(self.near.at[chunk], 4 + chunk)
        self.arrived(self.far.at[chunk], 8 + chunk)
        return (
            self.part[self.piece(0, 0, chunk), :].astype(f32)
            + self.near[chunk].astype(f32)
            + self.far[chunk].astype(f32)
        )

    def finish(self):
        for copy in self.started:
            copy.wait_send()


def scatter_scratch():
    return [pltpu.VMEM((4, 64, 1024), bf16)] * 3 + [pltpu.SemaphoreType.DMA((12,))] * 2


class GradScatter:
    COUNT = 61

    def __init__(self, me, part, recv_half, recv_full, sums, last, send, recv):
        self.me, self.part = me, part
        self.recv_half, self.recv_full = recv_half, recv_full
        self.sums, self.last = sums, last
        self.send, self.recv = send, recv
        self.started = []

    def rows(self, kind, first, second, part=None):
        dz, dy = offsets(kind, first, second)
        row = self.me.at(dz, dy, kind) * 32
        if part is None:
            return pl.ds(pl.multiple_of(row, 32), 32)
        return pl.ds(pl.multiple_of(row + part * 16, 16), 16)

    def push(self, src, dst, index, device):
        copy = remote(src, dst, self.send, self.recv, index, device)
        copy.start()
        self.started.append(copy)

    def arrived(self, ref, index):
        remote(ref, ref, self.send, self.recv, index, self.me.dp_device(dh=1)).wait_recv()

    def along(self, kind, level, step):
        dz, dy = offsets(kind, step, 0) if level == 0 else offsets(kind, 0, step)
        return self.me.dp_device(dz=dz, dy=dy)

    def slot(self, kind, level, chunk):
        return kind * 5 + (4 if level == 0 else chunk)

    def source(self, kind, level, chunk, offset):
        if level == 1:
            first = (0, -1, 1, 2)[chunk]
            return self.part, self.rows(kind, first, offset), [
                self.rows(kind, first, offset, part) for part in range(2)
            ]
        chunk = {0: 0, -1: 1, 1: 2, 2: 3}[offset]
        base = (kind * 4 + chunk) * 32
        return self.sums, pl.ds(base, 32), [pl.ds(base, 16), pl.ds(base + 16, 16)]

    def far(self, kind, level, chunk):
        slot = self.slot(kind, level, chunk)
        ref, _, halves = self.source(kind, level, chunk, 2)
        self.push(ref.at[halves[0]], self.recv_half.at[slot, 0], slot * 6, self.along(kind, level, 1))
        self.push(
            ref.at[halves[1]], self.recv_half.at[slot, 1], slot * 6 + 1, self.along(kind, level, -1)
        )

    def near(self, kind, level, chunk):
        slot = self.slot(kind, level, chunk)
        for side in range(2):
            step = 1 if side == 0 else -1
            ref, _, halves = self.source(kind, level, chunk, step)
            self.push(
                ref.at[halves[1 - side]],
                self.recv_full.at[slot, side, pl.ds(16 * (1 - side), 16)],
                slot * 6 + 4 + side,
                self.along(kind, level, step),
            )

    def middle(self, kind, level, chunk, side):
        slot = self.slot(kind, level, chunk)
        step = 1 if side == 0 else -1
        ref, _, halves = self.source(kind, level, chunk, step)
        self.arrived(self.recv_half.at[slot, side], slot * 6 + side)
        total = ref[halves[side], :].astype(f32) + self.recv_half[slot, side].astype(f32)
        ref[halves[side], :] = total.astype(bf16)
        self.push(
            ref.at[halves[side]],
            self.recv_full.at[slot, side, pl.ds(16 * side, 16)],
            slot * 6 + 2 + side,
            self.along(kind, level, step),
        )

    def total(self, kind, level, chunk):
        slot = self.slot(kind, level, chunk)
        ref, whole, _ = self.source(kind, level, chunk, 0)
        for side in range(2):
            full = self.recv_full.at[slot, side]
            self.arrived(full.at[pl.ds(16 * side, 16)], slot * 6 + 2 + side)
            self.arrived(full.at[pl.ds(16 * (1 - side), 16)], slot * 6 + 4 + side)
        return (
            ref[whole, :].astype(f32)
            + self.recv_full[slot, 0].astype(f32)
            + self.recv_full[slot, 1].astype(f32)
        )

    def begin(self, late=False):
        self.late = late
        for push in (self.far,) if late else (self.far, self.near):
            for chunk in range(4):
                for kind in range(2):
                    push(kind, 1, chunk)

    def step1(self, chunk):
        for kind in range(2):
            for side in range(2):
                self.middle(kind, 1, chunk, side)
        if self.late:
            for kind in range(2):
                self.near(kind, 1, chunk)

    def step2(self, chunk):
        for kind in range(2):
            total = self.total(kind, 1, chunk)
            self.sums[pl.ds((kind * 4 + chunk) * 32, 32), :] = total.astype(bf16)

    def step3(self):
        for kind in range(2):
            slot = self.slot(kind, 0, 0)
            for side in range(2):
                step = 1 if side == 0 else -1
                _, whole, _ = self.source(kind, 0, 0, step)
                self.push(
                    self.sums.at[whole],
                    self.recv_full.at[slot, side],
                    slot * 6 + 2 + side,
                    self.along(kind, 0, step),
                )
            _, _, halves = self.source(kind, 0, 0, 2)
            for side in range(2):
                self.push(
                    self.sums.at[halves[side]],
                    self.recv_half.at[slot, side],
                    slot * 6 + side,
                    self.along(kind, 0, 2),
                )

    def sum0(self, kind):
        slot = self.slot(kind, 0, 0)
        for side in range(2):
            self.arrived(self.recv_full.at[slot, side], slot * 6 + 2 + side)
            self.arrived(self.recv_half.at[slot, side], slot * 6 + side)
        _, whole, _ = self.source(kind, 0, 0, 0)
        far = jnp.concatenate([self.recv_half[slot, 0], self.recv_half[slot, 1]], axis=0)
        return (
            self.sums[whole, :].astype(f32)
            + self.recv_full[slot, 0].astype(f32)
            + self.recv_full[slot, 1].astype(f32)
            + far.astype(f32)
        )

    def step5(self):
        self.last[0] = self.sum0(1).astype(bf16)
        self.push(self.last.at[0], self.last.at[1], 60, self.me.dp_device(dh=1))

    def result(self):
        own = self.sum0(0)
        self.arrived(self.last.at[1], 60)
        return own + self.last[1].astype(f32)

    def finish(self):
        for copy in self.started:
            copy.wait_send()


def grad_scratch(width):
    return [
        pltpu.VMEM((10, 2, 16, width), bf16),
        pltpu.VMEM((10, 2, 32, width), bf16),
        pltpu.VMEM((256, width), bf16),
        pltpu.VMEM((2, 32, width), bf16),
        pltpu.SemaphoreType.DMA((61,)),
        pltpu.SemaphoreType.DMA((61,)),
    ]


def row_scale(values):
    return lax.rsqrt(jnp.mean(values * values, axis=-1, keepdims=True) + epsilon)


def norm_back(values, inverse, gain_vec, upstream):
    weighted = upstream * gain_vec
    row_inner = jnp.mean(weighted * values, axis=-1, keepdims=True)
    return inverse * weighted - values * inverse * inverse * inverse * row_inner


def call(kernel, outs, scratch, number, args, flops=0, moved=0):
    return pl.pallas_call(
        kernel,
        out_shape=outs,
        in_specs=[VMEM_SPEC] * len(args),
        out_specs=[VMEM_SPEC] * len(outs),
        scratch_shapes=scratch,
        cost_estimate=pl.CostEstimate(flops=flops, bytes_accessed=moved, transcendentals=0),
        compiler_params=pltpu.CompilerParams(
            collective_id=number, has_side_effects=True, vmem_limit_bytes=VMEM_LIMIT
        ),
    )(*args)


def dot(a, b):
    return jnp.dot(a, b, preferred_element_type=f32)


def dot_tb(a, b):
    return lax.dot_general(a, b, (((1,), (1,)), ((), ())), preferred_element_type=f32)


def head_scale(values):
    return lax.rsqrt(jnp.mean(values * values, axis=0, keepdims=True) + epsilon)


def rotate(values, cosine, sine):
    front, back = values[:32], values[32:]
    return jnp.concatenate([front * cosine - back * sine, back * cosine + front * sine], axis=0)


def rotate_back(values, cosine, sine):
    front, back = values[:32], values[32:]
    return jnp.concatenate([front * cosine + back * sine, back * cosine - front * sine], axis=0)


def project_block(block, rows_ref, weight_ref, pre_ref, low):
    here = pl.ds(pl.multiple_of(block * 256, 256), 256)
    flat = dot(rows_ref[here, :], weight_ref[:, 0:512])
    turned = flat.T
    pre_ref[:, here] = turned[:384]
    cosine, sine = low.cos[:, here], low.sin[:, here]
    for head in range(4):
        u = turned[64 * head : 64 * head + 64]
        u = u * head_scale(u) * low.q_gain[...]
        low.q[pl.ds(64 * head, 64), here] = (rotate(u, cosine, sine) * 0.125).astype(bf16)
    for head in range(2):
        u = turned[256 + 64 * head : 320 + 64 * head]
        u = rotate(u * head_scale(u) * low.k_gain[...], cosine, sine)
        low.kt[head, block] = u.astype(bf16)
        low.k[head, here, :] = u.T.astype(bf16)
        u = turned[384 + 64 * head : 448 + 64 * head]
        low.vt[head, block, 0:64, :] = u.astype(bf16)
        low.vt[head, block, 64:80, :] = jnp.ones((16, 256), bf16)
        low.v[head, here, :] = u.T.astype(bf16)


def pair_lanes(ref, head, here):
    return jnp.concatenate(
        [ref[pl.ds(128 * head, 64), here], ref[pl.ds(128 * head + 64, 64), here]], axis=1
    )


def seen(low, number, key_block, diagonal):
    here = pl.ds(number * 256, 256)
    key_row = lax.broadcasted_iota(jnp.int32, (256, 256), 0) + key_block * 256
    mask = key_row >= low.start[:, here]
    if diagonal:
        query_row = lax.broadcasted_iota(jnp.int32, (256, 256), 1) + number * 256
        mask = jnp.logical_and(mask, key_row <= query_row)
    return jnp.concatenate([mask, mask], axis=1)


def forward_block(low, head, number, acc):
    here = pl.ds(number * 256, 256)
    queries = pair_lanes(low.q, head, here)

    def step(key_block, diagonal):
        keys = low.k[head, pl.ds(pl.multiple_of(key_block * 256, 256), 256), :]
        weight = jnp.exp(dot(keys, queries))
        weight = jnp.where(seen(low, number, key_block, diagonal), weight, 0.0).astype(bf16)
        return dot(low.vt[head, key_block], weight)

    acc[...] = step(number, True)
    if number > 0:

        @pl.loop(0, number)
        def _(key_block):
            acc[...] += step(key_block, False)

    total = acc[64:65, :]
    mixed = acc[0:64, :] / total
    low.lse[2 * head : 2 * head + 1, here] = jnp.log(total[:, 0:256])
    low.lse[2 * head + 1 : 2 * head + 2, here] = jnp.log(total[:, 256:512])
    low.mixed[pl.ds(128 * head, 64), here] = mixed[:, 0:256]
    low.mixed[pl.ds(128 * head + 64, 64), here] = mixed[:, 256:512]


def backward_prepare(block, rows_ref, weight_ref, low):
    here = pl.ds(pl.multiple_of(block * 256, 256), 256)
    turned = dot(rows_ref[here, :], weight_ref[:, 512:768]).T.astype(bf16)
    low.gt[:, here] = turned
    for head in range(4):
        part = turned[64 * head : 64 * head + 64].astype(f32)
        low.g[head, here, :] = part.T.astype(bf16)
        mixed = low.mixed[pl.ds(64 * head, 64), here]
        low.inner[head : head + 1, here] = jnp.sum(part * mixed, axis=0, keepdims=True)
        low.qn[head, here, :] = low.q[pl.ds(64 * head, 64), here].astype(f32).T.astype(bf16)


def backward_block(low, head, number, acc):
    here = pl.ds(number * 256, 256)
    queries = pair_lanes(low.q, head, here)
    upstream = pair_lanes(low.gt, head, here)
    query_rows = jnp.concatenate([low.qn[2 * head, here, :], low.qn[2 * head + 1, here, :]], axis=0)
    upstream_rows = jnp.concatenate([low.g[2 * head, here, :], low.g[2 * head + 1, here, :]], axis=0)

    def both(ref):
        return jnp.concatenate(
            [ref[2 * head : 2 * head + 1, here], ref[2 * head + 1 : 2 * head + 2, here]], axis=1
        )

    lse = both(low.lse)
    inner = both(low.inner)

    def step(key_block, diagonal):
        rows = pl.ds(pl.multiple_of(key_block * 256, 256), 256)
        weight = jnp.exp(dot(low.k[head, rows, :], queries) - lse)
        weight = jnp.where(seen(low, number, key_block, diagonal), weight, 0.0)
        score = weight * (dot(low.v[head, rows, :], upstream) - inner)
        score = score.astype(bf16)
        value_part = dot(weight.astype(bf16), upstream_rows)
        key_part = dot(score, query_rows)
        if diagonal:
            low.dv[head, rows, :] = value_part
            low.dk[head, rows, :] = key_part
        else:
            low.dv[head, rows, :] += value_part
            low.dk[head, rows, :] += key_part
        return dot(low.kt[head, key_block], score)

    acc[0:64, :] = step(number, True)
    if number > 0:

        @pl.loop(0, number)
        def _(key_block):
            acc[0:64, :] += step(key_block, False)

    low.dq[pl.ds(128 * head, 64), here] = acc[0:64, 0:256]
    low.dq[pl.ds(128 * head + 64, 64), here] = acc[0:64, 256:512]


def head_norm_back(values, gain, upstream):
    inverse = head_scale(values)
    weighted = upstream * gain
    inner = jnp.mean(weighted * values, axis=0, keepdims=True)
    return inverse * weighted - values * inverse * inverse * inverse * inner, inverse


def backward_finish(block, low, pre_ref, turned_ref, flat_ref):
    here = pl.ds(pl.multiple_of(block * 256, 256), 256)
    cosine, sine = low.cos[:, here], low.sin[:, here]
    q_part = jnp.zeros((64, 1), f32)
    k_part = jnp.zeros((64, 1), f32)
    for head in range(4):
        rows = pl.ds(64 * head, 64)
        upstream = rotate_back(low.dq[rows, here] * 0.125, cosine, sine)
        values = pre_ref[rows, here]
        grad, inverse = head_norm_back(values, low.q_gain[...], upstream)
        q_part = q_part + jnp.sum(upstream * values * inverse, axis=1, keepdims=True)
        turned_ref[rows, here] = grad.astype(bf16)
    for head in range(2):
        rows = pl.ds(256 + 64 * head, 64)
        upstream = rotate_back(low.dk[head, here, :].T, cosine, sine)
        values = pre_ref[rows, here]
        grad, inverse = head_norm_back(values, low.k_gain[...], upstream)
        k_part = k_part + jnp.sum(upstream * values * inverse, axis=1, keepdims=True)
        turned_ref[rows, here] = grad.astype(bf16)
        turned_ref[pl.ds(384 + 64 * head, 64), here] = low.dv[head, here, :].T.astype(bf16)
    flat_ref[here, :] = turned_ref[:, here].astype(f32).T.astype(bf16)
    return q_part, k_part


class GainSum:
    def __init__(self, me, row, plane, send, recv):
        self.me, self.row, self.plane = me, row, plane
        self.send, self.recv = send, recv
        self.started = []

    def row_devices(self):
        me = self.me
        return [
            (me.at(dh=step // 4), lax.rem(me.t + step % 4, 4)) for step in range(1, 8)
        ]

    def plane_devices(self):
        return [self.me.dp_device(dz=step // 4, dy=step % 4) for step in range(1, 16)]

    def send_out(self, slots, place, value, devices, base):
        slots[place] = value
        for step, device in enumerate(devices):
            copy = remote(
                slots.at[place], slots.at[place], self.send, self.recv, base + step, device
            )
            copy.start()
            self.started.append(copy)

    def add_up(self, slots, place, devices, base):
        for step, device in enumerate(devices):
            remote(
                slots.at[place], slots.at[place], self.send, self.recv, base + step, device
            ).wait_recv()
        total = slots[0]
        for slot in range(1, len(devices) + 1):
            total = total + slots[slot]
        return total

    def begin(self, value):
        me = self.me
        self.send_out(self.row, me.h * 4 + me.t, value, self.row_devices(), 0)

    def middle(self):
        me = self.me
        value = self.add_up(self.row, me.h * 4 + me.t, self.row_devices(), 0)
        self.send_out(self.plane, me.z * 4 + me.y, value, self.plane_devices(), 7)

    def result(self):
        me = self.me
        value = self.add_up(self.plane, me.z * 4 + me.y, self.plane_devices(), 7)
        for copy in self.started:
            copy.wait_send()
        return value


def gain_scratch():
    return [
        pltpu.VMEM((8, 24, 128), f32),
        pltpu.VMEM((16, 24, 128), f32),
        pltpu.SemaphoreType.DMA((22,)),
        pltpu.SemaphoreType.DMA((22,)),
    ]


class Fields:
    def __init__(self, **refs):
        self.__dict__.update(refs)


def gather_services(gather):
    steps = [gather.step2, gather.step3]
    for chunk in range(4):

        def hand_bulk(chunk=chunk):
            for kind in range(2):
                for side in range(2):
                    gather.pass_on(kind, 1, chunk, side)

        steps.append(hand_bulk)
    return steps


def column(row_ref):
    return jnp.broadcast_to(row_ref[...], (128, 64)).T[:, 0:1]


def tables(position_ref, q_gain_ref, k_gain_ref, cos, sin, start, q_gain, k_gain):
    place = lax.broadcasted_iota(jnp.int32, (32, 1024), 0).astype(f32)
    frequency = jnp.exp(place * (-math.log(rope_base) * 2.0 / 64))
    angles = frequency * position_ref[...].astype(f32)
    cos[...] = jnp.cos(angles)
    sin[...] = jnp.sin(angles)
    start[...] = lax.broadcasted_iota(jnp.int32, (1, 1024), 1) - position_ref[...]
    q_gain[...] = column(q_gain_ref)
    k_gain[...] = column(k_gain_ref)


def table_scratch():
    return [
        pltpu.VMEM((32, 1024), f32),
        pltpu.VMEM((32, 1024), f32),
        pltpu.VMEM((1, 1024), jnp.int32),
        pltpu.VMEM((64, 1), f32),
        pltpu.VMEM((64, 1), f32),
    ]


def turn(values):
    return values.astype(f32).T.astype(bf16)


def ffn_block(here, low):
    rows = low.rows[here, :]
    grads = low.grad_rows[here, :]
    for first, count in ((0, 512), (512, 640)):
        columns = pl.ds(first, count)
        gate = dot(rows, low.full[:, pl.ds(first, count)])
        up = dot(rows, low.full[:, pl.ds(1152 + first, count)])
        hidden = dot(grads, low.full[:, pl.ds(2304 + first, count)])
        sigmoid = jax.nn.sigmoid(gate)
        silu = gate * sigmoid
        low.activation[here, columns] = (silu * up).astype(bf16)
        low.gate_low[here, columns] = (hidden * up * sigmoid * (1.0 + gate * (1.0 - sigmoid))).astype(bf16)
        low.up_low[here, columns] = (hidden * silu).astype(bf16)
    low.ffn_part[here, :] = dot_tb(low.activation[here, :], low.full[:, 2304:3456]).astype(bf16)
    low.part[here, :] = (
        dot_tb(low.gate_low[here, :], low.full[:, 0:1152]) + dot_tb(low.up_low[here, :], low.full[:, 1152:2304])
    ).astype(bf16)


def scatter_services(scatter):
    steps = []
    for chunk in range(4):
        steps.append(functools.partial(scatter.step1, chunk))
    for chunk in range(4):
        steps.append(functools.partial(scatter.step2, chunk))
    steps.append(scatter.step3)
    steps.append(scatter.step5)
    return steps


class Heads:
    def __init__(self, ref, first):
        self.ref, self.first = ref, first

    def lanes(self, head):
        return pl.ds((self.first + head) * 128, 64)

    def __getitem__(self, index):
        return self.ref[index[1], self.lanes(index[0])]

    def __setitem__(self, index, value):
        self.ref[index[1], self.lanes(index[0])] = value


def block_kernel(
    x_ref, position_ref, gain_ref, wq_ref, wk_ref, wv_ref, wo_ref, q_gain_ref, k_gain_ref, ffn_gain_ref,
    wg_ref, wu_ref, wd_ref, cot_ref,
    out_ref, input_grad_ref, attn_shard_ref, ffn_shard_ref, gains_ref,
    attn_full, ffn_full, normed_ref, grad_rows, grad_rows_t, rows_ref, back_rows, middle, part, ffn_part,
    activation, gate_low, up_low,
    pre_ref, mixed_ref, lse_ref, q_ref, kt_ref, k_ref, vt, v_ref, acc, inner, dk, dv, dq, gain_rows,
    *scratch,
):
    me = Place()
    scratch = list(scratch)

    def take(count):
        taken = scratch[:count]
        del scratch[:count]
        return taken

    cos, sin, start, q_gain, k_gain = take(5)
    buffers = take(5)
    scatter = TokenScatter(me, part, *buffers)
    first = TokenScatter(me, part, *buffers)
    third = TokenScatter(me, part, *buffers)
    last = TokenScatter(me, ffn_part, *take(5))
    attn = WeightGather(me, attn_full, True, *take(2))
    ffn = WeightGather(me, ffn_full, False, *take(2))
    tokens = TokenGather(me, normed_ref, *take(2))
    upstream = TokenGather(me, grad_rows, *take(2))
    second = TokenGather(me, rows_ref, *take(2))
    back = TokenGather(me, back_rows, *take(2))
    attn_grad = grad_rows_t.at[:, pl.ds(0, 768)]
    down_grad = GradScatter(me, ffn_full.at[:, pl.ds(2304, 1152)], *take(6))
    gate_grad = GradScatter(me, ffn_full.at[:, pl.ds(0, 2304)], *take(6))
    weight_grad = GradScatter(me, attn_grad, *take(6))
    gains = GainSum(me, *take(4))
    middle_grad = input_grad_ref
    turned = gate_low.at[pl.ds(0, 512), pl.ds(0, 1024)]
    flat = up_low.at[:, pl.ds(0, 512)]
    gt = gate_low.at[pl.ds(512, 256), pl.ds(0, 1024)]
    low = Fields(
        cos=cos, sin=sin, q_gain=q_gain, k_gain=k_gain, start=start,
        q=q_ref, kt=kt_ref, k=k_ref, vt=vt, v=v_ref, lse=lse_ref, mixed=mixed_ref,
        rows=rows_ref, full=ffn_full, grad_rows=grad_rows, part=part, ffn_part=ffn_part,
        activation=activation, gate_low=gate_low, up_low=up_low,
        gt=gt, g=Heads(activation, 0), inner=inner, qn=Heads(activation, 4), dk=dk, dv=dv, dq=dq,
    )
    own_rows = pl.ds(pl.multiple_of(me.d * 32, 32), 32)
    own_tokens = pl.ds(pl.multiple_of(me.t * 256, 256), 256)
    attn_full[own_rows, 0:256] = wq_ref[...]
    attn_full[own_rows, 256:384] = wk_ref[...]
    attn_full[own_rows, 384:512] = wv_ref[...]
    attn_full[own_rows, 512:768] = wo_ref[...]
    values = x_ref[...].astype(f32)
    normed_ref[own_tokens, :] = (values * row_scale(values) * gain_ref[...]).astype(bf16)
    greet(gains.row_devices() + gains.plane_devices())
    attn.begin()
    for chunk in range(4):
        tokens.begin(chunk)
    ffn_full[own_rows, 0:1152] = wg_ref[...]
    ffn_full[own_rows, 1152:2304] = wu_ref[...]
    ffn_full[own_rows, 2304:3456] = wd_ref[...]
    grad_rows[own_tokens, :] = cot_ref[...]
    attn.step1()
    lse_ref[...] = jnp.zeros((8, 1024), f32)
    tables(position_ref, q_gain_ref, k_gain_ref, cos, sin, start, q_gain, k_gain)
    attn.step2()
    attn.step3()
    attn.step4()
    ffn.begin()
    services = [ffn.step1] + [functools.partial(ffn.hand_on, kind, number) for kind in range(2) for number in range(2)]
    services += gather_services(ffn)[1:]

    def serve(count=1):
        for _ in range(count):
            if services:
                services.pop(0)()

    for chunk in range(4):
        tokens.pass_on(chunk)
    tokens.finish()
    attn.finish()
    serve()
    for chunk in range(4):
        upstream.begin(chunk)

    @pl.loop(0, 4)
    def _(block):
        project_block(block, normed_ref, attn_full, pre_ref, low)

    for number in range(4):
        for head in range(2):
            forward_block(low, head, number, acc)
            if number == 1 or number == 3:
                serve()
    for chunk in range(4):
        upstream.pass_on(chunk)

    def output_part(dx, dc):
        here = pl.ds(pl.multiple_of(me.token_block(dx, dc) * 256, 256), 256)
        flat = mixed_ref[:, here].T.astype(bf16)
        part[here, :] = dot_tb(flat, attn_full[:, 512:768]).astype(bf16)

    output_part(1, 1)
    for chunk in range(4):
        scatter.begin_far(chunk)
    output_part(1, 0)
    output_part(0, 1)
    for chunk in range(4):
        scatter.begin_near(chunk)
    output_part(0, 0)
    for chunk in range(4):
        scatter.relay_on(chunk)
    serve(2)
    upstream.finish()

    @pl.loop(0, 4)
    def _(block):
        here = pl.ds(pl.multiple_of(block * 256, 256), 256)
        grad_rows_t[:, here] = turn(grad_rows[here, :])

    for chunk in range(4):
        here = pl.ds(chunk * 64, 64)
        values = x_ref[here, :].astype(f32) + scatter.total(chunk)
        middle[here, :] = values
        own = pl.ds(pl.multiple_of(me.t * 256 + chunk * 64, 64), 64)
        rows_ref[own, :] = (values * row_scale(values) * ffn_gain_ref[...]).astype(bf16)
        if chunk == 3:
            scatter.finish()
        second.begin(chunk)
    serve(20)
    ffn.finish()

    passes = [
        remote(piece, piece, second.send, second.recv, 8 + chunk, me.core_device())
        for chunk, piece in enumerate(second.piece(1, 0, chunk) for chunk in range(4))
    ]

    @pl.loop(0, 4)
    def _(turn_number):
        @pl.when(turn_number == 1)
        def _():
            for chunk in range(4):
                second.arrived(second.piece(0, 1, chunk), 4 + chunk)

        @pl.when(turn_number == 2)
        def _():
            for chunk in range(4):
                second.arrived(second.piece(1, 0, chunk), chunk)
                passes[chunk].start()

        @pl.when(turn_number == 3)
        def _():
            for chunk in range(4):
                second.arrived(second.piece(1, 1, chunk), 8 + chunk)

        block = lax.rem(me.xl + lax.div(turn_number, 2), 2) * 2 + lax.rem(me.core + lax.rem(turn_number, 2), 2)
        ffn_block(pl.ds(pl.multiple_of(block * 256, 256), 256), low)

    for copy in second.started + passes:
        copy.wait_send()

    for chunk in range(4):
        first.begin_far(chunk)
    for chunk in range(4):
        first.begin_near(chunk)

    @pl.loop(0, 4)
    def _(tile):
        here = pl.ds(pl.multiple_of(tile * 256, 256), 256)
        ffn_full[here, 2304:3456] = dot(grad_rows_t[here, :], activation[...]).astype(bf16)

    down_grad.begin()
    for chunk in range(4):
        first.relay_on(chunk)

    @pl.loop(0, 4)
    def _(tile):
        here = pl.ds(pl.multiple_of(tile * 256, 256), 256)
        rows_t = turn(rows_ref[:, here])
        ffn_full[here, 0:1152] = dot(rows_t, gate_low[...]).astype(bf16)
        ffn_full[here, 1152:2304] = dot(rows_t, up_low[...]).astype(bf16)

    gate_grad.begin(late=True)
    ffn_gain_total = jnp.zeros((1, 1024), f32)
    for chunk in range(4):
        here = pl.ds(chunk * 64, 64)
        grad = first.total(chunk)
        values = middle[here, :]
        inverse = row_scale(values)
        ffn_gain_total = ffn_gain_total + jnp.sum(grad * values * inverse, axis=0, keepdims=True)
        total = cot_ref[here, :].astype(f32) + norm_back(values, inverse, ffn_gain_ref[...], grad)
        middle_grad[here, :] = total
        own = pl.ds(pl.multiple_of(me.t * 256 + chunk * 64, 64), 64)
        back_rows[own, :] = total.astype(bf16)
        if chunk == 3:
            first.finish()
        back.begin(chunk)
    for chunk in range(4):
        last.begin_far(chunk)
    for chunk in range(4):
        last.begin_near(chunk)
    down_steps = scatter_services(down_grad)
    gate_steps = scatter_services(gate_grad)
    services.extend(down_steps[0:4])
    serve(4)
    services.extend(gate_steps[0:4] + down_steps[4:9])
    for chunk in range(4):
        back.pass_on(chunk)
        if chunk >= 2:
            serve(2)
    for chunk in range(4):
        last.relay_on(chunk)
    back.finish()

    @pl.loop(0, 4)
    def _(block):
        backward_prepare(block, back_rows, attn_full, low)


    @pl.loop(0, 4)
    def _(tile):
        here = pl.ds(pl.multiple_of(tile * 256, 256), 256)
        attn_grad[here, 512:768] = dot(mixed_ref[...].astype(bf16), back_rows[:, here]).T.astype(bf16)

    services.extend(gate_steps[4:8] + down_steps[9:10] + gate_steps[8:10])
    for number in range(4):
        for head in range(2):
            backward_block(low, head, number, acc)
            if number == 0:
                serve(2)
            if (number, head) == (1, 0):
                serve(1)
            if (number, head) in ((2, 0), (2, 1)):
                serve(2)
            if (number, head) == (3, 0):
                serve(2)
    for chunk in range(4):
        here = pl.ds(chunk * 64, 64)
        out_ref[here, :] = (middle[here, :] + last.total(chunk)).astype(bf16)
    q_part = jnp.zeros((64, 1), f32)
    k_part = jnp.zeros((64, 1), f32)
    for block in range(4):
        q_more, k_more = backward_finish(block, low, pre_ref, turned, flat)
        q_part = q_part + q_more
        k_part = k_part + k_more

    serve(1)

    def first_part(dx, dc):
        here = pl.ds(pl.multiple_of(me.token_block(dx, dc) * 256, 256), 256)
        part[here, :] = dot_tb(flat[here, :], attn_full[:, 0:512]).astype(bf16)

    first_part(1, 1)
    for chunk in range(4):
        third.begin_far(chunk)

    @pl.loop(0, 4)
    def _(tile):
        here = pl.ds(pl.multiple_of(tile * 256, 256), 256)
        attn_grad[here, 0:512] = dot(turned[...], normed_ref[:, here]).T.astype(bf16)

    weight_grad.begin()
    first_part(1, 0)
    for chunk in range(4):
        third.relay_on(chunk)
    first_part(0, 1)
    for chunk in range(4):
        third.begin_near(chunk)
    first_part(0, 0)
    gain_rows[16:24, :] = jnp.zeros((8, 128), f32)
    gain_rows[16:17, 0:64] = jnp.broadcast_to(q_part, (64, 128)).T[0:1, :]
    gain_rows[17:18, 0:64] = jnp.broadcast_to(k_part, (64, 128)).T[0:1, :]
    for chunk in range(4):
        weight_grad.step1(chunk)
    for chunk in range(4):
        weight_grad.step2(chunk)
    weight_grad.step3()
    serve(20)
    gain_total = jnp.zeros((1, 1024), f32)
    for chunk in range(4):
        here = pl.ds(chunk * 64, 64)
        upstream = third.total(chunk)
        values = x_ref[here, :].astype(f32)
        inverse = row_scale(values)
        gain_total = gain_total + jnp.sum(upstream * values * inverse, axis=0, keepdims=True)
        input_grad_ref[here, :] = middle_grad[here, :] + norm_back(
            values, inverse, gain_ref[...], upstream
        )
    for part_number in range(8):
        lanes = slice(128 * part_number, 128 * part_number + 128)
        gain_rows[part_number : part_number + 1, :] = gain_total[:, lanes]
        gain_rows[8 + part_number : 9 + part_number, :] = ffn_gain_total[:, lanes]
    gains.begin(gain_rows[...])
    weight_grad.step5()
    gains.middle()
    ffn_shard_ref[:, 2304:3456] = down_grad.result()
    ffn_shard_ref[:, 0:2304] = gate_grad.result()
    attn_shard_ref[...] = weight_grad.result()
    gains_ref[...] = gains.result()
    for transfer in (third, last, down_grad, gate_grad, weight_grad):
        transfer.finish()


def unpack_kernel(
    out_ref, input_grad_ref, attn_ref, ffn_ref, gains_ref,
    out, input_grad, attn_gain, wq, wk, wv, wo, q_gain, k_gain, ffn_gain, wg, wu, wd,
):
    out[...] = out_ref[...]
    input_grad[...] = input_grad_ref[...]
    for part in range(8):
        lanes = slice(128 * part, 128 * part + 128)
        attn_gain[:, lanes] = gains_ref[part : part + 1, :]
        ffn_gain[:, lanes] = gains_ref[8 + part : 9 + part, :]
    q_gain[...] = gains_ref[16:17, 0:64]
    k_gain[...] = gains_ref[17:18, 0:64]
    wq[...] = attn_ref[:, 0:256]
    wk[...] = attn_ref[:, 256:384]
    wv[...] = attn_ref[:, 384:512]
    wo[...] = attn_ref[:, 512:768]
    wg[...] = ffn_ref[:, 0:1152]
    wu[...] = ffn_ref[:, 1152:2304]
    wd[...] = ffn_ref[:, 2304:3456]


def shape(rows, columns, kind):
    return jax.ShapeDtypeStruct((rows, columns), kind)


def sems(count):
    return [pltpu.SemaphoreType.DMA((count,))] * 2


def body(
    block_input,
    positions,
    attn_gain,
    w_query,
    w_key,
    w_value,
    w_output,
    q_gain,
    k_gain,
    ffn_gain,
    w_gate,
    w_up,
    w_down,
    cotangent,
):
    square = pltpu.VMEM((1024, 1024), bf16)
    hidden = pltpu.VMEM((1024, 1152), bf16)
    layer_output, input_grad, attn_out, ffn_out, gains = call(
        block_kernel,
        [
            shape(256, 1024, bf16),
            shape(256, 1024, f32),
            shape(32, 768, f32),
            shape(32, 3456, f32),
            shape(24, 128, f32),
        ],
        [
            pltpu.VMEM((1024, 768), bf16),
            pltpu.VMEM((1024, 3456), bf16),
            square,
            square,
            square,
            square,
            square,
            pltpu.VMEM((256, 1024), f32),
            square,
            square,
            hidden,
            hidden,
            hidden,
            pltpu.VMEM((384, 1024), f32),
            pltpu.VMEM((256, 1024), f32),
            pltpu.VMEM((8, 1024), f32),
            pltpu.VMEM((256, 1024), bf16),
            pltpu.VMEM((2, 4, 64, 256), bf16),
            pltpu.VMEM((2, 1024, 64), bf16),
            pltpu.VMEM((2, 4, 80, 256), bf16),
            pltpu.VMEM((2, 1024, 64), bf16),
            pltpu.VMEM((80, 512), f32),
            pltpu.VMEM((8, 1024), f32),
            pltpu.VMEM((2, 1024, 64), f32),
            pltpu.VMEM((2, 1024, 64), f32),
            pltpu.VMEM((256, 1024), f32),
            pltpu.VMEM((24, 128), f32),
        ]
        + table_scratch()
        + scatter_scratch() * 2
        + sems(41) * 2
        + sems(12) * 4
        + grad_scratch(1152)
        + grad_scratch(2304)
        + grad_scratch(768)
        + gain_scratch(),
        0,
        (
            block_input, positions[None, :], attn_gain[None, :], w_query, w_key, w_value, w_output.T,
            q_gain[None, :], k_gain[None, :], ffn_gain[None, :], w_gate, w_up, w_down.T, cotangent,
        ),
    )
    outs = pl.pallas_call(
        unpack_kernel,
        out_shape=[
            shape(256, 1024, bf16),
            shape(256, 1024, f32),
            shape(1, 1024, f32),
            shape(32, 256, f32),
            shape(32, 128, f32),
            shape(32, 128, f32),
            shape(32, 256, f32),
            shape(1, 64, f32),
            shape(1, 64, f32),
            shape(1, 1024, f32),
            shape(32, 1152, f32),
            shape(32, 1152, f32),
            shape(32, 1152, f32),
        ],
        in_specs=[VMEM_SPEC] * 5,
        out_specs=[VMEM_SPEC] * 13,
        compiler_params=pltpu.CompilerParams(vmem_limit_bytes=VMEM_LIMIT),
    )(layer_output, input_grad, attn_out, ffn_out, gains)
    outs = [out[0] if out.shape[0] == 1 else out for out in outs]
    return (*outs[:6], outs[6].T, *outs[7:12], outs[12].T)


def solution(mesh):
    placed = (
        P(("dp", "tensor"), None),
        P("dp"),
        P(),
        P("dp", "tensor"),
        P("dp", "tensor"),
        P("dp", "tensor"),
        P("tensor", "dp"),
        P(),
        P(),
        P(),
        P("dp", "tensor"),
        P("dp", "tensor"),
        P("tensor", "dp"),
        P(("dp", "tensor"), None),
    )
    return jax.shard_map(
        body,
        mesh=mesh,
        in_specs=placed,
        out_specs=(
            P(("dp", "tensor"), None),
            P(("dp", "tensor"), None),
            P(),
            P("dp", "tensor"),
            P("dp", "tensor"),
            P("dp", "tensor"),
            P("tensor", "dp"),
            P(),
            P(),
            P(),
            P("dp", "tensor"),
            P("dp", "tensor"),
            P("tensor", "dp"),
        ),
        check_vma=False,
    )
```
